32 devices in a mesh: row: 8 (over y, x, core), col: 4 (over z).
Axes of the slice: x: 2, y: 2, z: 4, core: 2. Of those that a mesh axis runs over, the one named last changes fastest.
Arguments:
- sqrt_iterate: float32 [64, 128, 1024], P(('row', 'col'))
- inverse_iterate: float32 [64, 128, 1024], P(('row', 'col'))
- pattern: int32 [64, 8], replicated, may hold values from 0 to 63, as said below
- keep_mask: int32 [64, 8], replicated, may hold values 0 or 1
- row_order: int32 [64], replicated, may hold values from 0 to 63, as said below
Outputs:
- sqrt_next: float32 [64, 128, 1024], P(('row', 'col'))
- inverse_next: float32 [64, 128, 1024], P(('row', 'col'))
The draws below stay inside these ranges and needn't reach their ends.
Inputs may be any that keep to these rules, and one draw needn't show every extreme that they name: row_order holds each of 0 to 63 once. pattern[s, 0] = row_order[s]; the labels of one row are distinct; each label in row s is that of a block row stored on the same device as s, on one of the two devices one step away along row (wrapping), or on the next device along col (wrapping). Stored position s lies on device index (s // 2) in the order of the mesh with row slowest.
All inputs are finite; a program needn't handle non-finite values.
Results may differ from the reference program's by a relative error of at most 0.00011.
Values sent between devices are 32-bit elements; how exact they have to be, the bound alone decides.
No kernel may reach another device: no remote copies, remote signals or barrier semaphores. Data moves between devices by JAX's collectives and lax.ppermute only.
A program may use at most 128 MiB of HBM per device.

```python
import jax
import jax.numpy as jnp
from jax import lax

BLOCK = 128
SLOTS = 8
ROWS_DEV = 2
NBLK = 64
N_ROW = 8
N_COL = 4


def shared_order(key):
    return jax.random.permutation(jax.random.fold_in(key, 11), NBLK).astype(jnp.int32)


def draw_row_order(key, part):
    return shared_order(key)


def draw_pattern(key, part):
    ordering = shared_order(key)
    row_ids = jnp.arange(NBLK, dtype=jnp.int32)
    candidates = 4 * ROWS_DEV
    cand_ids = jnp.arange(candidates, dtype=jnp.int32)
    scores = jax.random.randint(jax.random.fold_in(key, 12), (NBLK, candidates), 0, 2 ** 20) * candidates + cand_ids[None, :]
    self_cand = ROWS_DEV + row_ids % ROWS_DEV
    scores = jnp.where(cand_ids[None, :] == self_cand[:, None], -1, scores)
    unused, chosen_ids = lax.top_k(scores, SLOTS - 1)
    region = chosen_ids // ROWS_DEV
    offset = chosen_ids % ROWS_DEV
    device = row_ids // ROWS_DEV
    row_of = (device // N_COL)[:, None]
    col_of = (device % N_COL)[:, None]
    prev_dev = (row_of + N_ROW - 1) % N_ROW * N_COL + col_of
    next_dev = (row_of + 1) % N_ROW * N_COL + col_of
    own_dev = row_of * N_COL + col_of
    side_dev = row_of * N_COL + (col_of + 1) % N_COL
    target = jnp.where(region == 0, prev_dev, jnp.where(region == 1, own_dev, jnp.where(region == 2, next_dev, side_dev)))
    position = (target * ROWS_DEV + offset).astype(jnp.int32)
    columns_all = jnp.concatenate([row_ids[:, None], position], axis=1)
    return ordering[columns_all]


def block_matrix(key):
    full_shape = (NBLK, BLOCK, SLOTS * BLOCK)
    random_part = jax.random.normal(key, full_shape, jnp.float32)
    identity = (jnp.arange(SLOTS * BLOCK)[None, :] == jnp.arange(BLOCK)[:, None]).astype(jnp.float32)
    return 0.7 / BLOCK ** 0.5 * random_part + identity[None]


def draw_sqrt_iterate(key, part):
    return block_matrix(jax.random.fold_in(key, 21))


def draw_inverse_iterate(key, part):
    return block_matrix(jax.random.fold_in(key, 22))


def touch_ends(drawn, key, smallest, top_value):
    longest = drawn.shape.index(max(drawn.shape))
    spots = []
    for shift in (0, 1):
        where = [jax.random.randint(jax.random.fold_in(key, axis), (), 0, length) for axis, length in enumerate(drawn.shape)]
        where[longest] = (where[longest] + shift) % drawn.shape[longest]
        spots.append(tuple(where))
    return drawn.at[spots[0]].set(smallest).at[spots[1]].set(top_value)


def setup_inputs(seed: int = 0) -> dict:
    seeds = jax.random.split(jax.random.key(seed), 6)
    sqrt_iterate = draw_sqrt_iterate(jax.random.fold_in(seeds[5], 71), 0)
    inverse_iterate = draw_inverse_iterate(jax.random.fold_in(seeds[5], 71), 0)
    pattern = draw_pattern(jax.random.fold_in(seeds[5], 71), 0)
    keep_mask = touch_ends((jax.random.randint(seeds[3], (NBLK, SLOTS), 0, 4) < 3).astype(jnp.int32), jax.random.fold_in(seeds[3], 1), 0, 1)
    row_order = draw_row_order(jax.random.fold_in(seeds[5], 71), 0)
    return dict(sqrt_iterate=sqrt_iterate, inverse_iterate=inverse_iterate, pattern=pattern, keep_mask=keep_mask, row_order=row_order)


PRECISE = lax.Precision.HIGHEST

def filtered_product(left_factor, right_factor, position, selector, kept_cols):
    block_rows, block_size, row_width = left_factor.shape
    slot_count = row_width // block_size

    def row_product(row_items):
        row_block, positions, row_selector, keep_row = row_items
        picked = right_factor[positions].reshape(slot_count, block_size, slot_count, block_size)
        chosen = jnp.einsum('kimj,kpm->kipj', picked, row_selector, precision=PRECISE)
        chosen = chosen.reshape(row_width, row_width)
        return jnp.dot(row_block, chosen, precision=PRECISE, preferred_element_type=jnp.float32) * keep_row
    return lax.map(row_product, (left_factor, position, selector, kept_cols))

def reference(sqrt_iterate, inverse_iterate, pattern, keep_mask, row_order):
    block_rows, block_size, row_width = sqrt_iterate.shape
    slot_count = row_width // block_size
    inverse_order = jnp.zeros((block_rows,), jnp.int32).at[row_order].set(jnp.arange(block_rows, dtype=jnp.int32))
    position = inverse_order[pattern]
    selector = (pattern[position][:, :, None, :] == pattern[:, None, :, None]).astype(jnp.float32)
    slot_ids = jnp.arange(slot_count, dtype=jnp.int32)
    kept = jnp.maximum(keep_mask, (slot_ids == 0).astype(jnp.int32)[None, :])
    kept_cols = jnp.repeat(kept.astype(jnp.float32), block_size, axis=1)[:, None, :]
    identity = (jnp.arange(row_width)[None, :] == jnp.arange(block_size)[:, None]).astype(jnp.float32)
    product = filtered_product(inverse_iterate, sqrt_iterate, position, selector, kept_cols)
    factor = 1.5 * identity[None] - 0.5 * product
    sqrt_next = filtered_product(sqrt_iterate, factor, position, selector, kept_cols)
    inverse_next = filtered_product(factor, inverse_iterate, position, selector, kept_cols)
    return (sqrt_next, inverse_next)
```

```python
import functools

import jax
import jax.numpy as jnp
from jax import lax
from jax.experimental import pallas as pl
from jax.experimental.pallas import tpu as pltpu
from jax.sharding import PartitionSpec as P

PREV, OWN, NEXT, SIDE = range(4)
ROWS = 2
SLOTS = 8
SLOT_AT, KEPT_AT, KEPT_PREV_AT, KEPT_NEXT_AT, TABLE = 0, 16, 32, 36, 40
LARGEST = float(jnp.finfo(jnp.bfloat16).max)
VMEM_LIMIT = 24 * 2**20


def split(value):
    clipped = jnp.clip(value, -LARGEST, LARGEST)
    high = clipped.astype(jnp.bfloat16)
    low = (value - high.astype(jnp.float32)).astype(jnp.bfloat16)
    return high, low


def products(*pairs):
    left = [part for (high, low), _ in pairs for part in (high, low, high)]
    right = [part for _, (high, low) in pairs for part in (high, high, low)]
    return jnp.dot(
        jnp.concatenate(left, axis=1),
        jnp.concatenate(right, axis=0),
        preferred_element_type=jnp.float32,
    )


def filtered(table, value, region, scale=None, base=KEPT_AT, width=SLOTS):
    size = value.shape[0] // ROWS
    rows = []
    for i in range(ROWS):
        row = []
        for j in range(ROWS):
            kept = table[base + i * width + region * ROWS + j].astype(jnp.float32)
            if scale is not None:
                kept = kept * scale
            row.append(value[i * size:(i + 1) * size, j * size:(j + 1) * size] * kept)
        rows.append(jnp.concatenate(row, axis=1))
    return jnp.concatenate(rows, axis=0)


def store_slots(table, out, value, region):
    size = out.shape[1]
    for i in range(ROWS):
        for j in range(ROWS):
            slot = table[SLOT_AT + i * SLOTS + region * ROWS + j]
            out[i, :, pl.ds(pl.multiple_of(slot * size, size), size)] = value[
                i * size:(i + 1) * size, j * size:(j + 1) * size
            ]


def fill_table(row_devices, col_devices, pattern, keep, order, table):
    row = lax.axis_index("row")
    col = lax.axis_index("col")

    def first(row_of, col_of):
        return (lax.rem(row_of, row_devices) * col_devices + lax.rem(col_of, col_devices)) * ROWS

    prev = first(row + row_devices - 1, col)
    own = first(row, col)
    nxt = first(row + 1, col)
    side = first(row, col + 1)
    labels = [order[start + j] for start in (prev, own, nxt, side) for j in range(ROWS)]
    own_labels = labels[OWN * ROWS:(OWN + 1) * ROWS]

    def look_up(stored, wanted, slot_at, kept_at):
        slots = [jnp.int32(0)] * len(wanted)
        kepts = [jnp.int32(0)] * len(wanted)
        for k in range(SLOTS):
            label = pattern[k, stored]
            flag = jnp.int32(1) if k == 0 else (keep[k, stored] == 1).astype(jnp.int32)
            for j, want in enumerate(wanted):
                same = label == want
                slots[j] = jnp.where(same, k, slots[j])
                kepts[j] = jnp.where(same, flag, kepts[j])
        for j in range(len(wanted)):
            if slot_at is not None:
                table[slot_at + j] = slots[j]
            table[kept_at + j] = kepts[j]

    for i in range(ROWS):
        look_up(own + i, labels, SLOT_AT + i * SLOTS, KEPT_AT + i * SLOTS)
        look_up(prev + i, own_labels, None, KEPT_PREV_AT + i * ROWS)
        look_up(nxt + i, own_labels, None, KEPT_NEXT_AT + i * ROWS)


def gather(table, source, i, j):
    size = source.shape[1]
    slot = table[SLOT_AT + i * SLOTS + j]
    return source[i, :, pl.ds(pl.multiple_of(slot * size, size), size)]


def pack(table, source, to_prev, to_next, side_own, side):
    size = source.shape[1]
    for i in range(ROWS):
        rows = slice(i * size, (i + 1) * size)
        for j in range(SLOTS):
            region, offset = divmod(j, ROWS)
            cols = slice(offset * size, (offset + 1) * size)
            block = gather(table, source, i, j)
            if region == PREV:
                to_prev[0, rows, cols] = block
            elif region == OWN:
                to_prev[1, rows, cols] = block
                to_next[0, rows, cols] = block
                side_own[rows, cols] = block
            elif region == NEXT:
                to_next[1, rows, cols] = block
            else:
                side[rows, cols] = block


def pack_kernel(
    row_devices, col_devices, pattern, keep, order, sqrt_ref, inv_ref,
    table, y_to_prev, y_to_next, y_side, z_to_prev, z_to_next, z_side, to_side,
):
    fill_table(row_devices, col_devices, pattern, keep, order, table)
    pack(table, sqrt_ref, y_to_prev, y_to_next, to_side.at[0], y_side)
    pack(table, inv_ref, z_to_prev, z_to_next, to_side.at[1], z_side)


def factor_own_kernel(table, y_to_prev, z_to_prev, z_to_next, y_prev, y_next, factor):
    total = products(
        (split(z_to_prev[0]), split(y_prev[1])),
        (split(z_to_prev[1]), split(y_to_prev[1])),
        (split(z_to_next[1]), split(y_next[0])),
    )
    rows = lax.broadcasted_iota(jnp.int32, total.shape, 0)
    cols = lax.broadcasted_iota(jnp.int32, total.shape, 1)
    identity = jnp.where(rows == cols, 1.5, 0.0)
    factor[...] = identity + filtered(table, total, OWN, -0.5)


def factor_rest_kernel(
    table, y_to_prev, y_to_next, y_side, z_to_prev, z_to_next, z_side,
    y_prev, y_next, from_side, factors, partial,
):
    y_own = split(y_to_prev[1])
    z_own = split(z_to_prev[1])
    parts = (
        (PREV, z_to_prev[0], y_prev[0], y_to_prev[0]),
        (NEXT, z_to_next[1], y_next[1], y_to_next[1]),
        (SIDE, z_side[...], from_side[0], y_side[...]),
    )
    for at, (region, z_here, y_there, y_here) in enumerate(parts):
        total = products((split(z_here), split(y_there)), (z_own, split(y_here)))
        factor = filtered(table, total, region, -0.5)
        factors[at] = factor
        partial[at] = products((y_own, split(factor)))


def inverse_kernel(
    table, y_to_prev, y_to_next, z_to_prev, z_to_next, z_side,
    y_prev, y_next, z_prev, z_next, from_side, factor_own, factors,
    inverse_next, sqrt_own,
):
    y_own = split(y_to_prev[1])
    zp_own, zp_next = split(z_prev[0]), split(z_prev[1])
    zn_prev, zn_own = split(z_next[0]), split(z_next[1])
    prev_total = products((zp_own, split(y_prev[1])), (zp_next, y_own))
    prev_next = split(filtered(table, prev_total, 0, -0.5, KEPT_PREV_AT, ROWS))
    next_total = products((zn_own, split(y_next[0])), (zn_prev, y_own))
    next_prev = split(filtered(table, next_total, 0, -0.5, KEPT_NEXT_AT, ROWS))
    f_own = split(factor_own[...])
    f_prev, f_next, f_side = (split(factors[at]) for at in range(3))
    value = products(
        (split(y_to_prev[0]), prev_next), (y_own, f_own), (split(y_to_next[1]), next_prev)
    )
    sqrt_own[...] = filtered(table, value, OWN)
    results = (
        (PREV, ((f_prev, zp_own), (f_own, split(z_to_prev[0])))),
        (OWN, ((f_prev, zp_next), (f_own, split(z_to_prev[1])), (f_next, zn_prev))),
        (NEXT, ((f_own, split(z_to_next[1])), (f_next, zn_own))),
        (SIDE, ((f_own, split(z_side[...])), (f_side, split(from_side[1])))),
    )
    for region, pairs in results:
        store_slots(table, inverse_next, filtered(table, products(*pairs), region), region)


def sqrt_kernel(
    table, y_to_prev, y_to_next, y_side, partial, sqrt_own, f_prev, f_next, f_side, sqrt_next
):
    parts = (
        (PREV, y_to_prev[0], f_prev),
        (NEXT, y_to_next[1], f_next),
        (SIDE, y_side[...], f_side),
    )
    store_slots(table, sqrt_next, sqrt_own[...], OWN)
    for at, (region, y_here, f_there) in enumerate(parts):
        value = partial[at] + products((split(y_here), split(f_there[...])))
        store_slots(table, sqrt_next, filtered(table, value, region), region)


def call(kernel, outs, operands, terms):
    def spec(array):
        small = array.dtype == jnp.int32
        return pl.BlockSpec(memory_space=pltpu.SMEM if small else pltpu.VMEM)

    moved = sum(array.size * 4 for array in (*outs, *operands))
    return pl.pallas_call(
        kernel,
        out_shape=outs,
        in_specs=[spec(array) for array in operands],
        out_specs=jax.tree.map(spec, outs),
        compiler_params=pltpu.CompilerParams(vmem_limit_bytes=VMEM_LIMIT),
        cost_estimate=pl.CostEstimate(
            flops=terms * 6 * 256**3, bytes_accessed=moved, transcendentals=0
        ),
    )(*operands)


def shifted(value, axis, distance):
    count = lax.axis_size(axis)
    return lax.ppermute(value, axis, [((i + distance) % count, i) for i in range(count)])


def local(sqrt_iterate, inverse_iterate, pattern, keep_mask, row_order):
    rows_dev, block, width = sqrt_iterate.shape
    row_devices, col_devices = lax.axis_size("row"), lax.axis_size("col")
    assert rows_dev == ROWS and width == SLOTS * block and pattern.shape[1] == SLOTS
    assert row_devices > 3 and col_devices > 2
    size = ROWS * block

    def shape(*dims):
        return jax.ShapeDtypeStruct(dims, jnp.float32)

    pair, one = shape(2, size, size), shape(size, size)
    table, y_to_prev, y_to_next, y_side, z_to_prev, z_to_next, z_side, to_side = call(
        functools.partial(pack_kernel, row_devices, col_devices),
        (jax.ShapeDtypeStruct((TABLE,), jnp.int32), pair, pair, one, pair, pair, one, pair),
        (pattern.T, keep_mask.T, row_order, sqrt_iterate, inverse_iterate),
        0,
    )
    y_next = shifted(y_to_prev, "row", 1)
    y_prev = shifted(y_to_next, "row", -1)
    from_side = shifted(to_side, "col", 1)
    z_next = shifted(z_to_prev, "row", 1)
    z_prev = shifted(z_to_next, "row", -1)
    (factor_own,) = call(
        factor_own_kernel,
        (one,),
        (table, y_to_prev, z_to_prev, z_to_next, y_prev, y_next),
        3,
    )
    f_side = shifted(factor_own, "col", 1)
    f_next = shifted(factor_own, "row", 1)
    f_prev = shifted(factor_own, "row", -1)
    factors, partial = call(
        factor_rest_kernel,
        (shape(3, size, size), shape(3, size, size)),
        (
            table, y_to_prev, y_to_next, y_side, z_to_prev, z_to_next, z_side,
            y_prev, y_next, from_side,
        ),
        9,
    )
    inverse_next, sqrt_own = call(
        inverse_kernel,
        (shape(rows_dev, block, width), one),
        (
            table, y_to_prev, y_to_next, z_to_prev, z_to_next, z_side,
            y_prev, y_next, z_prev, z_next, from_side, factor_own, factors,
        ),
        16,
    )
    (sqrt_next,) = call(
        sqrt_kernel,
        (shape(rows_dev, block, width),),
        (table, y_to_prev, y_to_next, y_side, partial, sqrt_own, f_prev, f_next, f_side),
        3,
    )
    return sqrt_next, inverse_next


def solution(mesh):
    rows = P(("row", "col"), None, None)
    return jax.shard_map(
        local,
        mesh=mesh,
        in_specs=(rows, rows, P(), P(), P()),
        out_specs=(rows, rows),
        check_vma=False,
    )
```

```python
import functools

import jax
import jax.numpy as jnp
from jax import lax
from jax.experimental import pallas as pl
from jax.experimental.pallas import tpu as pltpu
from jax.sharding import PartitionSpec as P

PEER, OWN, MATE, SIDE = range(4)
ROWS = 2
SLOTS = 8
SLOT_AT, KEPT_AT, KEPT_PEER_AT, KEPT_MATE_AT, TABLE = 0, 16, 32, 36, 40
LARGEST = float(jnp.finfo(jnp.bfloat16).max)
VMEM_LIMIT = 24 * 2**20


def split(value):
    clipped = jnp.clip(value, -LARGEST, LARGEST)
    high = clipped.astype(jnp.bfloat16)
    low = (value - high.astype(jnp.float32)).astype(jnp.bfloat16)
    return high, low


def products(*pairs):
    left = [part for (high, low), _ in pairs for part in (high, low, high)]
    right = [part for _, (high, low) in pairs for part in (high, high, low)]
    return jnp.dot(
        jnp.concatenate(left, axis=1),
        jnp.concatenate(right, axis=0),
        preferred_element_type=jnp.float32,
    )


def filtered(table, value, region, scale=None, base=KEPT_AT, width=SLOTS):
    size = value.shape[0] // ROWS
    rows = []
    for i in range(ROWS):
        row = []
        for j in range(ROWS):
            kept = table[base + i * width + region * ROWS + j].astype(jnp.float32)
            if scale is not None:
                kept = kept * scale
            row.append(value[i * size:(i + 1) * size, j * size:(j + 1) * size] * kept)
        rows.append(jnp.concatenate(row, axis=1))
    return jnp.concatenate(rows, axis=0)


def fill_table(row_devices, col_devices, pattern, keep, order, table):
    row = lax.axis_index("row")
    col = lax.axis_index("col")
    odd = lax.rem(row, 2)

    def first(row_of, col_of):
        return (lax.rem(row_of, row_devices) * col_devices + lax.rem(col_of, col_devices)) * ROWS

    peer = first(row + row_devices - 1 + 2 * odd, col)
    own = first(row, col)
    mate = first(row + 1 - 2 * odd, col)
    side = first(row, col + 1)
    labels = [order[start + j] for start in (peer, own, mate, side) for j in range(ROWS)]
    own_labels = labels[OWN * ROWS:(OWN + 1) * ROWS]

    def look_up(stored, wanted, slot_at, kept_at):
        slots = [jnp.int32(0)] * len(wanted)
        kepts = [jnp.int32(0)] * len(wanted)
        for k in range(SLOTS):
            label = pattern[k, stored]
            flag = jnp.int32(1) if k == 0 else (keep[k, stored] == 1).astype(jnp.int32)
            for j, want in enumerate(wanted):
                same = label == want
                slots[j] = jnp.where(same, k, slots[j])
                kepts[j] = jnp.where(same, flag, kepts[j])
        for j in range(len(wanted)):
            if slot_at is not None:
                table[slot_at + j] = slots[j]
            table[kept_at + j] = kepts[j]

    for i in range(ROWS):
        look_up(own + i, labels, SLOT_AT + i * SLOTS, KEPT_AT + i * SLOTS)
        look_up(peer + i, own_labels, None, KEPT_PEER_AT + i * ROWS)
        look_up(mate + i, own_labels, None, KEPT_MATE_AT + i * ROWS)


def gather(table, source, places):
    size = source.shape[1]
    for i in range(ROWS):
        rows = slice(i * size, (i + 1) * size)
        for j in range(SLOTS):
            region, offset = divmod(j, ROWS)
            cols = slice(offset * size, (offset + 1) * size)
            slot = table[SLOT_AT + i * SLOTS + j]
            block = source[i, :, pl.ds(pl.multiple_of(slot * size, size), size)]
            for place in places[region]:
                place[rows, cols] = block


def pack_sqrt_kernel(
    row_devices, col_devices, pattern, keep, order, sqrt_iterate,
    table, y_peer, y_mate, y_side,
    pattern_here, keep_here, order_here, sqrt_here, sems,
):
    copies = [
        pltpu.make_async_copy(source, here, sems.at[at])
        for at, (source, here) in enumerate((
            (order, order_here), (pattern, pattern_here), (keep, keep_here),
            (sqrt_iterate, sqrt_here),
        ))
    ]
    for copy in copies:
        copy.start()
    for copy in copies[:3]:
        copy.wait()
    fill_table(row_devices, col_devices, pattern_here, keep_here, order_here, table)
    copies[3].wait()
    places = ((y_peer.at[0],), (y_peer.at[1], y_mate.at[1]), (y_mate.at[0],), (y_side,))
    gather(table, sqrt_here, places)


def pack_inverse_kernel(table, y_peer, inverse_iterate, z_peer, z_mate, z_side, to_side):
    to_side[0] = y_peer[1]
    places = ((z_peer,), (z_mate.at[1], to_side.at[1]), (z_mate.at[0],), (z_side,))
    gather(table, inverse_iterate, places)


def mate_kernel(
    table, y_peer, y_mate, z_peer, z_mate, mate_y,
    z_to_peer, factor_mate, own_partial, peer_partial,
):
    z_to_peer[0] = z_peer[...]
    z_to_peer[1] = z_mate[1]
    z_own, z_to_mate = split(z_mate[1]), split(z_mate[0])
    own_partial[...] = products((z_own, split(y_mate[1])), (z_to_mate, split(mate_y[0])))
    total = products((z_own, split(y_mate[0])), (z_to_mate, split(mate_y[1])))
    factor_mate[...] = filtered(table, total, MATE, -0.5)
    peer_partial[...] = products((z_own, split(y_peer[0])))


def factor_own_kernel(table, own_partial, z_peer, peer_y, factor_own):
    total = own_partial[...] + products((split(z_peer[...]), split(peer_y[0])))
    rows = lax.broadcasted_iota(jnp.int32, total.shape, 0)
    cols = lax.broadcasted_iota(jnp.int32, total.shape, 1)
    factor_own[...] = jnp.where(rows == cols, 1.5, 0.0) + filtered(table, total, OWN, -0.5)


Y_MATE, Z_MATE, Z_SIDE = range(3)
Y_OWN_PART, Y_PEER_PART, Y_SIDE_PART, Z_OWN_PART, Z_PEER_PART = range(5)
Y_PEER, Y_OWN, Y_SIDE, F_PEER, PEER_Y = range(5)


def middle_kernel(
    table, y_peer, y_mate, y_side, z_peer, z_mate, z_side, mate_y, mate_z, peer_y, from_side,
    factor_mate, peer_partial, factor_own, mate_factor,
    finished, partial, ready,
):
    def keep(at, parts):
        ready[at, 0], ready[at, 1] = parts

    y_own, z_own = split(y_peer[1]), split(z_mate[1])
    y_to_mate, z_to_mate = split(y_mate[0]), split(z_mate[0])
    y_to_side, z_to_side = split(y_side[...]), split(z_side[...])
    z_to_peer = split(z_peer[...])
    f_own, f_mate = split(factor_own[...]), split(factor_mate[...])
    mate_z_mate, mate_z_own = split(mate_z[0]), split(mate_z[1])
    keep(Y_OWN, y_own)
    keep(Y_SIDE, y_to_side)
    keep(Y_PEER, split(y_peer[0]))
    keep(PEER_Y, split(peer_y[0]))

    total = peer_partial[...] + products((z_to_peer, split(peer_y[1])))
    f_peer = split(filtered(table, total, PEER, -0.5))
    keep(F_PEER, f_peer)
    total = products((z_own, y_to_side), (z_to_side, split(from_side[0])))
    f_side = split(filtered(table, total, SIDE, -0.5))
    total = products((mate_z_own, split(mate_y[0])), (mate_z_mate, y_own))
    mate_f_mate = split(filtered(table, total, 0, -0.5, KEPT_MATE_AT, ROWS))

    partial[Y_PEER_PART] = products((y_own, f_peer))
    partial[Y_SIDE_PART] = products((y_own, f_side))
    partial[Y_OWN_PART] = products((y_to_mate, mate_f_mate), (y_own, f_own))
    partial[Z_PEER_PART] = products((f_own, z_to_peer))
    partial[Z_OWN_PART] = products((f_mate, mate_z_mate), (f_own, z_own))
    value = products((y_own, f_mate), (y_to_mate, split(mate_factor[...])))
    finished[Y_MATE] = filtered(table, value, MATE)
    value = products((f_mate, mate_z_own), (f_own, z_to_mate))
    finished[Z_MATE] = filtered(table, value, MATE)
    value = products((f_own, z_to_side), (f_side, split(from_side[1])))
    finished[Z_SIDE] = filtered(table, value, SIDE)


def last_kernel(
    table, finished, partial, ready, peer_z, peer_factor, side_factor,
    sqrt_next, inverse_next, result, sems,
):
    size = sqrt_next.shape[1]
    started = []

    def write(source, out, region):
        for i in range(ROWS):
            for j in range(ROWS):
                slot = table[SLOT_AT + i * SLOTS + region * ROWS + j]
                copy = pltpu.make_async_copy(
                    source.at[pl.ds(i * size, size), pl.ds(j * size, size)],
                    out.at[i, :, pl.ds(pl.multiple_of(slot * size, size), size)],
                    sems.at[len(started)],
                )
                copy.start()
                started.append(copy)

    def finish(at, value, out, region):
        result[at] = filtered(table, value, region)
        write(result.at[at], out, region)

    def held(at):
        return ready[at, 0], ready[at, 1]

    write(finished.at[Y_MATE], sqrt_next, MATE)
    write(finished.at[Z_MATE], inverse_next, MATE)
    write(finished.at[Z_SIDE], inverse_next, SIDE)
    peer_z_peer, peer_z_own = split(peer_z[0]), split(peer_z[1])
    f_peer, y_peer = held(F_PEER), held(Y_PEER)
    value = partial[Z_PEER_PART] + products((f_peer, peer_z_own))
    finish(0, value, inverse_next, PEER)
    value = partial[Z_OWN_PART] + products((f_peer, peer_z_peer))
    finish(1, value, inverse_next, OWN)
    total = products((peer_z_own, held(PEER_Y)), (peer_z_peer, held(Y_OWN)))
    peer_f_peer = split(filtered(table, total, 0, -0.5, KEPT_PEER_AT, ROWS))
    value = partial[Y_SIDE_PART] + products((held(Y_SIDE), split(side_factor[...])))
    finish(2, value, sqrt_next, SIDE)
    value = partial[Y_PEER_PART] + products((y_peer, split(peer_factor[...])))
    finish(3, value, sqrt_next, PEER)
    value = partial[Y_OWN_PART] + products((y_peer, peer_f_peer))
    finish(4, value, sqrt_next, OWN)
    for copy in started:
        copy.wait()


def call(kernel, outs, operands, terms, scratch=(), hbm_in=(), hbm_out=False):
    def spec(array, outside=False):
        if outside:
            return pl.BlockSpec(memory_space=pltpu.HBM)
        small = array.dtype == jnp.int32
        return pl.BlockSpec(memory_space=pltpu.SMEM if small else pltpu.VMEM)

    moved = sum(array.size * array.dtype.itemsize for array in (*outs, *operands))
    operands = [
        pltpu.with_memory_space_constraint(array, pltpu.HBM) if at in hbm_in else array
        for at, array in enumerate(operands)
    ]
    return pl.pallas_call(
        kernel,
        out_shape=outs,
        in_specs=[spec(array, at in hbm_in) for at, array in enumerate(operands)],
        out_specs=tuple(spec(array, hbm_out) for array in outs),
        scratch_shapes=scratch,
        compiler_params=pltpu.CompilerParams(vmem_limit_bytes=VMEM_LIMIT),
        cost_estimate=pl.CostEstimate(
            flops=terms * 6 * 256**3, bytes_accessed=moved, transcendentals=0
        ),
    )(*operands)


def local(sqrt_iterate, inverse_iterate, pattern, keep_mask, row_order):
    rows_dev, block, width = sqrt_iterate.shape
    row_devices, col_devices = lax.axis_size("row"), lax.axis_size("col")
    assert rows_dev == ROWS and width == SLOTS * block and pattern.shape[1] == SLOTS
    assert row_devices > 3 and row_devices % 2 == 0 and col_devices > 2
    size = ROWS * block

    def to_mate(value):
        return lax.ppermute(value, "row", [(i, i ^ 1) for i in range(row_devices)])

    def to_peer(value):
        route = [(i, (i + (1 if i % 2 else -1)) % row_devices) for i in range(row_devices)]
        return lax.ppermute(value, "row", route)

    def to_side(value):
        route = [((i + 1) % col_devices, i) for i in range(col_devices)]
        return lax.ppermute(value, "col", route)

    def shape(*dims, dtype=jnp.float32):
        return jax.ShapeDtypeStruct(dims, dtype)

    one, pair = shape(size, size), shape(2, size, size)
    table, y_peer, y_mate, y_side = call(
        functools.partial(pack_sqrt_kernel, row_devices, col_devices),
        (shape(TABLE, dtype=jnp.int32), pair, pair, one),
        (pattern.T, keep_mask.T, row_order, sqrt_iterate),
        0,
        scratch=[
            pltpu.SMEM(pattern.T.shape, jnp.int32),
            pltpu.SMEM(keep_mask.T.shape, jnp.int32),
            pltpu.SMEM(row_order.shape, jnp.int32),
            pltpu.VMEM(sqrt_iterate.shape, jnp.float32),
            pltpu.SemaphoreType.DMA((4,)),
        ],
        hbm_in=range(4),
    )
    mate_y = to_mate(y_mate)
    peer_y = to_peer(y_peer)
    z_peer, z_mate, z_side, own_pair = call(
        pack_inverse_kernel, (one, pair, one, pair), (table, y_peer, inverse_iterate), 0
    )
    from_side = to_side(own_pair)
    mate_z = to_mate(z_mate)
    z_to_peer, factor_mate, own_partial, peer_partial = call(
        mate_kernel, (pair, one, one, one), (table, y_peer, y_mate, z_peer, z_mate, mate_y), 5
    )
    peer_z = to_peer(z_to_peer)
    (factor_own,) = call(factor_own_kernel, (one,), (table, own_partial, z_peer, peer_y), 1)
    mate_factor = to_mate(factor_own)
    peer_factor = to_peer(factor_own)
    side_factor = to_side(factor_own)
    finished, partial, ready = call(
        middle_kernel,
        (
            shape(3, size, size), shape(5, size, size),
            shape(5, 2, size, size, dtype=jnp.bfloat16),
        ),
        (
            table, y_peer, y_mate, y_side, z_peer, z_mate, z_side, mate_y, mate_z, peer_y,
            from_side, factor_mate, peer_partial, factor_own, mate_factor,
        ),
        19,
    )
    sqrt_next, inverse_next = call(
        last_kernel,
        (shape(rows_dev, block, width), shape(rows_dev, block, width)),
        (table, finished, partial, ready, peer_z, peer_factor, side_factor),
        7,
        scratch=[pltpu.VMEM((5, size, size), jnp.float32), pltpu.SemaphoreType.DMA((32,))],
        hbm_out=True,
    )
    return sqrt_next, inverse_next


def solution(mesh):
    rows = P(("row", "col"), None, None)
    return jax.shard_map(
        local,
        mesh=mesh,
        in_specs=(rows, rows, P(), P(), P()),
        out_specs=(rows, rows),
        check_vma=False,
    )
```

```python
import functools

import jax
import jax.numpy as jnp
from jax import lax
from jax.experimental import pallas as pl
from jax.experimental.pallas import tpu as pltpu
from jax.sharding import PartitionSpec as P

PEER, OWN, MATE, SIDE = range(4)
ROWS = 2
SLOTS = 8
SLOT_AT, KEPT_AT, KEPT_PEER_AT, KEPT_MATE_AT, TABLE = 0, 16, 32, 36, 40
LARGEST = float(jnp.finfo(jnp.bfloat16).max)
VMEM_LIMIT = 24 * 2**20


def split(value):
    clipped = jnp.clip(value, -LARGEST, LARGEST)
    high = clipped.astype(jnp.bfloat16)
    low = (value - high.astype(jnp.float32)).astype(jnp.bfloat16)
    return high, low


def products(*pairs):
    left = [part for (high, low), _ in pairs for part in (high, low, high)]
    right = [part for _, (high, low) in pairs for part in (high, high, low)]
    return jnp.dot(
        jnp.concatenate(left, axis=1),
        jnp.concatenate(right, axis=0),
        preferred_element_type=jnp.float32,
    )


def filtered(table, value, region, scale=None, base=KEPT_AT, width=SLOTS):
    size = value.shape[0] // ROWS
    rows = []
    for i in range(ROWS):
        row = []
        for j in range(ROWS):
            kept = table[base + i * width + region * ROWS + j].astype(jnp.float32)
            if scale is not None:
                kept = kept * scale
            row.append(value[i * size:(i + 1) * size, j * size:(j + 1) * size] * kept)
        rows.append(jnp.concatenate(row, axis=1))
    return jnp.concatenate(rows, axis=0)


def neighbours(row_devices, col_devices, order):
    row = lax.axis_index("row")
    col = lax.axis_index("col")
    odd = lax.rem(row, 2)

    def first(row_of, col_of):
        return (lax.rem(row_of, row_devices) * col_devices + lax.rem(col_of, col_devices)) * ROWS

    starts = (
        first(row + row_devices - 1 + 2 * odd, col),
        first(row, col),
        first(row + 1 - 2 * odd, col),
        first(row, col + 1),
    )
    return starts, [order[start + j] for start in starts for j in range(ROWS)]


def find_slots(pattern, stored, wanted):
    slots = [jnp.int32(0)] * len(wanted)
    for k in range(SLOTS):
        label = pattern[k, stored]
        slots = [jnp.where(label == want, k, slot) for want, slot in zip(wanted, slots)]
    return slots


def fill_table(row_devices, col_devices, pattern, keep, order, table):
    starts, labels = neighbours(row_devices, col_devices, order)
    own_labels = labels[OWN * ROWS:(OWN + 1) * ROWS]

    def look_up(stored, wanted, slot_at, kept_at):
        for j, slot in enumerate(find_slots(pattern, stored, wanted)):
            if slot_at is not None:
                table[slot_at + j] = slot
            kept = (slot == 0) | (keep[slot, stored] == 1)
            table[kept_at + j] = kept.astype(jnp.int32)

    for i in range(ROWS):
        look_up(starts[OWN] + i, labels, SLOT_AT + i * SLOTS, KEPT_AT + i * SLOTS)
        look_up(starts[PEER] + i, own_labels, None, KEPT_PEER_AT + i * ROWS)
        look_up(starts[MATE] + i, own_labels, None, KEPT_MATE_AT + i * ROWS)


def gather(slot_of, source, places):
    size = source.shape[1]
    for i in range(ROWS):
        rows = slice(i * size, (i + 1) * size)
        for region, region_places in places.items():
            for j in range(ROWS):
                cols = slice(j * size, (j + 1) * size)
                start = pl.multiple_of(slot_of(i, region * ROWS + j) * size, size)
                block = source[i, :, pl.ds(start, size)]
                for place in region_places:
                    place[rows, cols] = block


def pack_first_kernel(
    row_devices, col_devices, pattern, order, sqrt_iterate,
    y_peer, y_mate, pattern_here, order_here, sqrt_here, sems,
):
    copies = [
        pltpu.make_async_copy(source, here, sems.at[at])
        for at, (source, here) in enumerate(
            ((order, order_here), (pattern, pattern_here), (sqrt_iterate, sqrt_here))
        )
    ]
    for copy in copies:
        copy.start()
    copies[0].wait()
    copies[1].wait()
    starts, labels = neighbours(row_devices, col_devices, order_here)
    wanted = labels[PEER * ROWS:(MATE + 1) * ROWS]
    slots = [find_slots(pattern_here, starts[OWN] + i, wanted) for i in range(ROWS)]
    copies[2].wait()
    places = {PEER: (y_peer.at[0],), OWN: (y_peer.at[1], y_mate.at[1]), MATE: (y_mate.at[0],)}
    gather(lambda i, j: slots[i][j], sqrt_here, places)


def pack_rest_kernel(
    row_devices, col_devices, pattern, keep, order, sqrt_iterate, inverse_iterate, y_peer,
    table, y_side, z_peer, z_mate, z_side, to_side,
    pattern_here, keep_here, order_here, sqrt_here, inverse_here, sems,
):
    copies = [
        pltpu.make_async_copy(source, here, sems.at[at])
        for at, (source, here) in enumerate((
            (order, order_here), (pattern, pattern_here), (keep, keep_here),
            (inverse_iterate, inverse_here), (sqrt_iterate, sqrt_here),
        ))
    ]
    for copy in copies:
        copy.start()
    to_side[0] = y_peer[1]
    for copy in copies[:3]:
        copy.wait()
    fill_table(row_devices, col_devices, pattern_here, keep_here, order_here, table)

    def slot_of(i, j):
        return table[SLOT_AT + i * SLOTS + j]

    places = {
        PEER: (z_peer,), OWN: (z_mate.at[1], to_side.at[1]), MATE: (z_mate.at[0],), SIDE: (z_side,)
    }
    copies[3].wait()
    gather(slot_of, inverse_here, places)
    copies[4].wait()
    gather(slot_of, sqrt_here, {SIDE: (y_side,)})


def mate_kernel(
    table, y_peer, y_mate, z_peer, z_mate, mate_y,
    z_to_peer, factor_mate, own_partial, peer_partial,
):
    z_to_peer[0] = z_peer[...]
    z_to_peer[1] = z_mate[1]
    z_own, z_to_mate = split(z_mate[1]), split(z_mate[0])
    own_partial[...] = products((z_own, split(y_mate[1])), (z_to_mate, split(mate_y[0])))
    total = products((z_own, split(y_mate[0])), (z_to_mate, split(mate_y[1])))
    factor_mate[...] = filtered(table, total, MATE, -0.5)
    peer_partial[...] = products((z_own, split(y_peer[0])))


def factor_own_kernel(table, own_partial, z_peer, peer_y, factor_own):
    total = own_partial[...] + products((split(z_peer[...]), split(peer_y[0])))
    rows = lax.broadcasted_iota(jnp.int32, total.shape, 0)
    cols = lax.broadcasted_iota(jnp.int32, total.shape, 1)
    factor_own[...] = jnp.where(rows == cols, 1.5, 0.0) + filtered(table, total, OWN, -0.5)


Y_MATE, Z_MATE, Z_SIDE = range(3)
Y_OWN_PART, Y_PEER_PART, Y_SIDE_PART, Z_OWN_PART, Z_PEER_PART = range(5)
Y_PEER, Y_OWN, Y_SIDE, F_PEER, PEER_Y = range(5)


def middle_kernel(
    table, y_peer, y_mate, y_side, z_peer, z_mate, z_side, mate_y, mate_z, peer_y, from_side,
    factor_mate, peer_partial, factor_own, mate_factor,
    finished, partial, ready,
):
    def keep(at, parts):
        ready[at, 0], ready[at, 1] = parts

    y_own, z_own = split(y_peer[1]), split(z_mate[1])
    y_to_mate, z_to_mate = split(y_mate[0]), split(z_mate[0])
    y_to_side, z_to_side = split(y_side[...]), split(z_side[...])
    z_to_peer = split(z_peer[...])
    f_own, f_mate = split(factor_own[...]), split(factor_mate[...])
    mate_z_mate, mate_z_own = split(mate_z[0]), split(mate_z[1])
    keep(Y_OWN, y_own)
    keep(Y_SIDE, y_to_side)
    keep(Y_PEER, split(y_peer[0]))
    keep(PEER_Y, split(peer_y[0]))

    total = peer_partial[...] + products((z_to_peer, split(peer_y[1])))
    f_peer = split(filtered(table, total, PEER, -0.5))
    keep(F_PEER, f_peer)
    total = products((z_own, y_to_side), (z_to_side, split(from_side[0])))
    f_side = split(filtered(table, total, SIDE, -0.5))
    total = products((mate_z_own, split(mate_y[0])), (mate_z_mate, y_own))
    mate_f_mate = split(filtered(table, total, 0, -0.5, KEPT_MATE_AT, ROWS))

    partial[Y_PEER_PART] = products((y_own, f_peer))
    partial[Y_SIDE_PART] = products((y_own, f_side))
    partial[Y_OWN_PART] = products((y_to_mate, mate_f_mate), (y_own, f_own))
    partial[Z_PEER_PART] = products((f_own, z_to_peer))
    partial[Z_OWN_PART] = products((f_mate, mate_z_mate), (f_own, z_own))
    value = products((y_own, f_mate), (y_to_mate, split(mate_factor[...])))
    finished[Y_MATE] = filtered(table, value, MATE)
    value = products((f_mate, mate_z_own), (f_own, z_to_mate))
    finished[Z_MATE] = filtered(table, value, MATE)
    value = products((f_own, z_to_side), (f_side, split(from_side[1])))
    finished[Z_SIDE] = filtered(table, value, SIDE)


class Writer:
    def __init__(self, table, result, sems):
        self.table, self.result, self.sems = table, result, sems
        self.started = []
        self.held = 0

    def write(self, source, out, region):
        size = out.shape[1]
        for i in range(ROWS):
            for j in range(ROWS):
                slot = self.table[SLOT_AT + i * SLOTS + region * ROWS + j]
                copy = pltpu.make_async_copy(
                    source.at[pl.ds(i * size, size), pl.ds(j * size, size)],
                    out.at[i, :, pl.ds(pl.multiple_of(slot * size, size), size)],
                    self.sems.at[len(self.started)],
                )
                copy.start()
                self.started.append(copy)

    def finish(self, value, out, region):
        place = self.result.at[self.held]
        self.held += 1
        place[...] = filtered(self.table, value, region)
        self.write(place, out, region)

    def wait(self):
        for copy in self.started:
            copy.wait()


def peer_kernel(
    table, finished, partial, ready, peer_z, sqrt_next, inverse_next, result, sems
):
    def held(at):
        return ready[at, 0], ready[at, 1]

    writer = Writer(table, result, sems)
    writer.write(finished.at[Y_MATE], sqrt_next, MATE)
    writer.write(finished.at[Z_MATE], inverse_next, MATE)
    writer.write(finished.at[Z_SIDE], inverse_next, SIDE)
    peer_z_peer, peer_z_own = split(peer_z[0]), split(peer_z[1])
    f_peer = held(F_PEER)
    value = partial[Z_PEER_PART] + products((f_peer, peer_z_own))
    writer.finish(value, inverse_next, PEER)
    value = partial[Z_OWN_PART] + products((f_peer, peer_z_peer))
    writer.finish(value, inverse_next, OWN)
    total = products((peer_z_own, held(PEER_Y)), (peer_z_peer, held(Y_OWN)))
    peer_f_peer = split(filtered(table, total, 0, -0.5, KEPT_PEER_AT, ROWS))
    value = partial[Y_OWN_PART] + products((held(Y_PEER), peer_f_peer))
    writer.finish(value, sqrt_next, OWN)
    writer.wait()


def last_kernel(
    table, partial, ready, peer_factor, side_factor, unfinished, sqrt_next, result, sems
):
    writer = Writer(table, result, sems)
    for region, part, here, factor in (
        (SIDE, Y_SIDE_PART, Y_SIDE, side_factor), (PEER, Y_PEER_PART, Y_PEER, peer_factor)
    ):
        left = (ready[here, 0], ready[here, 1])
        value = partial[part] + products((left, split(factor[...])))
        writer.finish(value, sqrt_next, region)
    writer.wait()


def call(kernel, outs, operands, terms, scratch=(), hbm_in=(), hbm_out=False, in_place=None):
    def spec(array, outside=False):
        if outside:
            return pl.BlockSpec(memory_space=pltpu.HBM)
        small = array.dtype == jnp.int32
        return pl.BlockSpec(memory_space=pltpu.SMEM if small else pltpu.VMEM)

    moved = sum(array.size * array.dtype.itemsize for array in (*outs, *operands))
    operands = [
        pltpu.with_memory_space_constraint(array, pltpu.HBM) if at in hbm_in else array
        for at, array in enumerate(operands)
    ]
    return pl.pallas_call(
        kernel,
        out_shape=outs,
        in_specs=[spec(array, at in hbm_in) for at, array in enumerate(operands)],
        out_specs=tuple(spec(array, hbm_out) for array in outs),
        scratch_shapes=scratch,
        input_output_aliases={} if in_place is None else {in_place: 0},
        compiler_params=pltpu.CompilerParams(vmem_limit_bytes=VMEM_LIMIT),
        cost_estimate=pl.CostEstimate(
            flops=terms * 6 * 256**3, bytes_accessed=moved, transcendentals=0
        ),
    )(*operands)


def local(sqrt_iterate, inverse_iterate, pattern, keep_mask, row_order):
    rows_dev, block, width = sqrt_iterate.shape
    row_devices, col_devices = lax.axis_size("row"), lax.axis_size("col")
    assert rows_dev == ROWS and width == SLOTS * block and pattern.shape[1] == SLOTS
    assert row_devices > 3 and row_devices % 2 == 0 and col_devices > 2
    size = ROWS * block

    def to_mate(value):
        return lax.ppermute(value, "row", [(i, i ^ 1) for i in range(row_devices)])

    def to_peer(value):
        route = [(i, (i + (1 if i % 2 else -1)) % row_devices) for i in range(row_devices)]
        return lax.ppermute(value, "row", route)

    def to_side(value):
        route = [((i + 1) % col_devices, i) for i in range(col_devices)]
        return lax.ppermute(value, "col", route)

    def shape(*dims, dtype=jnp.float32):
        return jax.ShapeDtypeStruct(dims, dtype)

    one, pair = shape(size, size), shape(2, size, size)
    labels = [
        pltpu.SMEM(pattern.T.shape, jnp.int32),
        pltpu.SMEM(keep_mask.T.shape, jnp.int32),
        pltpu.SMEM(row_order.shape, jnp.int32),
    ]
    y_peer, y_mate = call(
        functools.partial(pack_first_kernel, row_devices, col_devices),
        (pair, pair),
        (pattern.T, row_order, sqrt_iterate),
        0,
        scratch=[
            labels[0],
            labels[2],
            pltpu.VMEM(sqrt_iterate.shape, jnp.float32),
            pltpu.SemaphoreType.DMA((3,)),
        ],
        hbm_in=range(3),
    )
    mate_y = to_mate(y_mate)
    peer_y = to_peer(y_peer)
    table, y_side, z_peer, z_mate, z_side, own_pair = call(
        functools.partial(pack_rest_kernel, row_devices, col_devices),
        (shape(TABLE, dtype=jnp.int32), one, one, pair, one, pair),
        (pattern.T, keep_mask.T, row_order, sqrt_iterate, inverse_iterate, y_peer),
        0,
        scratch=[
            *labels,
            pltpu.VMEM(sqrt_iterate.shape, jnp.float32),
            pltpu.VMEM(inverse_iterate.shape, jnp.float32),
            pltpu.SemaphoreType.DMA((5,)),
        ],
        hbm_in=range(5),
    )
    mate_z = to_mate(z_mate)
    from_side = to_side(own_pair)
    z_to_peer, factor_mate, own_partial, peer_partial = call(
        mate_kernel, (pair, one, one, one), (table, y_peer, y_mate, z_peer, z_mate, mate_y), 5
    )
    peer_z = to_peer(z_to_peer)
    (factor_own,) = call(factor_own_kernel, (one,), (table, own_partial, z_peer, peer_y), 1)
    mate_factor = to_mate(factor_own)
    peer_factor = to_peer(factor_own)
    side_factor = to_side(factor_own)
    finished, partial, ready = call(
        middle_kernel,
        (
            shape(3, size, size), shape(5, size, size),
            shape(5, 2, size, size, dtype=jnp.bfloat16),
        ),
        (
            table, y_peer, y_mate, y_side, z_peer, z_mate, z_side, mate_y, mate_z, peer_y,
            from_side, factor_mate, peer_partial, factor_own, mate_factor,
        ),
        19,
    )
    unfinished, inverse_next = call(
        peer_kernel,
        (shape(rows_dev, block, width), shape(rows_dev, block, width)),
        (table, finished, partial, ready, peer_z),
        5,
        scratch=[pltpu.VMEM((3, size, size), jnp.float32), pltpu.SemaphoreType.DMA((24,))],
        hbm_out=True,
    )
    (sqrt_next,) = call(
        last_kernel,
        (shape(rows_dev, block, width),),
        (table, partial, ready, peer_factor, side_factor, unfinished),
        2,
        scratch=[pltpu.VMEM((2, size, size), jnp.float32), pltpu.SemaphoreType.DMA((8,))],
        hbm_in=(5,),
        hbm_out=True,
        in_place=5,
    )
    return sqrt_next, inverse_next


def solution(mesh):
    rows = P(("row", "col"), None, None)
    return jax.shard_map(
        local,
        mesh=mesh,
        in_specs=(rows, rows, P(), P(), P()),
        out_specs=(rows, rows),
        check_vma=False,
    )
```

```python
import functools

import jax
import jax.numpy as jnp
from jax import lax
from jax.experimental import pallas as pl
from jax.experimental.pallas import tpu as pltpu
from jax.sharding import PartitionSpec as P

PEER, OWN, MATE, SIDE = range(4)
ROWS = 2
SLOTS = 8
SLOT_AT, KEPT_AT, KEPT_PEER_AT, KEPT_MATE_AT, TABLE = 0, 16, 32, 36, 40
LARGEST = float(jnp.finfo(jnp.bfloat16).max)
VMEM_LIMIT = 24 * 2**20


def split(value):
    clipped = jnp.clip(value, -LARGEST, LARGEST)
    high = clipped.astype(jnp.bfloat16)
    low = (value - high.astype(jnp.float32)).astype(jnp.bfloat16)
    return high, low


def products(*pairs):
    left = [part for (high, low), _ in pairs for part in (high, low, high)]
    right = [part for _, (high, low) in pairs for part in (high, high, low)]
    return jnp.dot(
        jnp.concatenate(left, axis=1),
        jnp.concatenate(right, axis=0),
        preferred_element_type=jnp.float32,
    )


def filtered(table, value, region, scale=None, base=KEPT_AT, width=SLOTS):
    size = value.shape[0] // ROWS
    rows = []
    for i in range(ROWS):
        row = []
        for j in range(ROWS):
            kept = table[base + i * width + region * ROWS + j].astype(jnp.float32)
            if scale is not None:
                kept = kept * scale
            row.append(value[i * size:(i + 1) * size, j * size:(j + 1) * size] * kept)
        rows.append(jnp.concatenate(row, axis=1))
    return jnp.concatenate(rows, axis=0)


def neighbours(row_devices, col_devices, order):
    row = lax.axis_index("row")
    col = lax.axis_index("col")
    odd = lax.rem(row, 2)

    def first(row_of, col_of):
        return (lax.rem(row_of, row_devices) * col_devices + lax.rem(col_of, col_devices)) * ROWS

    starts = (
        first(row + row_devices - 1 + 2 * odd, col),
        first(row, col),
        first(row + 1 - 2 * odd, col),
        first(row, col + 1),
    )
    return starts, [order[start + j] for start in starts for j in range(ROWS)]


def find_slots(pattern, stored, wanted):
    slots = [jnp.int32(0)] * len(wanted)
    for k in range(SLOTS):
        label = pattern[k, stored]
        slots = [jnp.where(label == want, k, slot) for want, slot in zip(wanted, slots)]
    return slots


def fill_table(row_devices, col_devices, pattern, keep, order, table):
    starts, labels = neighbours(row_devices, col_devices, order)
    own_labels = labels[OWN * ROWS:(OWN + 1) * ROWS]

    def look_up(stored, wanted, slot_at, kept_at):
        for j, slot in enumerate(find_slots(pattern, stored, wanted)):
            if slot_at is not None:
                table[slot_at + j] = slot
            kept = (slot == 0) | (keep[slot, stored] == 1)
            table[kept_at + j] = kept.astype(jnp.int32)

    for i in range(ROWS):
        look_up(starts[OWN] + i, labels, SLOT_AT + i * SLOTS, KEPT_AT + i * SLOTS)
        look_up(starts[PEER] + i, own_labels, None, KEPT_PEER_AT + i * ROWS)
        look_up(starts[MATE] + i, own_labels, None, KEPT_MATE_AT + i * ROWS)


def gather(slot_of, source, places):
    size = source.shape[1]
    for i in range(ROWS):
        rows = slice(i * size, (i + 1) * size)
        for region, region_places in places.items():
            for j in range(ROWS):
                cols = slice(j * size, (j + 1) * size)
                start = pl.multiple_of(slot_of(i, region * ROWS + j) * size, size)
                block = source[i, :, pl.ds(start, size)]
                for place in region_places:
                    place[rows, cols] = block


def pack_first_kernel(
    row_devices, col_devices, pattern, order, sqrt_iterate,
    y_peer, pattern_here, order_here, sqrt_here, sems,
):
    copies = [
        pltpu.make_async_copy(source, here, sems.at[at])
        for at, (source, here) in enumerate(
            ((order, order_here), (pattern, pattern_here), (sqrt_iterate, sqrt_here))
        )
    ]
    for copy in copies:
        copy.start()
    copies[0].wait()
    copies[1].wait()
    starts, labels = neighbours(row_devices, col_devices, order_here)
    wanted = labels[PEER * ROWS:(OWN + 1) * ROWS]
    slots = [find_slots(pattern_here, starts[OWN] + i, wanted) for i in range(ROWS)]
    copies[2].wait()
    places = {PEER: (y_peer.at[0],), OWN: (y_peer.at[1],)}
    gather(lambda i, j: slots[i][j], sqrt_here, places)


def pack_rest_kernel(
    row_devices, col_devices, pattern, keep, order, sqrt_iterate, inverse_iterate, y_peer,
    table, z_peer, y_mate, z_mate, y_side, z_side, to_side,
    pattern_here, keep_here, order_here, sqrt_here, inverse_here, sems,
):
    copies = [
        pltpu.make_async_copy(source, here, sems.at[at])
        for at, (source, here) in enumerate((
            (order, order_here), (pattern, pattern_here), (keep, keep_here),
            (inverse_iterate, inverse_here), (sqrt_iterate, sqrt_here),
        ))
    ]
    for copy in copies:
        copy.start()
    y_mate[1] = y_peer[1]
    to_side[0] = y_peer[1]
    for copy in copies[:3]:
        copy.wait()
    fill_table(row_devices, col_devices, pattern_here, keep_here, order_here, table)

    def slot_of(i, j):
        return table[SLOT_AT + i * SLOTS + j]

    copies[3].wait()
    places = {
        PEER: (z_peer.at[0],), OWN: (z_peer.at[1], z_mate.at[1], to_side.at[1]),
        MATE: (z_mate.at[0],), SIDE: (z_side,),
    }
    gather(slot_of, inverse_here, places)
    copies[4].wait()
    gather(slot_of, sqrt_here, {MATE: (y_mate.at[0],), SIDE: (y_side,)})


def factor_part_kernel(y_peer, z_peer, peer_y, part):
    part[...] = products(
        (split(z_peer[0]), split(peer_y[0])), (split(z_peer[1]), split(y_peer[1]))
    )


def factor_own_kernel(table, part, z_mate, mate_y, factor_own):
    total = part[...] + products((split(z_mate[0]), split(mate_y[0])))
    rows = lax.broadcasted_iota(jnp.int32, total.shape, 0)
    cols = lax.broadcasted_iota(jnp.int32, total.shape, 1)
    factor_own[...] = jnp.where(rows == cols, 1.5, 0.0) + filtered(table, total, OWN, -0.5)


Y_MATE, Z_MATE, Z_SIDE = range(3)
Y_OWN_PART, Y_PEER_PART, Y_SIDE_PART, Z_OWN_PART, Z_PEER_PART = range(5)
Y_PEER, Y_OWN, Y_SIDE, F_PEER, PEER_Y = range(5)


def middle_kernel(
    table, y_peer, z_peer, y_mate, z_mate, y_side, z_side, mate_y, mate_z, peer_y, from_side,
    factor_own, mate_factor,
    finished, partial, ready,
):
    def keep(at, parts):
        ready[at, 0], ready[at, 1] = parts

    y_own, z_own = split(y_peer[1]), split(z_peer[1])
    y_to_peer, z_to_peer = split(y_peer[0]), split(z_peer[0])
    y_to_mate, z_to_mate = split(y_mate[0]), split(z_mate[0])
    y_to_side, z_to_side = split(y_side[...]), split(z_side[...])
    mate_y_mate, mate_y_own = split(mate_y[0]), split(mate_y[1])
    mate_z_mate, mate_z_own = split(mate_z[0]), split(mate_z[1])
    f_own = split(factor_own[...])
    keep(Y_OWN, y_own)
    keep(Y_SIDE, y_to_side)
    keep(Y_PEER, y_to_peer)
    keep(PEER_Y, split(peer_y[0]))

    total = products((z_own, y_to_mate), (z_to_mate, mate_y_own))
    f_mate = split(filtered(table, total, MATE, -0.5))
    total = products((z_own, y_to_peer), (z_to_peer, split(peer_y[1])))
    f_peer = split(filtered(table, total, PEER, -0.5))
    keep(F_PEER, f_peer)
    total = products((z_own, y_to_side), (z_to_side, split(from_side[0])))
    f_side = split(filtered(table, total, SIDE, -0.5))
    total = products((mate_z_own, mate_y_mate), (mate_z_mate, y_own))
    mate_f_mate = split(filtered(table, total, 0, -0.5, KEPT_MATE_AT, ROWS))

    partial[Y_PEER_PART] = products((y_own, f_peer))
    partial[Y_SIDE_PART] = products((y_own, f_side))
    partial[Y_OWN_PART] = products((y_to_mate, mate_f_mate), (y_own, f_own))
    partial[Z_PEER_PART] = products((f_own, z_to_peer))
    partial[Z_OWN_PART] = products((f_mate, mate_z_mate), (f_own, z_own))
    value = products((y_own, f_mate), (y_to_mate, split(mate_factor[...])))
    finished[Y_MATE] = filtered(table, value, MATE)
    value = products((f_mate, mate_z_own), (f_own, z_to_mate))
    finished[Z_MATE] = filtered(table, value, MATE)
    value = products((f_own, z_to_side), (f_side, split(from_side[1])))
    finished[Z_SIDE] = filtered(table, value, SIDE)


class Writer:
    def __init__(self, table, result, sems):
        self.table, self.result, self.sems = table, result, sems
        self.started = []
        self.held = 0

    def write(self, source, out, region):
        size = out.shape[1]
        for i in range(ROWS):
            for j in range(ROWS):
                slot = self.table[SLOT_AT + i * SLOTS + region * ROWS + j]
                copy = pltpu.make_async_copy(
                    source.at[pl.ds(i * size, size), pl.ds(j * size, size)],
                    out.at[i, :, pl.ds(pl.multiple_of(slot * size, size), size)],
                    self.sems.at[len(self.started)],
                )
                copy.start()
                self.started.append(copy)

    def finish(self, value, out, region):
        place = self.result.at[self.held]
        self.held += 1
        place[...] = filtered(self.table, value, region)
        self.write(place, out, region)

    def wait(self):
        for copy in self.started:
            copy.wait()


def peer_kernel(
    table, finished, partial, ready, peer_z, sqrt_next, inverse_next, result, sems
):
    def held(at):
        return ready[at, 0], ready[at, 1]

    writer = Writer(table, result, sems)
    writer.write(finished.at[Y_MATE], sqrt_next, MATE)
    writer.write(finished.at[Z_MATE], inverse_next, MATE)
    writer.write(finished.at[Z_SIDE], inverse_next, SIDE)
    peer_z_peer, peer_z_own = split(peer_z[0]), split(peer_z[1])
    f_peer = held(F_PEER)
    value = partial[Z_PEER_PART] + products((f_peer, peer_z_own))
    writer.finish(value, inverse_next, PEER)
    value = partial[Z_OWN_PART] + products((f_peer, peer_z_peer))
    writer.finish(value, inverse_next, OWN)
    total = products((peer_z_own, held(PEER_Y)), (peer_z_peer, held(Y_OWN)))
    peer_f_peer = split(filtered(table, total, 0, -0.5, KEPT_PEER_AT, ROWS))
    value = partial[Y_OWN_PART] + products((held(Y_PEER), peer_f_peer))
    writer.finish(value, sqrt_next, OWN)
    writer.wait()


def last_kernel(
    region, part, here, table, partial, ready, factor, unfinished,
    sqrt_next, table_here, result, sems,
):
    fetch = pltpu.make_async_copy(table, table_here, sems.at[4])
    fetch.start()
    value = partial[part] + products(((ready[here, 0], ready[here, 1]), split(factor[...])))
    fetch.wait()
    writer = Writer(table_here, result, sems)
    writer.finish(value, sqrt_next, region)
    writer.wait()


def call(
    kernel, outs, operands, terms, scratch=(), hbm_in=(), any_in=(), hbm_out=False, in_place=None
):
    def spec(array, outside=False, anywhere=False):
        if outside or anywhere:
            return pl.BlockSpec(memory_space=pltpu.HBM if outside else pl.ANY)
        small = array.dtype == jnp.int32
        return pl.BlockSpec(memory_space=pltpu.SMEM if small else pltpu.VMEM)

    moved = sum(array.size * array.dtype.itemsize for array in (*outs, *operands))
    operands = [
        pltpu.with_memory_space_constraint(array, pltpu.HBM) if at in hbm_in else array
        for at, array in enumerate(operands)
    ]
    return pl.pallas_call(
        kernel,
        out_shape=outs,
        in_specs=[spec(array, at in hbm_in, at in any_in) for at, array in enumerate(operands)],
        out_specs=tuple(spec(array, hbm_out) for array in outs),
        scratch_shapes=scratch,
        input_output_aliases={} if in_place is None else {in_place: 0},
        compiler_params=pltpu.CompilerParams(vmem_limit_bytes=VMEM_LIMIT),
        cost_estimate=pl.CostEstimate(
            flops=terms * 6 * 256**3, bytes_accessed=moved, transcendentals=0
        ),
    )(*operands)


def local(sqrt_iterate, inverse_iterate, pattern, keep_mask, row_order):
    rows_dev, block, width = sqrt_iterate.shape
    row_devices, col_devices = lax.axis_size("row"), lax.axis_size("col")
    assert rows_dev == ROWS and width == SLOTS * block and pattern.shape[1] == SLOTS
    assert row_devices > 3 and row_devices % 2 == 0 and col_devices > 2
    size = ROWS * block

    def to_mate(value):
        return lax.ppermute(value, "row", [(i, i ^ 1) for i in range(row_devices)])

    def to_peer(value):
        route = [(i, (i + (1 if i % 2 else -1)) % row_devices) for i in range(row_devices)]
        return lax.ppermute(value, "row", route)

    def to_side(value):
        route = [((i + 1) % col_devices, i) for i in range(col_devices)]
        return lax.ppermute(value, "col", route)

    def shape(*dims, dtype=jnp.float32):
        return jax.ShapeDtypeStruct(dims, dtype)

    one, pair = shape(size, size), shape(2, size, size)
    labels = [
        pltpu.SMEM(pattern.T.shape, jnp.int32),
        pltpu.SMEM(keep_mask.T.shape, jnp.int32),
        pltpu.SMEM(row_order.shape, jnp.int32),
    ]
    (y_peer,) = call(
        functools.partial(pack_first_kernel, row_devices, col_devices),
        (pair,),
        (pattern.T, row_order, sqrt_iterate),
        0,
        scratch=[
            labels[0],
            labels[2],
            pltpu.VMEM(sqrt_iterate.shape, jnp.float32),
            pltpu.SemaphoreType.DMA((3,)),
        ],
        hbm_in=range(3),
    )
    peer_y = to_peer(y_peer)
    table, z_peer, y_mate, z_mate, y_side, z_side, own_pair = call(
        functools.partial(pack_rest_kernel, row_devices, col_devices),
        (shape(TABLE, dtype=jnp.int32), pair, pair, pair, one, one, pair),
        (pattern.T, keep_mask.T, row_order, sqrt_iterate, inverse_iterate, y_peer),
        0,
        scratch=[
            *labels,
            pltpu.VMEM(sqrt_iterate.shape, jnp.float32),
            pltpu.VMEM(inverse_iterate.shape, jnp.float32),
            pltpu.SemaphoreType.DMA((5,)),
        ],
        hbm_in=range(5),
    )
    peer_z = to_peer(z_peer)
    mate_y = to_mate(y_mate)
    mate_z = to_mate(z_mate)
    from_side = to_side(own_pair)
    (part,) = call(factor_part_kernel, (one,), (y_peer, z_peer, peer_y), 2)
    (factor_own,) = call(factor_own_kernel, (one,), (table, part, z_mate, mate_y), 1)
    mate_factor = to_mate(factor_own)
    peer_factor = to_peer(factor_own)
    side_factor = to_side(factor_own)
    finished, partial, ready = call(
        middle_kernel,
        (
            shape(3, size, size), shape(5, size, size),
            shape(5, 2, size, size, dtype=jnp.bfloat16),
        ),
        (
            table, y_peer, z_peer, y_mate, z_mate, y_side, z_side, mate_y, mate_z, peer_y, from_side,
            factor_own, mate_factor,
        ),
        22,
    )
    sqrt_next, inverse_next = call(
        peer_kernel,
        (shape(rows_dev, block, width), shape(rows_dev, block, width)),
        (table, finished, partial, ready, peer_z),
        5,
        scratch=[pltpu.VMEM((3, size, size), jnp.float32), pltpu.SemaphoreType.DMA((24,))],
        hbm_out=True,
    )
    for region, part, here, factor in (
        (SIDE, Y_SIDE_PART, Y_SIDE, side_factor), (PEER, Y_PEER_PART, Y_PEER, peer_factor)
    ):
        (sqrt_next,) = call(
            functools.partial(last_kernel, region, part, here),
            (shape(rows_dev, block, width),),
            (table, partial, ready, factor, sqrt_next),
            1,
            scratch=[
                pltpu.SMEM((TABLE,), jnp.int32),
                pltpu.VMEM((1, size, size), jnp.float32),
                pltpu.SemaphoreType.DMA((5,)),
            ],
            hbm_in=(4,),
            any_in=(0,),
            hbm_out=True,
            in_place=4,
        )
    return sqrt_next, inverse_next


def solution(mesh):
    rows = P(("row", "col"), None, None)
    return jax.shard_map(
        local,
        mesh=mesh,
        in_specs=(rows, rows, P(), P(), P()),
        out_specs=(rows, rows),
        check_vma=False,
    )
```

```python
import functools

import jax
import jax.numpy as jnp
from jax import lax
from jax.experimental import pallas as pl
from jax.experimental.pallas import tpu as pltpu
from jax.sharding import PartitionSpec as P

PEER, OWN, MATE, SIDE = range(4)
ROWS = 2
SLOTS = 8
PIECES = 4
SLOT_AT, KEPT_AT, KEPT_PEER_AT, KEPT_MATE_AT, TABLE = 0, 16, 32, 36, 40
LARGEST = float(jnp.finfo(jnp.bfloat16).max)
VMEM_LIMIT = 24 * 2**20


def split(value):
    clipped = jnp.clip(value, -LARGEST, LARGEST)
    high = clipped.astype(jnp.bfloat16)
    low = (value - high.astype(jnp.float32)).astype(jnp.bfloat16)
    return high, low


def products(*pairs):
    left = [part for (high, low), _ in pairs for part in (high, low, high)]
    right = [part for _, (high, low) in pairs for part in (high, high, low)]
    return jnp.dot(
        jnp.concatenate(left, axis=1),
        jnp.concatenate(right, axis=0),
        preferred_element_type=jnp.float32,
    )


def filtered(table, value, region, scale=None, base=KEPT_AT, width=SLOTS):
    size = value.shape[0] // ROWS
    rows = []
    for i in range(ROWS):
        row = []
        for j in range(ROWS):
            kept = table[base + i * width + region * ROWS + j].astype(jnp.float32)
            if scale is not None:
                kept = kept * scale
            row.append(value[i * size:(i + 1) * size, j * size:(j + 1) * size] * kept)
        rows.append(jnp.concatenate(row, axis=1))
    return jnp.concatenate(rows, axis=0)


def neighbours(row_devices, col_devices, order):
    row = lax.axis_index("row")
    col = lax.axis_index("col")
    odd = lax.rem(row, 2)

    def first(row_of, col_of):
        return (lax.rem(row_of, row_devices) * col_devices + lax.rem(col_of, col_devices)) * ROWS

    starts = (
        first(row + row_devices - 1 + 2 * odd, col),
        first(row, col),
        first(row + 1 - 2 * odd, col),
        first(row, col + 1),
    )
    return starts, [order[start + j] for start in starts for j in range(ROWS)]


def find_slots(pattern, stored, wanted):
    slots = [jnp.int32(0)] * len(wanted)
    for k in range(SLOTS):
        label = pattern[k, stored]
        slots = [jnp.where(label == want, k, slot) for want, slot in zip(wanted, slots)]
    return slots


def fill_table(row_devices, col_devices, pattern, keep, order, table):
    starts, labels = neighbours(row_devices, col_devices, order)
    own_labels = labels[OWN * ROWS:(OWN + 1) * ROWS]

    def look_up(stored, wanted, slot_at, kept_at):
        for j, slot in enumerate(find_slots(pattern, stored, wanted)):
            if slot_at is not None:
                table[slot_at + j] = slot
            kept = (slot == 0) | (keep[slot, stored] == 1)
            table[kept_at + j] = kept.astype(jnp.int32)

    for i in range(ROWS):
        look_up(starts[OWN] + i, labels, SLOT_AT + i * SLOTS, KEPT_AT + i * SLOTS)
        look_up(starts[PEER] + i, own_labels, None, KEPT_PEER_AT + i * ROWS)
        look_up(starts[MATE] + i, own_labels, None, KEPT_MATE_AT + i * ROWS)


def gather(slot_of, source, places):
    size = source.shape[1]
    for i in range(ROWS):
        rows = slice(i * size, (i + 1) * size)
        for region, region_places in places.items():
            for j in range(ROWS):
                cols = slice(j * size, (j + 1) * size)
                start = pl.multiple_of(slot_of(i, region * ROWS + j) * size, size)
                block = source[i, :, pl.ds(start, size)]
                for place in region_places:
                    place[rows, cols] = block


def pack_first_kernel(
    row_devices, col_devices, pattern, order, sqrt_iterate,
    y_peer, pattern_here, order_here, sqrt_here, sems,
):
    pieces = [(order, order_here), (pattern, pattern_here)]
    height = sqrt_iterate.shape[1] // PIECES
    for i in range(ROWS):
        for piece in range(PIECES):
            rows = pl.ds(piece * height, height)
            pieces.append((sqrt_iterate.at[i, rows], sqrt_here.at[i, rows]))
    copies = [
        pltpu.make_async_copy(source, here, sems.at[at])
        for at, (source, here) in enumerate(pieces)
    ]
    for copy in copies:
        copy.start()
    copies[0].wait()
    copies[1].wait()
    starts, labels = neighbours(row_devices, col_devices, order_here)
    wanted = labels[PEER * ROWS:(OWN + 1) * ROWS]
    slots = [find_slots(pattern_here, starts[OWN] + i, wanted) for i in range(ROWS)]
    for copy in copies[2:]:
        copy.wait()
    places = {PEER: (y_peer.at[0],), OWN: (y_peer.at[1],)}
    gather(lambda i, j: slots[i][j], sqrt_here, places)


def pack_rest_kernel(
    row_devices, col_devices, pattern, keep, order, sqrt_iterate, inverse_iterate, y_peer,
    table, z_peer, y_mate, z_mate, y_side, z_side, to_side,
    pattern_here, keep_here, order_here, sqrt_here, inverse_here, sems,
):
    copies = [
        pltpu.make_async_copy(source, here, sems.at[at])
        for at, (source, here) in enumerate((
            (order, order_here), (pattern, pattern_here), (keep, keep_here),
            (inverse_iterate, inverse_here), (sqrt_iterate, sqrt_here),
        ))
    ]
    for copy in copies:
        copy.start()
    y_mate[1] = y_peer[1]
    to_side[0] = y_peer[1]
    for copy in copies[:3]:
        copy.wait()
    fill_table(row_devices, col_devices, pattern_here, keep_here, order_here, table)

    def slot_of(i, j):
        return table[SLOT_AT + i * SLOTS + j]

    copies[3].wait()
    places = {
        PEER: (z_peer.at[0],), OWN: (z_peer.at[1], z_mate.at[1], to_side.at[1]),
        MATE: (z_mate.at[0],), SIDE: (z_side,),
    }
    gather(slot_of, inverse_here, places)
    copies[4].wait()
    gather(slot_of, sqrt_here, {MATE: (y_mate.at[0],), SIDE: (y_side,)})


def factor_part_kernel(y_peer, z_peer, peer_y, part):
    part[...] = products(
        (split(z_peer[0]), split(peer_y[0])), (split(z_peer[1]), split(y_peer[1]))
    )


def factor_own_kernel(table, part, z_mate, mate_y, peer_y, factor_own, peer_term):
    total = part[...] + products((split(z_mate[0]), split(mate_y[0])))
    rows = lax.broadcasted_iota(jnp.int32, total.shape, 0)
    cols = lax.broadcasted_iota(jnp.int32, total.shape, 1)
    factor = jnp.where(rows == cols, 1.5, 0.0) + filtered(table, total, OWN, -0.5)
    factor_own[...] = factor
    term = products((split(peer_y[0]), split(factor)))
    peer_term[...] = filtered(table, term, 0, None, KEPT_PEER_AT, ROWS)


Y_MATE, Z_MATE, Z_SIDE = range(3)
Y_OWN_PART, Y_PEER_PART, Y_SIDE_PART, Z_OWN_PART, Z_PEER_PART = range(5)
Y_PEER, Y_OWN, Y_SIDE, F_PEER, PEER_Y = range(5)


def middle_kernel(
    table, y_peer, z_peer, y_mate, z_mate, y_side, z_side, mate_y, mate_z, peer_y, from_side,
    factor_own, mate_factor,
    finished, partial, ready,
):
    def keep(at, parts):
        ready[at, 0], ready[at, 1] = parts

    y_own, z_own = split(y_peer[1]), split(z_peer[1])
    y_to_peer, z_to_peer = split(y_peer[0]), split(z_peer[0])
    y_to_mate, z_to_mate = split(y_mate[0]), split(z_mate[0])
    y_to_side, z_to_side = split(y_side[...]), split(z_side[...])
    mate_y_mate, mate_y_own = split(mate_y[0]), split(mate_y[1])
    mate_z_mate, mate_z_own = split(mate_z[0]), split(mate_z[1])
    f_own = split(factor_own[...])
    keep(Y_OWN, y_own)
    keep(Y_SIDE, y_to_side)
    keep(Y_PEER, y_to_peer)
    keep(PEER_Y, split(peer_y[0]))

    total = products((z_own, y_to_mate), (z_to_mate, mate_y_own))
    f_mate = split(filtered(table, total, MATE, -0.5))
    total = products((z_own, y_to_peer), (z_to_peer, split(peer_y[1])))
    f_peer = split(filtered(table, total, PEER, -0.5))
    keep(F_PEER, f_peer)
    total = products((z_own, y_to_side), (z_to_side, split(from_side[0])))
    f_side = split(filtered(table, total, SIDE, -0.5))
    total = products((mate_z_own, mate_y_mate), (mate_z_mate, y_own))
    mate_f_mate = split(filtered(table, total, 0, -0.5, KEPT_MATE_AT, ROWS))

    partial[Y_PEER_PART] = filtered(table, products((y_own, f_peer)), PEER)
    partial[Y_SIDE_PART] = products((y_own, f_side))
    partial[Y_OWN_PART] = products((y_to_mate, mate_f_mate), (y_own, f_own))
    partial[Z_PEER_PART] = products((f_own, z_to_peer))
    partial[Z_OWN_PART] = products((f_mate, mate_z_mate), (f_own, z_own))
    value = products((y_own, f_mate), (y_to_mate, split(mate_factor[...])))
    finished[Y_MATE] = filtered(table, value, MATE)
    value = products((f_mate, mate_z_own), (f_own, z_to_mate))
    finished[Z_MATE] = filtered(table, value, MATE)
    value = products((f_own, z_to_side), (f_side, split(from_side[1])))
    finished[Z_SIDE] = filtered(table, value, SIDE)


class Writer:
    def __init__(self, table, result, sems):
        self.table, self.result, self.sems = table, result, sems
        self.started = []
        self.held = 0

    def write(self, source, out, region):
        size = out.shape[1]
        for i in range(ROWS):
            for j in range(ROWS):
                slot = self.table[SLOT_AT + i * SLOTS + region * ROWS + j]
                copy = pltpu.make_async_copy(
                    source.at[pl.ds(i * size, size), pl.ds(j * size, size)],
                    out.at[i, :, pl.ds(pl.multiple_of(slot * size, size), size)],
                    self.sems.at[len(self.started)],
                )
                copy.start()
                self.started.append(copy)

    def finish(self, value, out, region):
        place = self.result.at[self.held]
        self.held += 1
        place[...] = filtered(self.table, value, region)
        self.write(place, out, region)

    def wait(self):
        for copy in self.started:
            copy.wait()


def peer_kernel(
    table, finished, partial, ready, peer_z, sqrt_next, inverse_next, result, sems
):
    def held(at):
        return ready[at, 0], ready[at, 1]

    writer = Writer(table, result, sems)
    writer.write(finished.at[Y_MATE], sqrt_next, MATE)
    writer.write(finished.at[Z_MATE], inverse_next, MATE)
    writer.write(finished.at[Z_SIDE], inverse_next, SIDE)
    peer_z_peer, peer_z_own = split(peer_z[0]), split(peer_z[1])
    f_peer = held(F_PEER)
    value = partial[Z_PEER_PART] + products((f_peer, peer_z_own))
    writer.finish(value, inverse_next, PEER)
    value = partial[Z_OWN_PART] + products((f_peer, peer_z_peer))
    writer.finish(value, inverse_next, OWN)
    total = products((peer_z_own, held(PEER_Y)), (peer_z_peer, held(Y_OWN)))
    peer_f_peer = split(filtered(table, total, 0, -0.5, KEPT_PEER_AT, ROWS))
    value = partial[Y_OWN_PART] + products((held(Y_PEER), peer_f_peer))
    writer.finish(value, sqrt_next, OWN)
    writer.wait()


def side_kernel(
    table, partial, ready, factor, unfinished, sqrt_next, table_here, result, sems
):
    fetch = pltpu.make_async_copy(table, table_here, sems.at[4])
    fetch.start()
    left = (ready[Y_SIDE, 0], ready[Y_SIDE, 1])
    value = partial[Y_SIDE_PART] + products((left, split(factor[...])))
    fetch.wait()
    writer = Writer(table_here, result, sems)
    writer.finish(value, sqrt_next, SIDE)
    writer.wait()


def last_kernel(table, partial, term, unfinished, sqrt_next, table_here, result, sems):
    fetch = pltpu.make_async_copy(table, table_here, sems.at[4])
    fetch.start()
    result[0] = partial[Y_PEER_PART] + term[...]
    fetch.wait()
    writer = Writer(table_here, result, sems)
    writer.write(result.at[0], sqrt_next, PEER)
    writer.wait()


def call(
    kernel, outs, operands, terms, scratch=(), hbm_in=(), any_in=(), hbm_out=False, in_place=None
):
    def spec(array, outside=False, anywhere=False):
        if outside or anywhere:
            return pl.BlockSpec(memory_space=pltpu.HBM if outside else pl.ANY)
        small = array.dtype == jnp.int32
        return pl.BlockSpec(memory_space=pltpu.SMEM if small else pltpu.VMEM)

    moved = sum(array.size * array.dtype.itemsize for array in (*outs, *operands))
    operands = [
        pltpu.with_memory_space_constraint(array, pltpu.HBM) if at in hbm_in else array
        for at, array in enumerate(operands)
    ]
    return pl.pallas_call(
        kernel,
        out_shape=outs,
        in_specs=[spec(array, at in hbm_in, at in any_in) for at, array in enumerate(operands)],
        out_specs=tuple(spec(array, hbm_out) for array in outs),
        scratch_shapes=scratch,
        input_output_aliases={} if in_place is None else {in_place: 0},
        compiler_params=pltpu.CompilerParams(vmem_limit_bytes=VMEM_LIMIT),
        cost_estimate=pl.CostEstimate(
            flops=terms * 6 * 256**3, bytes_accessed=moved, transcendentals=0
        ),
    )(*operands)


def local(sqrt_iterate, inverse_iterate, pattern, keep_mask, row_order):
    rows_dev, block, width = sqrt_iterate.shape
    row_devices, col_devices = lax.axis_size("row"), lax.axis_size("col")
    assert rows_dev == ROWS and width == SLOTS * block and pattern.shape[1] == SLOTS
    assert row_devices > 3 and row_devices % 2 == 0 and col_devices > 2
    size = ROWS * block

    def to_mate(value):
        return lax.ppermute(value, "row", [(i, i ^ 1) for i in range(row_devices)])

    def to_peer(value):
        route = [(i, (i + (1 if i % 2 else -1)) % row_devices) for i in range(row_devices)]
        return lax.ppermute(value, "row", route)

    def to_side(value):
        route = [((i + 1) % col_devices, i) for i in range(col_devices)]
        return lax.ppermute(value, "col", route)

    def shape(*dims, dtype=jnp.float32):
        return jax.ShapeDtypeStruct(dims, dtype)

    one, pair = shape(size, size), shape(2, size, size)
    labels = [
        pltpu.SMEM(pattern.T.shape, jnp.int32),
        pltpu.SMEM(keep_mask.T.shape, jnp.int32),
        pltpu.SMEM(row_order.shape, jnp.int32),
    ]
    (y_peer,) = call(
        functools.partial(pack_first_kernel, row_devices, col_devices),
        (pair,),
        (pattern.T, row_order, sqrt_iterate),
        0,
        scratch=[
            labels[0],
            labels[2],
            pltpu.VMEM(sqrt_iterate.shape, jnp.float32),
            pltpu.SemaphoreType.DMA((2 + ROWS * PIECES,)),
        ],
        hbm_in=range(3),
    )
    peer_y = to_peer(y_peer)
    table, z_peer, y_mate, z_mate, y_side, z_side, own_pair = call(
        functools.partial(pack_rest_kernel, row_devices, col_devices),
        (shape(TABLE, dtype=jnp.int32), pair, pair, pair, one, one, pair),
        (pattern.T, keep_mask.T, row_order, sqrt_iterate, inverse_iterate, y_peer),
        0,
        scratch=[
            *labels,
            pltpu.VMEM(sqrt_iterate.shape, jnp.float32),
            pltpu.VMEM(inverse_iterate.shape, jnp.float32),
            pltpu.SemaphoreType.DMA((5,)),
        ],
        hbm_in=range(5),
    )
    peer_z = to_peer(z_peer)
    mate_y = to_mate(y_mate)
    mate_z = to_mate(z_mate)
    from_side = to_side(own_pair)
    (part,) = call(factor_part_kernel, (one,), (y_peer, z_peer, peer_y), 2)
    factor_own, peer_term = call(
        factor_own_kernel, (one, one), (table, part, z_mate, mate_y, peer_y), 2
    )
    mate_factor = to_mate(factor_own)
    term = to_peer(peer_term)
    side_factor = to_side(factor_own)
    finished, partial, ready = call(
        middle_kernel,
        (
            shape(3, size, size), shape(5, size, size),
            shape(5, 2, size, size, dtype=jnp.bfloat16),
        ),
        (
            table, y_peer, z_peer, y_mate, z_mate, y_side, z_side, mate_y, mate_z, peer_y, from_side,
            factor_own, mate_factor,
        ),
        22,
    )
    sqrt_next, inverse_next = call(
        peer_kernel,
        (shape(rows_dev, block, width), shape(rows_dev, block, width)),
        (table, finished, partial, ready, peer_z),
        5,
        scratch=[pltpu.VMEM((3, size, size), jnp.float32), pltpu.SemaphoreType.DMA((24,))],
        hbm_out=True,
    )
    for kernel, operands in (
        (side_kernel, (table, partial, ready, side_factor)),
        (last_kernel, (table, partial, term)),
    ):
        (sqrt_next,) = call(
            kernel,
            (shape(rows_dev, block, width),),
            (*operands, sqrt_next),
            1,
            scratch=[
                pltpu.SMEM((TABLE,), jnp.int32),
                pltpu.VMEM((1, size, size), jnp.float32),
                pltpu.SemaphoreType.DMA((5,)),
            ],
            hbm_in=(len(operands),),
            any_in=(0,),
            hbm_out=True,
            in_place=len(operands),
        )
    return sqrt_next, inverse_next


def solution(mesh):
    rows = P(("row", "col"), None, None)
    return jax.shard_map(
        local,
        mesh=mesh,
        in_specs=(rows, rows, P(), P(), P()),
        out_specs=(rows, rows),
        check_vma=False,
    )
```

```python
import functools

import jax
import jax.numpy as jnp
from jax import lax
from jax.experimental import pallas as pl
from jax.experimental.pallas import tpu as pltpu
from jax.sharding import PartitionSpec as P

PEER, OWN, MATE, SIDE = range(4)
ROWS = 2
SLOTS = 8
SLOT_AT, KEPT_AT, KEPT_PEER_AT, KEPT_MATE_AT, TABLE = 0, 16, 32, 36, 40
LARGEST = float(jnp.finfo(jnp.bfloat16).max)
VMEM_LIMIT = 24 * 2**20
PEAK = 1.153e9


def split(value):
    clipped = jnp.clip(value, -LARGEST, LARGEST)
    high = clipped.astype(jnp.bfloat16)
    low = (value - high.astype(jnp.float32)).astype(jnp.bfloat16)
    return high, low


def products(*pairs):
    left = [part for (high, low), _ in pairs for part in (high, low, high)]
    right = [part for _, (high, low) in pairs for part in (high, high, low)]
    return jnp.dot(
        jnp.concatenate(left, axis=1),
        jnp.concatenate(right, axis=0),
        preferred_element_type=jnp.float32,
    )


def filtered(table, value, region, scale=None, base=KEPT_AT, width=SLOTS):
    size = value.shape[0] // ROWS
    rows = []
    for i in range(ROWS):
        row = []
        for j in range(ROWS):
            kept = table[base + i * width + region * ROWS + j].astype(jnp.float32)
            if scale is not None:
                kept = kept * scale
            row.append(value[i * size:(i + 1) * size, j * size:(j + 1) * size] * kept)
        rows.append(jnp.concatenate(row, axis=1))
    return jnp.concatenate(rows, axis=0)


def neighbours(row_devices, col_devices, order):
    row = lax.axis_index("row")
    col = lax.axis_index("col")
    odd = lax.rem(row, 2)

    def first(row_of, col_of):
        return (lax.rem(row_of, row_devices) * col_devices + lax.rem(col_of, col_devices)) * ROWS

    starts = (
        first(row + row_devices - 1 + 2 * odd, col),
        first(row, col),
        first(row + 1 - 2 * odd, col),
        first(row, col + 1),
    )
    return starts, [order[start + j] for start in starts for j in range(ROWS)]


def find_slots(pattern, stored, wanted):
    slots = [jnp.int32(0)] * len(wanted)
    for k in range(SLOTS):
        label = pattern[k, stored]
        slots = [jnp.where(label == want, k, slot) for want, slot in zip(wanted, slots)]
    return slots


def fill_table(row_devices, col_devices, pattern, keep, order, table):
    starts, labels = neighbours(row_devices, col_devices, order)
    own_labels = labels[OWN * ROWS:(OWN + 1) * ROWS]

    def look_up(stored, wanted, slot_at, kept_at):
        for j, slot in enumerate(find_slots(pattern, stored, wanted)):
            if slot_at is not None:
                table[slot_at + j] = slot
            kept = (slot == 0) | (keep[slot, stored] == 1)
            table[kept_at + j] = kept.astype(jnp.int32)

    for i in range(ROWS):
        look_up(starts[OWN] + i, labels, SLOT_AT + i * SLOTS, KEPT_AT + i * SLOTS)
        look_up(starts[PEER] + i, own_labels, None, KEPT_PEER_AT + i * ROWS)
        look_up(starts[MATE] + i, own_labels, None, KEPT_MATE_AT + i * ROWS)


def quarter(i, j, size):
    return slice(i * size, (i + 1) * size), slice(j * size, (j + 1) * size)


def gather(slot_of, source, places):
    size = source.shape[1]
    for region, region_places in places.items():
        for i in range(ROWS):
            for j in range(ROWS):
                start = pl.multiple_of(slot_of(i, region * ROWS + j) * size, size)
                block = source[i, :, pl.ds(start, size)]
                for place in region_places:
                    place(i, j, size, block)


def into(out):
    def place(i, j, size, block):
        rows, cols = quarter(i, j, size)
        out[rows, cols] = block

    return place


def strip_peer(out):
    def place(i, j, size, block):
        out[i, :, j * size:(j + 1) * size] = block

    return place


def strip_own(out):
    def place(i, j, size, block):
        if i != j:
            out[ROWS, :, i * size:(i + 1) * size] = block

    return place


def peer_part(strips):
    return jnp.concatenate([strips[i] for i in range(ROWS)], axis=0)


def own_part(strips, spread):
    size = strips.shape[1]
    beside = strips[ROWS]
    return jnp.concatenate(
        [
            jnp.concatenate([spread[:size, :size], beside[:, :size]], axis=1),
            jnp.concatenate([beside[:, size:], spread[size:, size:]], axis=1),
        ],
        axis=0,
    )


def diagonal_kernel(sqrt_iterate, inverse_iterate, diagonal, sems):
    size = sqrt_iterate.shape[1]
    copies = []
    for source in (sqrt_iterate, inverse_iterate):
        for i in range(ROWS):
            at = len(copies)
            copies.append(
                pltpu.make_async_copy(source.at[i, :, pl.ds(0, size)], diagonal.at[at], sems.at[at])
            )
            copies[at].start()
    for copy in copies:
        copy.wait()


def pack_kernel(
    row_devices, col_devices, pattern, keep, order, sqrt_iterate, inverse_iterate, after,
    table, y_strips, z_strips, y_mate, mate_rest, y_side, z_side, to_side, last_slots,
    pattern_here, keep_here, order_here, sqrt_here, inverse_here, sems,
):
    copies = [
        pltpu.make_async_copy(source, here, sems.at[at])
        for at, (source, here) in enumerate((
            (order, order_here), (pattern, pattern_here), (keep, keep_here),
            (sqrt_iterate, sqrt_here), (inverse_iterate, inverse_here),
        ))
    ]
    for copy in copies:
        copy.start()
    for copy in copies[:3]:
        copy.wait()
    fill_table(row_devices, col_devices, pattern_here, keep_here, order_here, table)

    def slot_of(i, j):
        return table[SLOT_AT + i * SLOTS + j]

    line = lax.broadcasted_iota(jnp.int32, last_slots.shape, 0)
    tile = jnp.zeros(last_slots.shape, jnp.int32)
    for at, region in enumerate((PEER, SIDE)):
        for i in range(ROWS):
            for j in range(ROWS):
                here = line == (at * ROWS + i) * ROWS + j
                tile = jnp.where(here, slot_of(i, region * ROWS + j), tile)
    last_slots[...] = tile
    copies[3].wait()
    places = {
        PEER: (strip_peer(y_strips),),
        OWN: (strip_own(y_strips), into(mate_rest.at[0]), into(to_side.at[0])),
        MATE: (into(y_mate),),
        SIDE: (into(y_side),),
    }
    gather(slot_of, sqrt_here, places)
    copies[4].wait()
    places = {
        PEER: (strip_peer(z_strips),),
        OWN: (strip_own(z_strips), into(mate_rest.at[2]), into(to_side.at[1])),
        MATE: (into(mate_rest.at[1]),),
        SIDE: (into(z_side),),
    }
    gather(slot_of, inverse_here, places)


def spread_kernel(diagonal, spread):
    size = diagonal.shape[1]
    for at in range(2):
        for i in range(ROWS):
            for j in range(ROWS):
                rows, cols = quarter(i, j, size)
                block = diagonal[at * ROWS + i]
                spread[at, rows, cols] = block if i == j else jnp.zeros_like(block)


def factor_part_kernel(
    y_strips, mate_rest, z_strips, peer_y, peer_spread, own_total, peer_total
):
    z_own, z_to_peer = split(mate_rest[2]), split(peer_part(z_strips))
    own_total[...] = products(
        (z_to_peer, split(peer_part(peer_y))), (z_own, split(mate_rest[0]))
    )
    peer_total[...] = products(
        (z_own, split(peer_part(y_strips))), (z_to_peer, split(own_part(peer_y, peer_spread[0])))
    )


def factor_own_kernel(table, part, mate_rest, mate_y, peer_y, factor_own, peer_term):
    total = part[...] + products((split(mate_rest[1]), split(mate_y[...])))
    rows = lax.broadcasted_iota(jnp.int32, total.shape, 0)
    cols = lax.broadcasted_iota(jnp.int32, total.shape, 1)
    factor = jnp.where(rows == cols, 1.5, 0.0) + filtered(table, total, OWN, -0.5)
    factor_own[...] = factor
    term = products((split(peer_part(peer_y)), split(factor)))
    peer_term[...] = filtered(table, term, 0, None, KEPT_PEER_AT, ROWS)


Y_MATE, Z_MATE, Z_SIDE = range(3)
Y_OWN_PART, Y_PEER_PART, Y_SIDE_PART, Z_OWN_PART, Z_PEER_PART = range(5)
Y_PEER, Y_OWN, Y_SIDE, F_PEER, PEER_Y = range(5)


def middle_kernel(
    table, y_strips, z_strips, y_mate, mate_rest, y_side, z_side, mate_y, from_mate,
    peer_y, peer_total, from_side, factor_own, mate_factor,
    finished, partial, ready,
):
    def keep(at, parts):
        ready[at, 0], ready[at, 1] = parts

    y_own, z_own = split(mate_rest[0]), split(mate_rest[2])
    y_to_peer, z_to_peer = split(peer_part(y_strips)), split(peer_part(z_strips))
    y_to_mate, z_to_mate = split(y_mate[...]), split(mate_rest[1])
    y_to_side, z_to_side = split(y_side[...]), split(z_side[...])
    mate_y_mate, mate_y_own = split(mate_y[...]), split(from_mate[0])
    mate_z_mate, mate_z_own = split(from_mate[1]), split(from_mate[2])
    f_own = split(factor_own[...])
    keep(Y_OWN, y_own)
    keep(Y_SIDE, y_to_side)
    keep(Y_PEER, y_to_peer)
    keep(PEER_Y, split(peer_part(peer_y)))

    total = products((z_own, y_to_mate), (z_to_mate, mate_y_own))
    f_mate = split(filtered(table, total, MATE, -0.5))
    f_peer = split(filtered(table, peer_total[...], PEER, -0.5))
    keep(F_PEER, f_peer)
    total = products((z_own, y_to_side), (z_to_side, split(from_side[0])))
    f_side = split(filtered(table, total, SIDE, -0.5))
    total = products((mate_z_own, mate_y_mate), (mate_z_mate, y_own))
    mate_f_mate = split(filtered(table, total, 0, -0.5, KEPT_MATE_AT, ROWS))

    partial[Y_PEER_PART] = filtered(table, products((y_own, f_peer)), PEER)
    partial[Y_SIDE_PART] = products((y_own, f_side))
    partial[Y_OWN_PART] = products((y_to_mate, mate_f_mate), (y_own, f_own))
    partial[Z_PEER_PART] = products((f_own, z_to_peer))
    partial[Z_OWN_PART] = products((f_mate, mate_z_mate), (f_own, z_own))
    value = products((y_own, f_mate), (y_to_mate, split(mate_factor[...])))
    finished[Y_MATE] = filtered(table, value, MATE)
    value = products((f_mate, mate_z_own), (f_own, z_to_mate))
    finished[Z_MATE] = filtered(table, value, MATE)
    value = products((f_own, z_to_side), (f_side, split(from_side[1])))
    finished[Z_SIDE] = filtered(table, value, SIDE)


class Writer:
    def __init__(self, table, result, sems):
        self.table, self.result, self.sems = table, result, sems
        self.started = []
        self.held = 0

    def write(self, source, out, region):
        size = out.shape[1]
        for i in range(ROWS):
            for j in range(ROWS):
                slot = self.table[SLOT_AT + i * SLOTS + region * ROWS + j]
                copy = pltpu.make_async_copy(
                    source.at[pl.ds(i * size, size), pl.ds(j * size, size)],
                    out.at[i, :, pl.ds(pl.multiple_of(slot * size, size), size)],
                    self.sems.at[len(self.started)],
                )
                copy.start()
                self.started.append(copy)

    def finish(self, value, out, region):
        place = self.result.at[self.held]
        self.held += 1
        place[...] = filtered(self.table, value, region)
        self.write(place, out, region)

    def wait(self):
        for copy in self.started:
            copy.wait()


def peer_kernel(
    table, finished, partial, ready, peer_z, peer_spread,
    sqrt_next, inverse_next, result, sems,
):
    def held(at):
        return ready[at, 0], ready[at, 1]

    writer = Writer(table, result, sems)
    writer.write(finished.at[Y_MATE], sqrt_next, MATE)
    writer.write(finished.at[Z_MATE], inverse_next, MATE)
    writer.write(finished.at[Z_SIDE], inverse_next, SIDE)
    peer_z_peer = split(peer_part(peer_z))
    peer_z_own = split(own_part(peer_z, peer_spread[1]))
    f_peer = held(F_PEER)
    value = partial[Z_PEER_PART] + products((f_peer, peer_z_own))
    writer.finish(value, inverse_next, PEER)
    value = partial[Z_OWN_PART] + products((f_peer, peer_z_peer))
    writer.finish(value, inverse_next, OWN)
    total = products((peer_z_own, held(PEER_Y)), (peer_z_peer, held(Y_OWN)))
    peer_f_peer = split(filtered(table, total, 0, -0.5, KEPT_PEER_AT, ROWS))
    value = partial[Y_OWN_PART] + products((held(Y_PEER), peer_f_peer))
    writer.finish(value, sqrt_next, OWN)
    writer.wait()


def side_kernel(
    table, partial, ready, factor, unfinished, sqrt_next, table_here, result, sems
):
    fetch = pltpu.make_async_copy(table, table_here, sems.at[4])
    fetch.start()
    left = (ready[Y_SIDE, 0], ready[Y_SIDE, 1])
    value = partial[Y_SIDE_PART] + products((left, split(factor[...])))
    fetch.wait()
    writer = Writer(table_here, result, sems)
    writer.finish(value, sqrt_next, SIDE)
    writer.wait()


def last_kernel(slots, partial, term, unfinished, sqrt_next, result, sems):
    size = sqrt_next.shape[1]
    copies = []
    for i in range(ROWS):
        for j in range(ROWS):
            at = len(copies)
            rows, cols = quarter(i, j, size)
            result[at] = partial[Y_PEER_PART, rows, cols] + term[rows, cols]
            start = pl.multiple_of(slots[at, 0] * size, size)
            out = sqrt_next.at[i, :, pl.ds(start, size)]
            copies.append(pltpu.make_async_copy(result.at[at], out, sems.at[at]))
            copies[at].start()
    for copy in copies:
        copy.wait()


def call(
    kernel, outs, operands, micros=0, scratch=(), hbm_in=(), any_in=(), hbm_out=False, in_place=None
):
    def spec(array, outside=False, anywhere=False):
        if outside or anywhere:
            return pl.BlockSpec(memory_space=pltpu.HBM if outside else pl.ANY)
        small = array.dtype == jnp.int32 and array.ndim == 1
        return pl.BlockSpec(memory_space=pltpu.SMEM if small else pltpu.VMEM)

    operands = [
        pltpu.with_memory_space_constraint(array, pltpu.HBM) if at in hbm_in else array
        for at, array in enumerate(operands)
    ]
    return pl.pallas_call(
        kernel,
        out_shape=outs,
        in_specs=[spec(array, at in hbm_in, at in any_in) for at, array in enumerate(operands)],
        out_specs=tuple(spec(array, hbm_out) for array in outs),
        scratch_shapes=scratch,
        input_output_aliases={} if in_place is None else {in_place: 0},
        compiler_params=pltpu.CompilerParams(vmem_limit_bytes=VMEM_LIMIT),
        cost_estimate=pl.CostEstimate(
            flops=int(micros * PEAK), bytes_accessed=0, transcendentals=0
        ),
    )(*operands)


def local(sqrt_iterate, inverse_iterate, pattern, keep_mask, row_order):
    rows_dev, block, width = sqrt_iterate.shape
    row_devices, col_devices = lax.axis_size("row"), lax.axis_size("col")
    assert rows_dev == ROWS and width == SLOTS * block and pattern.shape[1] == SLOTS
    assert row_devices > 3 and row_devices % 2 == 0 and col_devices > 2
    size = ROWS * block

    def to_mate(value):
        return lax.ppermute(value, "row", [(i, i ^ 1) for i in range(row_devices)])

    def to_peer(value):
        route = [(i, (i + (1 if i % 2 else -1)) % row_devices) for i in range(row_devices)]
        return lax.ppermute(value, "row", route)

    def to_side(value):
        route = [((i + 1) % col_devices, i) for i in range(col_devices)]
        return lax.ppermute(value, "col", route)

    def shape(*dims, dtype=jnp.float32):
        return jax.ShapeDtypeStruct(dims, dtype)

    one, pair = shape(size, size), shape(2, size, size)
    (diagonal,) = call(
        diagonal_kernel,
        (shape(2 * ROWS, block, block),),
        (sqrt_iterate, inverse_iterate),
        scratch=[pltpu.SemaphoreType.DMA((2 * ROWS,))],
        hbm_in=range(2),
    )
    peer_diagonal = to_peer(diagonal)
    strips = shape(ROWS + 1, block, size)
    (
        table, y_strips, z_strips, y_mate, mate_rest, y_side, z_side, own_pair, last_slots
    ) = call(
        functools.partial(pack_kernel, row_devices, col_devices),
        (
            shape(TABLE, dtype=jnp.int32), strips, strips, one, shape(3, size, size), one, one,
            pair, shape(8, 128, dtype=jnp.int32),
        ),
        (pattern.T, keep_mask.T, row_order, sqrt_iterate, inverse_iterate, diagonal),
        scratch=[
            pltpu.SMEM(pattern.T.shape, jnp.int32),
            pltpu.SMEM(keep_mask.T.shape, jnp.int32),
            pltpu.SMEM(row_order.shape, jnp.int32),
            pltpu.VMEM(sqrt_iterate.shape, jnp.float32),
            pltpu.VMEM(inverse_iterate.shape, jnp.float32),
            pltpu.SemaphoreType.DMA((5,)),
        ],
        hbm_in=range(5),
        any_in=(5,),
    )
    peer_y = to_peer(y_strips)
    peer_z = to_peer(z_strips)
    mate_y = to_mate(y_mate)
    from_mate = to_mate(mate_rest)
    from_side = to_side(own_pair)
    (peer_spread,) = call(spread_kernel, (pair,), (peer_diagonal,), micros=3)
    part, peer_total = call(
        factor_part_kernel,
        (one, one),
        (y_strips, mate_rest, z_strips, peer_y, peer_spread),
    )
    factor_own, peer_term = call(
        factor_own_kernel, (one, one), (table, part, mate_rest, mate_y, peer_y), micros=5
    )
    mate_factor = to_mate(factor_own)
    term = to_peer(peer_term)
    side_factor = to_side(factor_own)
    finished, partial, ready = call(
        middle_kernel,
        (
            shape(3, size, size), shape(5, size, size),
            shape(5, 2, size, size, dtype=jnp.bfloat16),
        ),
        (
            table, y_strips, z_strips, y_mate, mate_rest, y_side, z_side, mate_y, from_mate,
            peer_y, peer_total, from_side, factor_own, mate_factor,
        ),
    )
    output = shape(rows_dev, block, width)
    sqrt_next, inverse_next = call(
        peer_kernel,
        (output, output),
        (table, finished, partial, ready, peer_z, peer_spread),
        scratch=[pltpu.VMEM((3, size, size), jnp.float32), pltpu.SemaphoreType.DMA((24,))],
        hbm_out=True,
    )
    (sqrt_next,) = call(
        side_kernel,
        (output,),
        (table, partial, ready, side_factor, sqrt_next),
        scratch=[
            pltpu.SMEM((TABLE,), jnp.int32),
            pltpu.VMEM((1, size, size), jnp.float32),
            pltpu.SemaphoreType.DMA((5,)),
        ],
        hbm_in=(4,),
        any_in=(0,),
        hbm_out=True,
        in_place=4,
    )
    (sqrt_next,) = call(
        last_kernel,
        (output,),
        (last_slots, partial, term, sqrt_next),
        scratch=[
            pltpu.VMEM((ROWS * ROWS, block, block), jnp.float32),
            pltpu.SemaphoreType.DMA((ROWS * ROWS,)),
        ],
        hbm_in=(3,),
        hbm_out=True,
        in_place=3,
    )
    return sqrt_next, inverse_next


def solution(mesh):
    rows = P(("row", "col"), None, None)
    return jax.shard_map(
        local,
        mesh=mesh,
        in_specs=(rows, rows, P(), P(), P()),
        out_specs=(rows, rows),
        check_vma=False,
    )
```

```python
import functools

import jax
import jax.numpy as jnp
from jax import lax
from jax.experimental import pallas as pl
from jax.experimental.pallas import tpu as pltpu
from jax.sharding import PartitionSpec as P

PEER, OWN, MATE, SIDE = range(4)
ROWS = 2
SLOTS = 8
KEPT_PEER_AT, KEPT_MATE_AT, KEPT_LINES = 16, 20, 24
LARGEST = float(jnp.finfo(jnp.bfloat16).max)
VMEM_LIMIT = 24 * 2**20
PEAK = 1.153e9


def split(value):
    clipped = jnp.clip(value, -LARGEST, LARGEST)
    high = clipped.astype(jnp.bfloat16)
    low = (value - high.astype(jnp.float32)).astype(jnp.bfloat16)
    return high, low


def products(*pairs):
    left = [part for (high, low), _ in pairs for part in (high, low, high)]
    right = [part for _, (high, low) in pairs for part in (high, high, low)]
    return jnp.dot(
        jnp.concatenate(left, axis=1),
        jnp.concatenate(right, axis=0),
        preferred_element_type=jnp.float32,
    )


def filtered(kept, value, region, scale=None, base=0, width=SLOTS):
    size = value.shape[0] // ROWS
    rows = []
    for i in range(ROWS):
        row = []
        for j in range(ROWS):
            at = base + i * width + region * ROWS + j
            flag = kept[at:at + 1, :]
            if scale is not None:
                flag = flag * scale
            row.append(value[i * size:(i + 1) * size, j * size:(j + 1) * size] * flag)
        rows.append(jnp.concatenate(row, axis=1))
    return jnp.concatenate(rows, axis=0)


def neighbours(row_devices, col_devices, order):
    row = lax.axis_index("row")
    col = lax.axis_index("col")
    odd = lax.rem(row, 2)

    def first(row_of, col_of):
        return (lax.rem(row_of, row_devices) * col_devices + lax.rem(col_of, col_devices)) * ROWS

    starts = (
        first(row + row_devices - 1 + 2 * odd, col),
        first(row, col),
        first(row + 1 - 2 * odd, col),
        first(row, col + 1),
    )
    return starts, [order[start + j] for start in starts for j in range(ROWS)]


def find_slots(pattern, stored, wanted):
    slots = [jnp.int32(0)] * len(wanted)
    for k in range(SLOTS):
        label = pattern[k, stored]
        slots = [jnp.where(label == want, k, slot) for want, slot in zip(wanted, slots)]
    return slots


def look_up(row_devices, col_devices, pattern, keep, order, slots, kept):
    starts, labels = neighbours(row_devices, col_devices, order)
    own_labels = labels[OWN * ROWS:(OWN + 1) * ROWS]

    def write_flags(stored, found, line):
        for j, slot in enumerate(found):
            flag = ((slot == 0) | (keep[slot, stored] == 1)).astype(jnp.float32)
            kept[line + j:line + j + 1, :] = jnp.full((1, kept.shape[1]), flag)

    result = []
    for i in range(ROWS):
        found = find_slots(pattern, starts[OWN] + i, labels)
        result.append(found)
        for j, slot in enumerate(found):
            line = i * SLOTS + j
            slots[line:line + 1, :] = jnp.full((1, slots.shape[1]), slot)
        write_flags(starts[OWN] + i, found, i * SLOTS)
        for region, line in ((PEER, KEPT_PEER_AT), (MATE, KEPT_MATE_AT)):
            stored = starts[region] + i
            write_flags(stored, find_slots(pattern, stored, own_labels), line + i * ROWS)
    return result


def quarter(i, j, size):
    return slice(i * size, (i + 1) * size), slice(j * size, (j + 1) * size)


def gather(slot_of, source, places):
    size = source.shape[1]
    for region, region_places in places.items():
        for i in range(ROWS):
            for j in range(ROWS):
                start = pl.multiple_of(slot_of(i, region * ROWS + j) * size, size)
                block = source[i, :, pl.ds(start, size)]
                for place in region_places:
                    place(i, j, size, block)


def into(out):
    def place(i, j, size, block):
        rows, cols = quarter(i, j, size)
        out[rows, cols] = block

    return place


def strip_peer(out):
    def place(i, j, size, block):
        out[i, :, j * size:(j + 1) * size] = block

    return place


def strip_own(out):
    def place(i, j, size, block):
        if i != j:
            out[ROWS, :, i * size:(i + 1) * size] = block

    return place


def peer_part(strips):
    return jnp.concatenate([strips[i] for i in range(ROWS)], axis=0)


def own_part(strips, spread):
    size = strips.shape[1]
    beside = strips[ROWS]
    return jnp.concatenate(
        [
            jnp.concatenate([spread[:size, :size], beside[:, :size]], axis=1),
            jnp.concatenate([beside[:, size:], spread[size:, size:]], axis=1),
        ],
        axis=0,
    )


def diagonal_kernel(sqrt_iterate, inverse_iterate, diagonal, sems):
    size = sqrt_iterate.shape[1]
    copies = []
    for source in (sqrt_iterate, inverse_iterate):
        for i in range(ROWS):
            at = len(copies)
            copies.append(
                pltpu.make_async_copy(source.at[i, :, pl.ds(0, size)], diagonal.at[at], sems.at[at])
            )
            copies[at].start()
    for copy in copies:
        copy.wait()


def pack_kernel(
    row_devices, col_devices, pattern, keep, order, sqrt_iterate, inverse_iterate, after,
    slots, kept, y_strips, z_strips, y_mate, mate_rest, y_side, z_side, to_side,
    pattern_here, keep_here, order_here, sqrt_here, inverse_here, sems,
):
    copies = [
        pltpu.make_async_copy(source, here, sems.at[at])
        for at, (source, here) in enumerate((
            (order, order_here), (pattern, pattern_here), (keep, keep_here),
            (sqrt_iterate, sqrt_here), (inverse_iterate, inverse_here),
        ))
    ]
    for copy in copies:
        copy.start()
    for copy in copies[:3]:
        copy.wait()
    found = look_up(
        row_devices, col_devices, pattern_here, keep_here, order_here, slots, kept
    )

    def slot_of(i, j):
        return found[i][j]

    copies[3].wait()
    places = {
        PEER: (strip_peer(y_strips),),
        OWN: (strip_own(y_strips), into(mate_rest.at[0]), into(to_side.at[0])),
        MATE: (into(y_mate),),
        SIDE: (into(y_side),),
    }
    gather(slot_of, sqrt_here, places)
    copies[4].wait()
    places = {
        PEER: (strip_peer(z_strips),),
        OWN: (strip_own(z_strips), into(mate_rest.at[2]), into(to_side.at[1])),
        MATE: (into(mate_rest.at[1]),),
        SIDE: (into(z_side),),
    }
    gather(slot_of, inverse_here, places)


def spread_kernel(diagonal, spread):
    size = diagonal.shape[1]
    for at in range(2):
        for i in range(ROWS):
            for j in range(ROWS):
                rows, cols = quarter(i, j, size)
                block = diagonal[at * ROWS + i]
                spread[at, rows, cols] = block if i == j else jnp.zeros_like(block)


M_OWN, M_Y_OWN, M_Y_MATE, M_Z_OWN, M_Z_MATE = range(5)


def mate_kernel(
    kept, y_mate, mate_rest, mate_y, from_mate, after, mate_terms
):
    y_own, z_to_mate, z_own = (split(mate_rest[at]) for at in range(3))
    y_to_mate = split(y_mate[...])
    mate_y_mate, mate_y_own = split(mate_y[...]), split(from_mate[0])
    mate_z_mate, mate_z_own = split(from_mate[1]), split(from_mate[2])
    mate_terms[M_OWN] = products((z_own, y_own), (z_to_mate, mate_y_mate))
    total = products((z_own, y_to_mate), (z_to_mate, mate_y_own))
    f_mate = split(filtered(kept, total, MATE, -0.5))
    total = products((mate_z_own, mate_y_mate), (mate_z_mate, y_own))
    mate_f_mate = split(filtered(kept, total, 0, -0.5, KEPT_MATE_AT, ROWS))
    mate_terms[M_Y_OWN] = products((y_to_mate, mate_f_mate))
    mate_terms[M_Y_MATE] = products((y_own, f_mate))
    mate_terms[M_Z_OWN] = products((f_mate, mate_z_mate))
    mate_terms[M_Z_MATE] = products((f_mate, mate_z_own))


def factor_own_kernel(kept, mate_terms, z_strips, peer_y, factor_own, peer_term):
    peer_y_peer = split(peer_part(peer_y))
    total = mate_terms[M_OWN] + products((split(peer_part(z_strips)), peer_y_peer))
    rows = lax.broadcasted_iota(jnp.int32, total.shape, 0)
    cols = lax.broadcasted_iota(jnp.int32, total.shape, 1)
    factor = jnp.where(rows == cols, 1.5, 0.0) + filtered(kept, total, OWN, -0.5)
    factor_own[...] = factor
    term = products((peer_y_peer, split(factor)))
    peer_term[...] = filtered(kept, term, 0, None, KEPT_PEER_AT, ROWS)


Y_MATE, Z_MATE, Z_SIDE = range(3)
Y_OWN_PART, Y_PEER_PART, Y_SIDE_PART, Z_OWN_PART, Z_PEER_PART = range(5)
Y_PEER, Y_OWN, Y_SIDE, F_PEER, PEER_Y = range(5)


def middle_kernel(
    kept, y_strips, z_strips, y_mate, mate_rest, y_side, z_side, mate_terms,
    peer_y, peer_spread, from_side, factor_own, mate_factor,
    finished, partial, ready,
):
    def keep(at, parts):
        ready[at, 0], ready[at, 1] = parts

    y_own, z_to_mate, z_own = (split(mate_rest[at]) for at in range(3))
    y_to_peer, z_to_peer = split(peer_part(y_strips)), split(peer_part(z_strips))
    y_to_side, z_to_side = split(y_side[...]), split(z_side[...])
    f_own = split(factor_own[...])
    keep(Y_OWN, y_own)
    keep(Y_SIDE, y_to_side)
    keep(Y_PEER, y_to_peer)
    keep(PEER_Y, split(peer_part(peer_y)))

    peer_y_own = split(own_part(peer_y, peer_spread[0]))
    total = products((z_own, y_to_peer), (z_to_peer, peer_y_own))
    f_peer = split(filtered(kept, total, PEER, -0.5))
    keep(F_PEER, f_peer)
    total = products((z_own, y_to_side), (z_to_side, split(from_side[0])))
    f_side = split(filtered(kept, total, SIDE, -0.5))

    partial[Y_PEER_PART] = filtered(kept, products((y_own, f_peer)), PEER)
    partial[Y_SIDE_PART] = products((y_own, f_side))
    partial[Y_OWN_PART] = mate_terms[M_Y_OWN] + products((y_own, f_own))
    partial[Z_PEER_PART] = products((f_own, z_to_peer))
    partial[Z_OWN_PART] = mate_terms[M_Z_OWN] + products((f_own, z_own))
    value = mate_terms[M_Y_MATE] + products((split(y_mate[...]), split(mate_factor[...])))
    finished[Y_MATE] = filtered(kept, value, MATE)
    value = mate_terms[M_Z_MATE] + products((f_own, z_to_mate))
    finished[Z_MATE] = filtered(kept, value, MATE)
    value = products((f_own, z_to_side), (f_side, split(from_side[1])))
    finished[Z_SIDE] = filtered(kept, value, SIDE)


class Writer:
    def __init__(self, slots, kept, result, sems):
        self.slots, self.kept, self.result, self.sems = slots, kept, result, sems
        self.started = []
        self.held = 0

    def write(self, source, out, region):
        size = out.shape[1]
        for i in range(ROWS):
            for j in range(ROWS):
                rows, cols = quarter(i, j, size)
                slot = self.slots[i * SLOTS + region * ROWS + j, 0]
                copy = pltpu.make_async_copy(
                    source.at[rows, cols],
                    out.at[i, :, pl.ds(pl.multiple_of(slot * size, size), size)],
                    self.sems.at[len(self.started)],
                )
                copy.start()
                self.started.append(copy)

    def finish(self, value, out, region):
        place = self.result.at[self.held]
        self.held += 1
        place[...] = value if self.kept is None else filtered(self.kept, value, region)
        self.write(place, out, region)

    def wait(self):
        for copy in self.started:
            copy.wait()


def peer_kernel(
    slots, kept, finished, partial, ready, peer_z, peer_spread,
    sqrt_next, inverse_next, result, sems,
):
    def held(at):
        return ready[at, 0], ready[at, 1]

    writer = Writer(slots, kept, result, sems)
    writer.write(finished.at[Y_MATE], sqrt_next, MATE)
    writer.write(finished.at[Z_MATE], inverse_next, MATE)
    writer.write(finished.at[Z_SIDE], inverse_next, SIDE)
    peer_z_peer = split(peer_part(peer_z))
    peer_z_own = split(own_part(peer_z, peer_spread[1]))
    f_peer = held(F_PEER)
    value = partial[Z_PEER_PART] + products((f_peer, peer_z_own))
    writer.finish(value, inverse_next, PEER)
    value = partial[Z_OWN_PART] + products((f_peer, peer_z_peer))
    writer.finish(value, inverse_next, OWN)
    total = products((peer_z_own, held(PEER_Y)), (peer_z_peer, held(Y_OWN)))
    peer_f_peer = split(filtered(kept, total, 0, -0.5, KEPT_PEER_AT, ROWS))
    value = partial[Y_OWN_PART] + products((held(Y_PEER), peer_f_peer))
    writer.finish(value, sqrt_next, OWN)
    writer.wait()


def side_kernel(slots, kept, partial, ready, factor, unfinished, sqrt_next, result, sems):
    left = (ready[Y_SIDE, 0], ready[Y_SIDE, 1])
    value = partial[Y_SIDE_PART] + products((left, split(factor[...])))
    writer = Writer(slots, kept, result, sems)
    writer.finish(value, sqrt_next, SIDE)
    writer.wait()


def last_kernel(slots, partial, term, unfinished, sqrt_next, result, sems):
    writer = Writer(slots, None, result, sems)
    writer.finish(partial[Y_PEER_PART] + term[...], sqrt_next, PEER)
    writer.wait()


def call(
    kernel, outs, operands, micros=0, scratch=(), hbm_in=(), any_in=(), hbm_out=False, in_place=None
):
    def spec(space=pltpu.VMEM):
        return pl.BlockSpec(memory_space=space)

    operands = [
        pltpu.with_memory_space_constraint(array, pltpu.HBM) if at in hbm_in else array
        for at, array in enumerate(operands)
    ]
    return pl.pallas_call(
        kernel,
        out_shape=outs,
        in_specs=[
            spec(pltpu.HBM if at in hbm_in else pl.ANY if at in any_in else pltpu.VMEM)
            for at in range(len(operands))
        ],
        out_specs=tuple(spec(pltpu.HBM if hbm_out else pltpu.VMEM) for _ in outs),
        scratch_shapes=scratch,
        input_output_aliases={} if in_place is None else {in_place: 0},
        compiler_params=pltpu.CompilerParams(vmem_limit_bytes=VMEM_LIMIT),
        cost_estimate=pl.CostEstimate(
            flops=int(micros * PEAK), bytes_accessed=0, transcendentals=0
        ),
    )(*operands)


def local(sqrt_iterate, inverse_iterate, pattern, keep_mask, row_order):
    rows_dev, block, width = sqrt_iterate.shape
    row_devices, col_devices = lax.axis_size("row"), lax.axis_size("col")
    assert rows_dev == ROWS and width == SLOTS * block and pattern.shape[1] == SLOTS
    assert row_devices > 3 and row_devices % 2 == 0 and col_devices > 2
    size = ROWS * block

    def to_mate(value):
        return lax.ppermute(value, "row", [(i, i ^ 1) for i in range(row_devices)])

    def to_peer(value):
        route = [(i, (i + (1 if i % 2 else -1)) % row_devices) for i in range(row_devices)]
        return lax.ppermute(value, "row", route)

    def to_side(value):
        route = [((i + 1) % col_devices, i) for i in range(col_devices)]
        return lax.ppermute(value, "col", route)

    def shape(*dims, dtype=jnp.float32):
        return jax.ShapeDtypeStruct(dims, dtype)

    one, pair = shape(size, size), shape(2, size, size)
    (diagonal,) = call(
        diagonal_kernel,
        (shape(2 * ROWS, block, block),),
        (sqrt_iterate, inverse_iterate),
        scratch=[pltpu.SemaphoreType.DMA((2 * ROWS,))],
        hbm_in=range(2),
    )
    peer_diagonal = to_peer(diagonal)
    strips = shape(ROWS + 1, block, size)
    slots, kept, y_strips, z_strips, y_mate, mate_rest, y_side, z_side, own_pair = call(
        functools.partial(pack_kernel, row_devices, col_devices),
        (
            shape(ROWS * SLOTS, block, dtype=jnp.int32), shape(KEPT_LINES, block),
            strips, strips, one, shape(3, size, size), one, one, pair,
        ),
        (pattern.T, keep_mask.T, row_order, sqrt_iterate, inverse_iterate, diagonal),
        scratch=[
            pltpu.SMEM(pattern.T.shape, jnp.int32),
            pltpu.SMEM(keep_mask.T.shape, jnp.int32),
            pltpu.SMEM(row_order.shape, jnp.int32),
            pltpu.VMEM(sqrt_iterate.shape, jnp.float32),
            pltpu.VMEM(inverse_iterate.shape, jnp.float32),
            pltpu.SemaphoreType.DMA((5,)),
        ],
        hbm_in=range(5),
        any_in=(5,),
    )
    peer_y = to_peer(y_strips)
    peer_z = to_peer(z_strips)
    mate_y = to_mate(y_mate)
    from_mate = to_mate(mate_rest)
    from_side = to_side(own_pair)
    (peer_spread,) = call(spread_kernel, (pair,), (peer_diagonal,), micros=10)
    (mate_terms,) = call(
        mate_kernel,
        (shape(5, size, size),),
        (kept, y_mate, mate_rest, mate_y, from_mate, peer_spread),
        any_in=(5,),
    )
    factor_own, peer_term = call(
        factor_own_kernel, (one, one), (kept, mate_terms, z_strips, peer_y), micros=5
    )
    mate_factor = to_mate(factor_own)
    term = to_peer(peer_term)
    side_factor = to_side(factor_own)
    finished, partial, ready = call(
        middle_kernel,
        (
            shape(3, size, size), shape(5, size, size),
            shape(5, 2, size, size, dtype=jnp.bfloat16),
        ),
        (
            kept, y_strips, z_strips, y_mate, mate_rest, y_side, z_side, mate_terms,
            peer_y, peer_spread, from_side, factor_own, mate_factor,
        ),
    )
    output = shape(rows_dev, block, width)

    def writing(blocks):
        return [
            pltpu.VMEM((blocks, size, size), jnp.float32),
            pltpu.SemaphoreType.DMA((24,)),
        ]

    sqrt_next, inverse_next = call(
        peer_kernel,
        (output, output),
        (slots, kept, finished, partial, ready, peer_z, peer_spread),
        scratch=writing(3),
        hbm_out=True,
    )
    (sqrt_next,) = call(
        side_kernel,
        (output,),
        (slots, kept, partial, ready, side_factor, sqrt_next),
        scratch=writing(1),
        hbm_in=(5,),
        hbm_out=True,
        in_place=5,
    )
    (sqrt_next,) = call(
        last_kernel,
        (output,),
        (slots, partial, term, sqrt_next),
        scratch=writing(1),
        hbm_in=(3,),
        hbm_out=True,
        in_place=3,
    )
    return sqrt_next, inverse_next


def solution(mesh):
    rows = P(("row", "col"), None, None)
    return jax.shard_map(
        local,
        mesh=mesh,
        in_specs=(rows, rows, P(), P(), P()),
        out_specs=(rows, rows),
        check_vma=False,
    )
```

```python
import functools

import jax
import jax.numpy as jnp
from jax import lax
from jax.experimental import pallas as pl
from jax.experimental.pallas import tpu as pltpu
from jax.sharding import PartitionSpec as P

PEER, OWN, MATE, SIDE = range(4)
ROWS = 2
SLOTS = 8
KEPT_PEER_AT, KEPT_MATE_AT, KEPT_LINES = 16, 20, 24
LARGEST = float(jnp.finfo(jnp.bfloat16).max)
VMEM_LIMIT = 24 * 2**20
PEAK = 1.153e9


def split(value):
    clipped = jnp.clip(value, -LARGEST, LARGEST)
    high = clipped.astype(jnp.bfloat16)
    low = (value - high.astype(jnp.float32)).astype(jnp.bfloat16)
    return high, low


def products(*pairs):
    left = [part for (high, low), _ in pairs for part in (high, low, high)]
    right = [part for _, (high, low) in pairs for part in (high, high, low)]
    return jnp.dot(
        jnp.concatenate(left, axis=1),
        jnp.concatenate(right, axis=0),
        preferred_element_type=jnp.float32,
    )


def filtered(kept, value, region, scale=None, base=0, width=SLOTS):
    size = value.shape[0] // ROWS
    rows = []
    for i in range(ROWS):
        row = []
        for j in range(ROWS):
            at = base + i * width + region * ROWS + j
            flag = kept[at:at + 1, :]
            if scale is not None:
                flag = flag * scale
            row.append(value[i * size:(i + 1) * size, j * size:(j + 1) * size] * flag)
        rows.append(jnp.concatenate(row, axis=1))
    return jnp.concatenate(rows, axis=0)


def neighbours(row_devices, col_devices, order):
    row = lax.axis_index("row")
    col = lax.axis_index("col")
    odd = lax.rem(row, 2)

    def first(row_of, col_of):
        return (lax.rem(row_of, row_devices) * col_devices + lax.rem(col_of, col_devices)) * ROWS

    starts = (
        first(row + row_devices - 1 + 2 * odd, col),
        first(row, col),
        first(row + 1 - 2 * odd, col),
        first(row, col + 1),
    )
    return starts, [order[start + j] for start in starts for j in range(ROWS)]


def find_slots(pattern, stored, wanted):
    slots = [jnp.int32(0)] * len(wanted)
    for k in range(SLOTS):
        label = pattern[k, stored]
        slots = [jnp.where(label == want, k, slot) for want, slot in zip(wanted, slots)]
    return slots


def look_up(row_devices, col_devices, pattern, keep, order, slots, kept):
    starts, labels = neighbours(row_devices, col_devices, order)
    own_labels = labels[OWN * ROWS:(OWN + 1) * ROWS]

    def write_flags(stored, found, line):
        for j, slot in enumerate(found):
            flag = ((slot == 0) | (keep[slot, stored] == 1)).astype(jnp.float32)
            kept[line + j:line + j + 1, :] = jnp.full((1, kept.shape[1]), flag)

    result = []
    for i in range(ROWS):
        found = find_slots(pattern, starts[OWN] + i, labels)
        result.append(found)
        for j, slot in enumerate(found):
            line = i * SLOTS + j
            slots[line:line + 1, :] = jnp.full((1, slots.shape[1]), slot)
        write_flags(starts[OWN] + i, found, i * SLOTS)
        for region, line in ((PEER, KEPT_PEER_AT), (MATE, KEPT_MATE_AT)):
            stored = starts[region] + i
            write_flags(stored, find_slots(pattern, stored, own_labels), line + i * ROWS)
    return result


def quarter(i, j, size):
    return slice(i * size, (i + 1) * size), slice(j * size, (j + 1) * size)


def gather(slot_of, source, places):
    size = source.shape[1]
    for region, region_places in places.items():
        for i in range(ROWS):
            for j in range(ROWS):
                start = pl.multiple_of(slot_of(i, region * ROWS + j) * size, size)
                block = source[i, :, pl.ds(start, size)]
                for place in region_places:
                    place(i, j, size, block)


def into(out):
    def place(i, j, size, block):
        rows, cols = quarter(i, j, size)
        out[rows, cols] = block

    return place


def strip_peer(out):
    def place(i, j, size, block):
        out[i, :, j * size:(j + 1) * size] = block

    return place


def strip_own(out, at):
    def place(i, j, size, block):
        if i != j:
            out[at, :, i * size:(i + 1) * size] = block

    return place


Y_BESIDE, Z_BESIDE = ROWS, ROWS + 1


def peer_part(strips):
    return jnp.concatenate([strips[i] for i in range(ROWS)], axis=0)


def own_part(beside, spread):
    size = beside.shape[0]
    return jnp.concatenate(
        [
            jnp.concatenate([spread[:size, :size], beside[:, :size]], axis=1),
            jnp.concatenate([beside[:, size:], spread[size:, size:]], axis=1),
        ],
        axis=0,
    )


def diagonal_kernel(sqrt_iterate, inverse_iterate, diagonal, sems):
    size = sqrt_iterate.shape[1]
    copies = []
    for source in (sqrt_iterate, inverse_iterate):
        for i in range(ROWS):
            at = len(copies)
            copies.append(
                pltpu.make_async_copy(source.at[i, :, pl.ds(0, size)], diagonal.at[at], sems.at[at])
            )
            copies[at].start()
    for copy in copies:
        copy.wait()


def pack_kernel(
    row_devices, col_devices, pattern, keep, order, sqrt_iterate, inverse_iterate, after,
    slots, kept, y_peer, strips, y_mate, mate_rest, y_side, z_side, to_side,
    pattern_here, keep_here, order_here, sqrt_here, inverse_here, sems,
):
    copies = [
        pltpu.make_async_copy(source, here, sems.at[at])
        for at, (source, here) in enumerate((
            (order, order_here), (pattern, pattern_here), (keep, keep_here),
            (sqrt_iterate, sqrt_here), (inverse_iterate, inverse_here),
        ))
    ]
    for copy in copies:
        copy.start()
    for copy in copies[:3]:
        copy.wait()
    found = look_up(
        row_devices, col_devices, pattern_here, keep_here, order_here, slots, kept
    )

    def slot_of(i, j):
        return found[i][j]

    copies[3].wait()
    places = {
        PEER: (into(y_peer),),
        OWN: (strip_own(strips, Y_BESIDE), into(mate_rest.at[0]), into(to_side.at[0])),
        MATE: (into(y_mate),),
        SIDE: (into(y_side),),
    }
    gather(slot_of, sqrt_here, places)
    copies[4].wait()
    places = {
        PEER: (strip_peer(strips),),
        OWN: (strip_own(strips, Z_BESIDE), into(mate_rest.at[2]), into(to_side.at[1])),
        MATE: (into(mate_rest.at[1]),),
        SIDE: (into(z_side),),
    }
    gather(slot_of, inverse_here, places)


def spread_kernel(diagonal, spread):
    size = diagonal.shape[1]
    for at in range(2):
        for i in range(ROWS):
            for j in range(ROWS):
                rows, cols = quarter(i, j, size)
                block = diagonal[at * ROWS + i]
                spread[at, rows, cols] = block if i == j else jnp.zeros_like(block)


M_OWN, M_Y_OWN, M_Y_MATE, M_Z_OWN, M_Z_MATE = range(5)


def mate_kernel(
    kept, y_mate, mate_rest, mate_y, from_mate, after, mate_terms
):
    y_own, z_to_mate, z_own = (split(mate_rest[at]) for at in range(3))
    y_to_mate = split(y_mate[...])
    mate_y_mate, mate_y_own = split(mate_y[...]), split(from_mate[0])
    mate_z_mate, mate_z_own = split(from_mate[1]), split(from_mate[2])
    mate_terms[M_OWN] = products((z_own, y_own), (z_to_mate, mate_y_mate))
    total = products((z_own, y_to_mate), (z_to_mate, mate_y_own))
    f_mate = split(filtered(kept, total, MATE, -0.5))
    total = products((mate_z_own, mate_y_mate), (mate_z_mate, y_own))
    mate_f_mate = split(filtered(kept, total, 0, -0.5, KEPT_MATE_AT, ROWS))
    mate_terms[M_Y_OWN] = products((y_to_mate, mate_f_mate))
    mate_terms[M_Y_MATE] = products((y_own, f_mate))
    mate_terms[M_Z_OWN] = products((f_mate, mate_z_mate))
    mate_terms[M_Z_MATE] = products((f_mate, mate_z_own))


def factor_own_kernel(kept, mate_terms, strips, peer_y, factor_own, peer_term):
    peer_y_peer = split(peer_y[...])
    total = mate_terms[M_OWN] + products((split(peer_part(strips)), peer_y_peer))
    rows = lax.broadcasted_iota(jnp.int32, total.shape, 0)
    cols = lax.broadcasted_iota(jnp.int32, total.shape, 1)
    factor = jnp.where(rows == cols, 1.5, 0.0) + filtered(kept, total, OWN, -0.5)
    factor_own[...] = factor
    term = products((peer_y_peer, split(factor)))
    peer_term[...] = filtered(kept, term, 0, None, KEPT_PEER_AT, ROWS)


Y_MATE, Z_MATE, Z_SIDE = range(3)
Y_OWN_PART, Y_SIDE_PART, Z_OWN_PART, Z_PEER_PART, PEER_PART = range(5)
Y_PEER, Y_OWN, Y_SIDE, PEER_Y, Z_PEER = range(5)


def middle_kernel(
    kept, y_peer, strips, y_mate, mate_rest, y_side, z_side, mate_terms,
    peer_y, from_side, factor_own, mate_factor,
    finished, partial, ready,
):
    def keep(at, parts):
        ready[at, 0], ready[at, 1] = parts

    y_own, z_to_mate, z_own = (split(mate_rest[at]) for at in range(3))
    y_to_peer, z_to_peer = split(y_peer[...]), split(peer_part(strips))
    y_to_side, z_to_side = split(y_side[...]), split(z_side[...])
    f_own = split(factor_own[...])
    keep(Y_OWN, y_own)
    keep(Y_SIDE, y_to_side)
    keep(Y_PEER, y_to_peer)
    keep(Z_PEER, z_to_peer)
    keep(PEER_Y, split(peer_y[...]))

    total = products((z_own, y_to_side), (z_to_side, split(from_side[0])))
    f_side = split(filtered(kept, total, SIDE, -0.5))
    partial[PEER_PART] = products((z_own, y_to_peer))
    partial[Y_SIDE_PART] = products((y_own, f_side))
    partial[Y_OWN_PART] = mate_terms[M_Y_OWN] + products((y_own, f_own))
    partial[Z_PEER_PART] = products((f_own, z_to_peer))
    partial[Z_OWN_PART] = mate_terms[M_Z_OWN] + products((f_own, z_own))
    value = mate_terms[M_Y_MATE] + products((split(y_mate[...]), split(mate_factor[...])))
    finished[Y_MATE] = filtered(kept, value, MATE)
    value = mate_terms[M_Z_MATE] + products((f_own, z_to_mate))
    finished[Z_MATE] = filtered(kept, value, MATE)
    value = products((f_own, z_to_side), (f_side, split(from_side[1])))
    finished[Z_SIDE] = filtered(kept, value, SIDE)


class Writer:
    def __init__(self, slots, kept, result, sems):
        self.slots, self.kept, self.result, self.sems = slots, kept, result, sems
        self.started = []
        self.held = 0

    def write(self, source, out, region):
        size = out.shape[1]
        for i in range(ROWS):
            for j in range(ROWS):
                rows, cols = quarter(i, j, size)
                slot = self.slots[i * SLOTS + region * ROWS + j, 0]
                copy = pltpu.make_async_copy(
                    source.at[rows, cols],
                    out.at[i, :, pl.ds(pl.multiple_of(slot * size, size), size)],
                    self.sems.at[len(self.started)],
                )
                copy.start()
                self.started.append(copy)

    def finish(self, value, out, region):
        place = self.result.at[self.held]
        self.held += 1
        place[...] = filtered(self.kept, value, region)
        self.write(place, out, region)

    def wait(self):
        for copy in self.started:
            copy.wait()


def peer_kernel(
    slots, kept, finished, partial, ready, from_peer, peer_spread,
    sqrt_next, inverse_next, y_peer_part, result, sems,
):
    def held(at):
        return ready[at, 0], ready[at, 1]

    writer = Writer(slots, kept, result, sems)
    writer.write(finished.at[Y_MATE], sqrt_next, MATE)
    writer.write(finished.at[Z_MATE], inverse_next, MATE)
    writer.write(finished.at[Z_SIDE], inverse_next, SIDE)
    peer_y_own = split(own_part(from_peer[Y_BESIDE], peer_spread[0]))
    peer_z_own = split(own_part(from_peer[Z_BESIDE], peer_spread[1]))
    peer_z_peer = split(peer_part(from_peer))
    total = partial[PEER_PART] + products((held(Z_PEER), peer_y_own))
    f_peer = split(filtered(kept, total, PEER, -0.5))
    total = products((peer_z_own, held(PEER_Y)), (peer_z_peer, held(Y_OWN)))
    peer_f_peer = split(filtered(kept, total, 0, -0.5, KEPT_PEER_AT, ROWS))
    value = partial[Z_PEER_PART] + products((f_peer, peer_z_own))
    writer.finish(value, inverse_next, PEER)
    value = partial[Z_OWN_PART] + products((f_peer, peer_z_peer))
    writer.finish(value, inverse_next, OWN)
    value = partial[Y_OWN_PART] + products((held(Y_PEER), peer_f_peer))
    writer.finish(value, sqrt_next, OWN)
    y_peer_part[...] = filtered(kept, products((held(Y_OWN), f_peer)), PEER)
    writer.wait()


def side_kernel(slots, kept, partial, ready, factor, unfinished, sqrt_next, result, sems):
    left = (ready[Y_SIDE, 0], ready[Y_SIDE, 1])
    value = partial[Y_SIDE_PART] + products((left, split(factor[...])))
    writer = Writer(slots, kept, result, sems)
    writer.finish(value, sqrt_next, SIDE)
    writer.wait()


def last_kernel(slots, part, term, unfinished, sqrt_next, result, sems):
    size = sqrt_next.shape[1]
    copies = []
    for i in range(ROWS):
        for j in range(ROWS):
            at = len(copies)
            rows, cols = quarter(i, j, size)
            result[at] = part[rows, cols] + term[rows, cols]
            slot = slots[i * SLOTS + PEER * ROWS + j, 0]
            out = sqrt_next.at[i, :, pl.ds(pl.multiple_of(slot * size, size), size)]
            copies.append(pltpu.make_async_copy(result.at[at], out, sems.at[at]))
            copies[at].start()
    for copy in copies:
        copy.wait()


def call(
    kernel, outs, operands, micros=0, scratch=(), hbm_in=(), any_in=(), hbm_out=(), in_place=None
):
    def spec(space=pltpu.VMEM):
        return pl.BlockSpec(memory_space=space)

    operands = [
        pltpu.with_memory_space_constraint(array, pltpu.HBM) if at in hbm_in else array
        for at, array in enumerate(operands)
    ]
    return pl.pallas_call(
        kernel,
        out_shape=outs,
        in_specs=[
            spec(pltpu.HBM if at in hbm_in else pl.ANY if at in any_in else pltpu.VMEM)
            for at in range(len(operands))
        ],
        out_specs=tuple(
            spec(pltpu.HBM if at in hbm_out else pltpu.VMEM) for at in range(len(outs))
        ),
        scratch_shapes=scratch,
        input_output_aliases={} if in_place is None else {in_place: 0},
        compiler_params=pltpu.CompilerParams(vmem_limit_bytes=VMEM_LIMIT),
        cost_estimate=pl.CostEstimate(
            flops=int(micros * PEAK), bytes_accessed=0, transcendentals=0
        ),
    )(*operands)


def local(sqrt_iterate, inverse_iterate, pattern, keep_mask, row_order):
    rows_dev, block, width = sqrt_iterate.shape
    row_devices, col_devices = lax.axis_size("row"), lax.axis_size("col")
    assert rows_dev == ROWS and width == SLOTS * block and pattern.shape[1] == SLOTS
    assert row_devices > 3 and row_devices % 2 == 0 and col_devices > 2
    size = ROWS * block

    def to_mate(value):
        return lax.ppermute(value, "row", [(i, i ^ 1) for i in range(row_devices)])

    def to_peer(value):
        route = [(i, (i + (1 if i % 2 else -1)) % row_devices) for i in range(row_devices)]
        return lax.ppermute(value, "row", route)

    def to_side(value):
        route = [((i + 1) % col_devices, i) for i in range(col_devices)]
        return lax.ppermute(value, "col", route)

    def shape(*dims, dtype=jnp.float32):
        return jax.ShapeDtypeStruct(dims, dtype)

    one, pair = shape(size, size), shape(2, size, size)
    (diagonal,) = call(
        diagonal_kernel,
        (shape(2 * ROWS, block, block),),
        (sqrt_iterate, inverse_iterate),
        scratch=[pltpu.SemaphoreType.DMA((2 * ROWS,))],
        hbm_in=range(2),
    )
    peer_diagonal = to_peer(diagonal)
    slots, kept, y_peer, strips, y_mate, mate_rest, y_side, z_side, own_pair = call(
        functools.partial(pack_kernel, row_devices, col_devices),
        (
            shape(ROWS * SLOTS, block, dtype=jnp.int32), shape(KEPT_LINES, block),
            one, shape(ROWS + 2, block, size), one, shape(3, size, size), one, one, pair,
        ),
        (pattern.T, keep_mask.T, row_order, sqrt_iterate, inverse_iterate, diagonal),
        scratch=[
            pltpu.SMEM(pattern.T.shape, jnp.int32),
            pltpu.SMEM(keep_mask.T.shape, jnp.int32),
            pltpu.SMEM(row_order.shape, jnp.int32),
            pltpu.VMEM(sqrt_iterate.shape, jnp.float32),
            pltpu.VMEM(inverse_iterate.shape, jnp.float32),
            pltpu.SemaphoreType.DMA((5,)),
        ],
        hbm_in=range(5),
        any_in=(5,),
    )
    peer_y = to_peer(y_peer)
    from_peer = to_peer(strips)
    mate_y = to_mate(y_mate)
    from_mate = to_mate(mate_rest)
    from_side = to_side(own_pair)
    (peer_spread,) = call(spread_kernel, (pair,), (peer_diagonal,), micros=10)
    (mate_terms,) = call(
        mate_kernel,
        (shape(5, size, size),),
        (kept, y_mate, mate_rest, mate_y, from_mate, peer_spread),
        any_in=(5,),
    )
    factor_own, peer_term = call(
        factor_own_kernel, (one, one), (kept, mate_terms, strips, peer_y), micros=5
    )
    mate_factor = to_mate(factor_own)
    term = to_peer(peer_term)
    side_factor = to_side(factor_own)
    finished, partial, ready = call(
        middle_kernel,
        (
            shape(3, size, size), shape(5, size, size),
            shape(5, 2, size, size, dtype=jnp.bfloat16),
        ),
        (
            kept, y_peer, strips, y_mate, mate_rest, y_side, z_side, mate_terms,
            peer_y, from_side, factor_own, mate_factor,
        ),
    )
    output = shape(rows_dev, block, width)

    def writing(blocks):
        return [
            pltpu.VMEM((blocks, size, size), jnp.float32),
            pltpu.SemaphoreType.DMA((24,)),
        ]

    sqrt_next, inverse_next, y_peer_part = call(
        peer_kernel,
        (output, output, one),
        (slots, kept, finished, partial, ready, from_peer, peer_spread),
        scratch=writing(3),
        hbm_out=(0, 1),
    )
    (sqrt_next,) = call(
        side_kernel,
        (output,),
        (slots, kept, partial, ready, side_factor, sqrt_next),
        scratch=writing(1),
        hbm_in=(5,),
        hbm_out=(0,),
        in_place=5,
    )
    (sqrt_next,) = call(
        last_kernel,
        (output,),
        (slots, y_peer_part, term, sqrt_next),
        scratch=[
            pltpu.VMEM((ROWS * ROWS, block, block), jnp.float32),
            pltpu.SemaphoreType.DMA((ROWS * ROWS,)),
        ],
        hbm_in=(3,),
        hbm_out=(0,),
        in_place=3,
    )
    return sqrt_next, inverse_next


def solution(mesh):
    rows = P(("row", "col"), None, None)
    return jax.shard_map(
        local,
        mesh=mesh,
        in_specs=(rows, rows, P(), P(), P()),
        out_specs=(rows, rows),
        check_vma=False,
    )
```

```python
import functools

import jax
import jax.numpy as jnp
from jax import lax
from jax.experimental import pallas as pl
from jax.experimental.pallas import tpu as pltpu
from jax.sharding import PartitionSpec as P

PEER, OWN, MATE, SIDE = range(4)
ROWS = 2
SLOTS = 8
KEPT_PEER_AT, KEPT_MATE_AT, KEPT_LINES = 16, 20, 24
LARGEST = float(jnp.finfo(jnp.bfloat16).max)
VMEM_LIMIT = 24 * 2**20
PEAK = 1.153e9


def split(value):
    clipped = jnp.clip(value, -LARGEST, LARGEST)
    high = clipped.astype(jnp.bfloat16)
    low = (value - high.astype(jnp.float32)).astype(jnp.bfloat16)
    return high, low


def products(*pairs):
    left = [part for (high, low), _ in pairs for part in (high, low, high)]
    right = [part for _, (high, low) in pairs for part in (high, high, low)]
    return jnp.dot(
        jnp.concatenate(left, axis=1),
        jnp.concatenate(right, axis=0),
        preferred_element_type=jnp.float32,
    )


def filtered(kept, value, region, scale=None, base=0, width=SLOTS):
    size = value.shape[0] // ROWS
    rows = []
    for i in range(ROWS):
        row = []
        for j in range(ROWS):
            at = base + i * width + region * ROWS + j
            flag = kept[at:at + 1, :]
            if scale is not None:
                flag = flag * scale
            row.append(value[i * size:(i + 1) * size, j * size:(j + 1) * size] * flag)
        rows.append(jnp.concatenate(row, axis=1))
    return jnp.concatenate(rows, axis=0)


def neighbours(row_devices, col_devices, order):
    row = lax.axis_index("row")
    col = lax.axis_index("col")
    odd = lax.rem(row, 2)

    def first(row_of, col_of):
        return (lax.rem(row_of, row_devices) * col_devices + lax.rem(col_of, col_devices)) * ROWS

    starts = (
        first(row + row_devices - 1 + 2 * odd, col),
        first(row, col),
        first(row + 1 - 2 * odd, col),
        first(row, col + 1),
    )
    return starts, [order[start + j] for start in starts for j in range(ROWS)]


def find_slots(pattern, stored, wanted):
    slots = [jnp.int32(0)] * len(wanted)
    for k in range(SLOTS):
        label = pattern[k, stored]
        slots = [jnp.where(label == want, k, slot) for want, slot in zip(wanted, slots)]
    return slots


def look_up(row_devices, col_devices, pattern, keep, order, slots, kept):
    starts, labels = neighbours(row_devices, col_devices, order)
    own_labels = labels[OWN * ROWS:(OWN + 1) * ROWS]

    def write_flags(stored, found, line):
        for j, slot in enumerate(found):
            flag = ((slot == 0) | (keep[slot, stored] == 1)).astype(jnp.float32)
            kept[line + j:line + j + 1, :] = jnp.full((1, kept.shape[1]), flag)

    result = []
    for i in range(ROWS):
        found = find_slots(pattern, starts[OWN] + i, labels)
        result.append(found)
        for j, slot in enumerate(found):
            line = i * SLOTS + j
            slots[line:line + 1, :] = jnp.full((1, slots.shape[1]), slot)
        write_flags(starts[OWN] + i, found, i * SLOTS)
        for region, line in ((PEER, KEPT_PEER_AT), (MATE, KEPT_MATE_AT)):
            stored = starts[region] + i
            write_flags(stored, find_slots(pattern, stored, own_labels), line + i * ROWS)
    return result


def quarter(i, j, size):
    return slice(i * size, (i + 1) * size), slice(j * size, (j + 1) * size)


def gather(slot_of, source, places):
    size = source.shape[1]
    for region, region_places in places.items():
        for i in range(ROWS):
            for j in range(ROWS):
                start = pl.multiple_of(slot_of(i, region * ROWS + j) * size, size)
                block = source[i, :, pl.ds(start, size)]
                for place in region_places:
                    place(i, j, size, block)


def into(out):
    def place(i, j, size, block):
        rows, cols = quarter(i, j, size)
        out[rows, cols] = block

    return place


def strip_peer(out):
    def place(i, j, size, block):
        out[i, :, j * size:(j + 1) * size] = block

    return place


def strip_own(out, at):
    def place(i, j, size, block):
        if i != j:
            out[at, :, i * size:(i + 1) * size] = block

    return place


Y_BESIDE, Z_BESIDE = ROWS, ROWS + 1


def peer_part(strips):
    return jnp.concatenate([strips[i] for i in range(ROWS)], axis=0)


def own_part(beside, spread):
    size = beside.shape[0]
    return jnp.concatenate(
        [
            jnp.concatenate([spread[:size, :size], beside[:, :size]], axis=1),
            jnp.concatenate([beside[:, size:], spread[size:, size:]], axis=1),
        ],
        axis=0,
    )


def diagonal_kernel(sqrt_iterate, inverse_iterate, diagonal, sems):
    size = sqrt_iterate.shape[1]
    copies = [
        pltpu.make_async_copy(
            source.at[:, :, pl.ds(0, size)], diagonal.at[pl.ds(at * ROWS, ROWS)], sems.at[at]
        )
        for at, source in enumerate((sqrt_iterate, inverse_iterate))
    ]
    for copy in copies:
        copy.start()
    for copy in copies:
        copy.wait()


def pack_kernel(
    row_devices, col_devices, pattern, keep, order, sqrt_iterate, inverse_iterate, after,
    slots, kept, y_peer, strips, mate, y_side, z_side, to_side,
    pattern_here, keep_here, order_here, sqrt_here, inverse_here, sems,
):
    copies = [
        pltpu.make_async_copy(source, here, sems.at[at])
        for at, (source, here) in enumerate((
            (order, order_here), (pattern, pattern_here), (keep, keep_here),
            (sqrt_iterate, sqrt_here), (inverse_iterate, inverse_here),
        ))
    ]
    for copy in copies:
        copy.start()
    for copy in copies[:3]:
        copy.wait()
    found = look_up(
        row_devices, col_devices, pattern_here, keep_here, order_here, slots, kept
    )

    def slot_of(i, j):
        return found[i][j]

    copies[3].wait()
    places = {
        PEER: (into(y_peer),),
        OWN: (strip_own(strips, Y_BESIDE), into(mate.at[1]), into(to_side.at[0])),
        MATE: (into(mate.at[0]),),
        SIDE: (into(y_side),),
    }
    gather(slot_of, sqrt_here, places)
    copies[4].wait()
    places = {
        PEER: (strip_peer(strips),),
        OWN: (strip_own(strips, Z_BESIDE), into(mate.at[3]), into(to_side.at[1])),
        MATE: (into(mate.at[2]),),
        SIDE: (into(z_side),),
    }
    gather(slot_of, inverse_here, places)


def spread_kernel(diagonal, spread):
    size = diagonal.shape[1]
    for at in range(2):
        for i in range(ROWS):
            for j in range(ROWS):
                rows, cols = quarter(i, j, size)
                block = diagonal[at * ROWS + i]
                spread[at, rows, cols] = block if i == j else jnp.zeros_like(block)


M_OWN, M_Y_OWN, M_Y_MATE, M_Z_OWN, M_Z_MATE = range(5)


def mate_kernel(kept, mate, from_mate, after, mate_terms):
    y_to_mate, y_own, z_to_mate, z_own = (split(mate[at]) for at in range(4))
    mate_y_mate, mate_y_own, mate_z_mate, mate_z_own = (split(from_mate[at]) for at in range(4))
    mate_terms[M_OWN] = products((z_own, y_own), (z_to_mate, mate_y_mate))
    total = products((z_own, y_to_mate), (z_to_mate, mate_y_own))
    f_mate = split(filtered(kept, total, MATE, -0.5))
    total = products((mate_z_own, mate_y_mate), (mate_z_mate, y_own))
    mate_f_mate = split(filtered(kept, total, 0, -0.5, KEPT_MATE_AT, ROWS))
    mate_terms[M_Y_OWN] = products((y_to_mate, mate_f_mate))
    mate_terms[M_Y_MATE] = products((y_own, f_mate))
    mate_terms[M_Z_OWN] = products((f_mate, mate_z_mate))
    mate_terms[M_Z_MATE] = products((f_mate, mate_z_own))


def factor_own_kernel(kept, mate_terms, strips, peer_y, factor_own, peer_term):
    peer_y_peer = split(peer_y[...])
    total = mate_terms[M_OWN] + products((split(peer_part(strips)), peer_y_peer))
    rows = lax.broadcasted_iota(jnp.int32, total.shape, 0)
    cols = lax.broadcasted_iota(jnp.int32, total.shape, 1)
    factor = jnp.where(rows == cols, 1.5, 0.0) + filtered(kept, total, OWN, -0.5)
    factor_own[...] = factor
    term = products((peer_y_peer, split(factor)))
    peer_term[...] = filtered(kept, term, 0, None, KEPT_PEER_AT, ROWS)


Y_MATE, Z_MATE, Z_SIDE = range(3)
Y_OWN_PART, Y_SIDE_PART, Z_OWN_PART, Z_PEER_PART, PEER_PART = range(5)
Y_PEER, Y_OWN, Y_SIDE, PEER_Y, Z_PEER = range(5)


def middle_kernel(
    kept, y_peer, strips, mate, y_side, z_side, mate_terms,
    peer_y, from_side, factor_own, mate_factor,
    finished, partial, ready,
):
    def keep(at, parts):
        ready[at, 0], ready[at, 1] = parts

    y_to_mate, y_own, z_to_mate, z_own = (split(mate[at]) for at in range(4))
    y_to_peer, z_to_peer = split(y_peer[...]), split(peer_part(strips))
    y_to_side, z_to_side = split(y_side[...]), split(z_side[...])
    f_own = split(factor_own[...])
    keep(Y_OWN, y_own)
    keep(Y_SIDE, y_to_side)
    keep(Y_PEER, y_to_peer)
    keep(Z_PEER, z_to_peer)
    keep(PEER_Y, split(peer_y[...]))

    total = products((z_own, y_to_side), (z_to_side, split(from_side[0])))
    f_side = split(filtered(kept, total, SIDE, -0.5))
    partial[PEER_PART] = products((z_own, y_to_peer))
    partial[Y_SIDE_PART] = products((y_own, f_side))
    partial[Y_OWN_PART] = mate_terms[M_Y_OWN] + products((y_own, f_own))
    partial[Z_PEER_PART] = products((f_own, z_to_peer))
    partial[Z_OWN_PART] = mate_terms[M_Z_OWN] + products((f_own, z_own))
    value = mate_terms[M_Y_MATE] + products((y_to_mate, split(mate_factor[...])))
    finished[Y_MATE] = filtered(kept, value, MATE)
    value = mate_terms[M_Z_MATE] + products((f_own, z_to_mate))
    finished[Z_MATE] = filtered(kept, value, MATE)
    value = products((f_own, z_to_side), (f_side, split(from_side[1])))
    finished[Z_SIDE] = filtered(kept, value, SIDE)


class Writer:
    def __init__(self, slots, kept, result, sems):
        self.slots, self.kept, self.result, self.sems = slots, kept, result, sems
        self.started = []
        self.held = 0

    def write(self, source, out, region):
        size = out.shape[1]
        for i in range(ROWS):
            for j in range(ROWS):
                rows, cols = quarter(i, j, size)
                slot = self.slots[i * SLOTS + region * ROWS + j, 0]
                copy = pltpu.make_async_copy(
                    source.at[rows, cols],
                    out.at[i, :, pl.ds(pl.multiple_of(slot * size, size), size)],
                    self.sems.at[len(self.started)],
                )
                copy.start()
                self.started.append(copy)

    def finish(self, value, out, region):
        place = self.result.at[self.held]
        self.held += 1
        place[...] = filtered(self.kept, value, region)
        self.write(place, out, region)

    def wait(self):
        for copy in self.started:
            copy.wait()


def peer_kernel(
    slots, kept, finished, partial, ready, from_peer, peer_spread,
    sqrt_next, inverse_next, y_peer_part, result, sems,
):
    def held(at):
        return ready[at, 0], ready[at, 1]

    writer = Writer(slots, kept, result, sems)
    writer.write(finished.at[Y_MATE], sqrt_next, MATE)
    writer.write(finished.at[Z_MATE], inverse_next, MATE)
    writer.write(finished.at[Z_SIDE], inverse_next, SIDE)
    peer_y_own = split(own_part(from_peer[Y_BESIDE], peer_spread[0]))
    peer_z_own = split(own_part(from_peer[Z_BESIDE], peer_spread[1]))
    peer_z_peer = split(peer_part(from_peer))
    total = partial[PEER_PART] + products((held(Z_PEER), peer_y_own))
    f_peer = split(filtered(kept, total, PEER, -0.5))
    total = products((peer_z_own, held(PEER_Y)), (peer_z_peer, held(Y_OWN)))
    peer_f_peer = split(filtered(kept, total, 0, -0.5, KEPT_PEER_AT, ROWS))
    value = partial[Z_PEER_PART] + products((f_peer, peer_z_own))
    writer.finish(value, inverse_next, PEER)
    value = partial[Z_OWN_PART] + products((f_peer, peer_z_peer))
    writer.finish(value, inverse_next, OWN)
    value = partial[Y_OWN_PART] + products((held(Y_PEER), peer_f_peer))
    writer.finish(value, sqrt_next, OWN)
    y_peer_part[...] = filtered(kept, products((held(Y_OWN), f_peer)), PEER)
    writer.wait()


def side_kernel(slots, kept, partial, ready, factor, unfinished, sqrt_next, result, sems):
    left = (ready[Y_SIDE, 0], ready[Y_SIDE, 1])
    value = partial[Y_SIDE_PART] + products((left, split(factor[...])))
    writer = Writer(slots, kept, result, sems)
    writer.finish(value, sqrt_next, SIDE)
    writer.wait()


def last_kernel(slots, part, term, unfinished, sqrt_next, result, sems):
    size = sqrt_next.shape[1]
    copies = []
    blocks = [(i, j) for i in range(ROWS) for j in range(ROWS)]
    starts = [slots[i * SLOTS + PEER * ROWS + j, 0] * size for i, j in blocks]
    for at, (i, j) in enumerate(blocks):
        rows, cols = quarter(i, j, size)
        result[at] = part[rows, cols] + term[rows, cols]
        out = sqrt_next.at[i, :, pl.ds(pl.multiple_of(starts[at], size), size)]
        copies.append(pltpu.make_async_copy(result.at[at], out, sems.at[at]))
        copies[at].start()
    for copy in copies:
        copy.wait()


def call(
    kernel, outs, operands, micros=0, scratch=(), hbm_in=(), any_in=(), hbm_out=(), in_place=None
):
    def spec(space=pltpu.VMEM):
        return pl.BlockSpec(memory_space=space)

    operands = [
        pltpu.with_memory_space_constraint(array, pltpu.HBM) if at in hbm_in else array
        for at, array in enumerate(operands)
    ]
    return pl.pallas_call(
        kernel,
        out_shape=outs,
        in_specs=[
            spec(pltpu.HBM if at in hbm_in else pl.ANY if at in any_in else pltpu.VMEM)
            for at in range(len(operands))
        ],
        out_specs=tuple(
            spec(pltpu.HBM if at in hbm_out else pltpu.VMEM) for at in range(len(outs))
        ),
        scratch_shapes=scratch,
        input_output_aliases={} if in_place is None else {in_place: 0},
        compiler_params=pltpu.CompilerParams(vmem_limit_bytes=VMEM_LIMIT),
        cost_estimate=pl.CostEstimate(
            flops=int(micros * PEAK), bytes_accessed=0, transcendentals=0
        ),
    )(*operands)


def local(sqrt_iterate, inverse_iterate, pattern, keep_mask, row_order):
    rows_dev, block, width = sqrt_iterate.shape
    row_devices, col_devices = lax.axis_size("row"), lax.axis_size("col")
    assert rows_dev == ROWS and width == SLOTS * block and pattern.shape[1] == SLOTS
    assert row_devices > 3 and row_devices % 2 == 0 and col_devices > 2
    size = ROWS * block

    def to_mate(value):
        return lax.ppermute(value, "row", [(i, i ^ 1) for i in range(row_devices)])

    def to_peer(value):
        route = [(i, (i + (1 if i % 2 else -1)) % row_devices) for i in range(row_devices)]
        return lax.ppermute(value, "row", route)

    def to_side(value):
        route = [((i + 1) % col_devices, i) for i in range(col_devices)]
        return lax.ppermute(value, "col", route)

    def shape(*dims, dtype=jnp.float32):
        return jax.ShapeDtypeStruct(dims, dtype)

    one, pair = shape(size, size), shape(2, size, size)
    (diagonal,) = call(
        diagonal_kernel,
        (shape(2 * ROWS, block, block),),
        (sqrt_iterate, inverse_iterate),
        scratch=[pltpu.SemaphoreType.DMA((2,))],
        hbm_in=range(2),
    )
    peer_diagonal = to_peer(diagonal)
    slots, kept, y_peer, strips, mate, y_side, z_side, own_pair = call(
        functools.partial(pack_kernel, row_devices, col_devices),
        (
            shape(ROWS * SLOTS, block, dtype=jnp.int32), shape(KEPT_LINES, block),
            one, shape(ROWS + 2, block, size), shape(4, size, size), one, one, pair,
        ),
        (pattern.T, keep_mask.T, row_order, sqrt_iterate, inverse_iterate, diagonal),
        scratch=[
            pltpu.SMEM(pattern.T.shape, jnp.int32),
            pltpu.SMEM(keep_mask.T.shape, jnp.int32),
            pltpu.SMEM(row_order.shape, jnp.int32),
            pltpu.VMEM(sqrt_iterate.shape, jnp.float32),
            pltpu.VMEM(inverse_iterate.shape, jnp.float32),
            pltpu.SemaphoreType.DMA((5,)),
        ],
        hbm_in=range(5),
        any_in=(5,),
    )
    peer_y = to_peer(y_peer)
    from_peer = to_peer(strips)
    from_mate = to_mate(mate)
    from_side = to_side(own_pair)
    (peer_spread,) = call(spread_kernel, (pair,), (peer_diagonal,), micros=10)
    (mate_terms,) = call(
        mate_kernel,
        (shape(5, size, size),),
        (kept, mate, from_mate, peer_spread),
        any_in=(3,),
    )
    factor_own, peer_term = call(
        factor_own_kernel, (one, one), (kept, mate_terms, strips, peer_y), micros=5
    )
    mate_factor = to_mate(factor_own)
    term = to_peer(peer_term)
    side_factor = to_side(factor_own)
    finished, partial, ready = call(
        middle_kernel,
        (
            shape(3, size, size), shape(5, size, size),
            shape(5, 2, size, size, dtype=jnp.bfloat16),
        ),
        (
            kept, y_peer, strips, mate, y_side, z_side, mate_terms,
            peer_y, from_side, factor_own, mate_factor,
        ),
    )
    output = shape(rows_dev, block, width)

    def writing(blocks):
        return [
            pltpu.VMEM((blocks, size, size), jnp.float32),
            pltpu.SemaphoreType.DMA((24,)),
        ]

    sqrt_next, inverse_next, y_peer_part = call(
        peer_kernel,
        (output, output, one),
        (slots, kept, finished, partial, ready, from_peer, peer_spread),
        scratch=writing(3),
        hbm_out=(0, 1),
    )
    (sqrt_next,) = call(
        side_kernel,
        (output,),
        (slots, kept, partial, ready, side_factor, sqrt_next),
        scratch=writing(1),
        hbm_in=(5,),
        hbm_out=(0,),
        in_place=5,
    )
    (sqrt_next,) = call(
        last_kernel,
        (output,),
        (slots, y_peer_part, term, sqrt_next),
        scratch=[
            pltpu.VMEM((ROWS * ROWS, block, block), jnp.float32),
            pltpu.SemaphoreType.DMA((ROWS * ROWS,)),
        ],
        hbm_in=(3,),
        hbm_out=(0,),
        in_place=3,
    )
    return sqrt_next, inverse_next


def solution(mesh):
    rows = P(("row", "col"), None, None)
    return jax.shard_map(
        local,
        mesh=mesh,
        in_specs=(rows, rows, P(), P(), P()),
        out_specs=(rows, rows),
        check_vma=False,
    )
```

```python
import functools

import jax
import jax.numpy as jnp
from jax import lax
from jax.experimental import pallas as pl
from jax.experimental.pallas import tpu as pltpu
from jax.sharding import PartitionSpec as P

PEER, OWN, MATE, SIDE = range(4)
ROWS = 2
SLOTS = 8
KEPT_PEER_AT, KEPT_MATE_AT, KEPT_LINES = 16, 20, 24
MATE_SLOT_AT, SLOT_LINES = 16, 24
LARGEST = float(jnp.finfo(jnp.bfloat16).max)
VMEM_LIMIT = 24 * 2**20
PEAK = 1.153e9


def split(value):
    clipped = jnp.clip(value, -LARGEST, LARGEST)
    high = clipped.astype(jnp.bfloat16)
    low = (value - high.astype(jnp.float32)).astype(jnp.bfloat16)
    return high, low


def products(*pairs):
    left = [part for (high, low), _ in pairs for part in (high, low, high)]
    right = [part for _, (high, low) in pairs for part in (high, high, low)]
    return jnp.dot(
        jnp.concatenate(left, axis=1),
        jnp.concatenate(right, axis=0),
        preferred_element_type=jnp.float32,
    )


def filtered(kept, value, region, scale=None, base=0, width=SLOTS):
    size = value.shape[0] // ROWS
    rows = []
    for i in range(ROWS):
        row = []
        for j in range(ROWS):
            at = base + i * width + region * ROWS + j
            flag = kept[at:at + 1, :]
            if scale is not None:
                flag = flag * scale
            row.append(value[i * size:(i + 1) * size, j * size:(j + 1) * size] * flag)
        rows.append(jnp.concatenate(row, axis=1))
    return jnp.concatenate(rows, axis=0)


def neighbours(row_devices, col_devices, order):
    row = lax.axis_index("row")
    col = lax.axis_index("col")
    odd = lax.rem(row, 2)

    def first(row_of, col_of):
        return (lax.rem(row_of, row_devices) * col_devices + lax.rem(col_of, col_devices)) * ROWS

    starts = (
        first(row + row_devices - 1 + 2 * odd, col),
        first(row, col),
        first(row + 1 - 2 * odd, col),
        first(row, col + 1),
    )
    return starts, [order[start + j] for start in starts for j in range(ROWS)]


def find_slots(pattern, stored, wanted):
    slots = [jnp.int32(0)] * len(wanted)
    for k in range(SLOTS):
        label = pattern[k, stored]
        slots = [jnp.where(label == want, k, slot) for want, slot in zip(wanted, slots)]
    return slots


def look_up(row_devices, col_devices, pattern, keep, order, slots, kept):
    starts, labels = neighbours(row_devices, col_devices, order)
    own_labels = labels[OWN * ROWS:(OWN + 1) * ROWS]
    mate_labels = labels[MATE * ROWS:(MATE + 1) * ROWS]

    def write_flags(stored, found, line):
        for j, slot in enumerate(found):
            flag = ((slot == 0) | (keep[slot, stored] == 1)).astype(jnp.float32)
            kept[line + j:line + j + 1, :] = jnp.full((1, kept.shape[1]), flag)

    result = []
    for i in range(ROWS):
        found = find_slots(pattern, starts[OWN] + i, labels)
        result.append(found)
        there = find_slots(pattern, starts[MATE] + i, own_labels + mate_labels)
        for line, slot in (
            *enumerate(found, i * SLOTS), *enumerate(there, MATE_SLOT_AT + i * 2 * ROWS)
        ):
            slots[line:line + 1, :] = jnp.full((1, slots.shape[1]), slot)
        write_flags(starts[OWN] + i, found, i * SLOTS)
        for region, line in ((PEER, KEPT_PEER_AT), (MATE, KEPT_MATE_AT)):
            stored = starts[region] + i
            write_flags(stored, find_slots(pattern, stored, own_labels), line + i * ROWS)
    return result


def quarter(i, j, size):
    return slice(i * size, (i + 1) * size), slice(j * size, (j + 1) * size)


def gather(slot_of, source, places):
    size = source.shape[1]
    for region, region_places in places.items():
        for i in range(ROWS):
            for j in range(ROWS):
                start = pl.multiple_of(slot_of(i, region * ROWS + j) * size, size)
                block = source[i, :, pl.ds(start, size)]
                for place in region_places:
                    place(i, j, size, block)


def into(out):
    def place(i, j, size, block):
        rows, cols = quarter(i, j, size)
        out[rows, cols] = block

    return place


def strip_peer(out):
    def place(i, j, size, block):
        out[i, :, j * size:(j + 1) * size] = block

    return place


def strip_own(out, at):
    def place(i, j, size, block):
        if i != j:
            out[at, :, i * size:(i + 1) * size] = block

    return place


Y_BESIDE, Z_BESIDE = ROWS, ROWS + 1


def peer_part(strips):
    return jnp.concatenate([strips[i] for i in range(ROWS)], axis=0)


def own_part(beside, spread):
    size = beside.shape[0]
    return jnp.concatenate(
        [
            jnp.concatenate([spread[:size, :size], beside[:, :size]], axis=1),
            jnp.concatenate([beside[:, size:], spread[size:, size:]], axis=1),
        ],
        axis=0,
    )


def diagonal_kernel(sqrt_iterate, inverse_iterate, diagonal, sems):
    size = sqrt_iterate.shape[1]
    copies = [
        pltpu.make_async_copy(
            source.at[:, :, pl.ds(0, size)], diagonal.at[pl.ds(at * ROWS, ROWS)], sems.at[at]
        )
        for at, source in enumerate((sqrt_iterate, inverse_iterate))
    ]
    for copy in copies:
        copy.start()
    for copy in copies:
        copy.wait()


def pack_kernel(
    row_devices, col_devices, pattern, keep, order, sqrt_iterate, inverse_iterate, after,
    slots, kept, y_peer, strips, y_mate, z_mate, y_side, z_side, to_side,
    pattern_here, keep_here, order_here, sqrt_here, inverse_here, sems,
):
    copies = [
        pltpu.make_async_copy(source, here, sems.at[at])
        for at, (source, here) in enumerate((
            (order, order_here), (pattern, pattern_here), (keep, keep_here),
            (sqrt_iterate, sqrt_here), (inverse_iterate, inverse_here),
        ))
    ]
    for copy in copies:
        copy.start()
    for copy in copies[:3]:
        copy.wait()
    found = look_up(
        row_devices, col_devices, pattern_here, keep_here, order_here, slots, kept
    )

    def slot_of(i, j):
        return found[i][j]

    copies[3].wait()
    places = {
        PEER: (into(y_peer),),
        OWN: (strip_own(strips, Y_BESIDE), into(y_mate.at[1]), into(to_side.at[0])),
        MATE: (into(y_mate.at[0]),),
        SIDE: (into(y_side),),
    }
    gather(slot_of, sqrt_here, places)
    copies[4].wait()
    places = {
        PEER: (strip_peer(strips),),
        OWN: (strip_own(strips, Z_BESIDE), into(z_mate.at[1]), into(to_side.at[1])),
        MATE: (into(z_mate.at[0]),),
        SIDE: (into(z_side),),
    }
    gather(slot_of, inverse_here, places)


def unpack_kernel(slots, whole, mate_y):
    size = whole.shape[1]
    for at in range(2):
        for i in range(ROWS):
            for j in range(ROWS):
                slot = slots[MATE_SLOT_AT + (i * 2 + at) * ROWS + j, 0]
                rows, cols = quarter(i, j, size)
                start = pl.multiple_of(slot * size, size)
                mate_y[at, rows, cols] = whole[i, :, pl.ds(start, size)]


def spread_kernel(diagonal, after, spread):
    size = diagonal.shape[1]
    for at in range(2):
        for i in range(ROWS):
            for j in range(ROWS):
                rows, cols = quarter(i, j, size)
                block = diagonal[at * ROWS + i]
                spread[at, rows, cols] = block if i == j else jnp.zeros_like(block)


M_OWN, M_Y_OWN, M_Y_MATE, M_Z_OWN, M_Z_MATE = range(5)


def mate_kernel(kept, y_mate, z_mate, mate_y, mate_z, after, mate_terms):
    y_to_mate, y_own = split(y_mate[0]), split(y_mate[1])
    z_to_mate, z_own = split(z_mate[0]), split(z_mate[1])
    mate_y_mate, mate_y_own = split(mate_y[0]), split(mate_y[1])
    mate_z_mate, mate_z_own = split(mate_z[0]), split(mate_z[1])
    mate_terms[M_OWN] = products((z_own, y_own), (z_to_mate, mate_y_mate))
    total = products((z_own, y_to_mate), (z_to_mate, mate_y_own))
    f_mate = split(filtered(kept, total, MATE, -0.5))
    total = products((mate_z_own, mate_y_mate), (mate_z_mate, y_own))
    mate_f_mate = split(filtered(kept, total, 0, -0.5, KEPT_MATE_AT, ROWS))
    mate_terms[M_Y_OWN] = products((y_to_mate, mate_f_mate))
    mate_terms[M_Y_MATE] = products((y_own, f_mate))
    mate_terms[M_Z_OWN] = products((f_mate, mate_z_mate))
    mate_terms[M_Z_MATE] = products((f_mate, mate_z_own))


def factor_own_kernel(kept, mate_terms, strips, peer_y, factor_own, peer_term):
    peer_y_peer = split(peer_y[...])
    total = mate_terms[M_OWN] + products((split(peer_part(strips)), peer_y_peer))
    rows = lax.broadcasted_iota(jnp.int32, total.shape, 0)
    cols = lax.broadcasted_iota(jnp.int32, total.shape, 1)
    factor = jnp.where(rows == cols, 1.5, 0.0) + filtered(kept, total, OWN, -0.5)
    factor_own[...] = factor
    term = products((peer_y_peer, split(factor)))
    peer_term[...] = filtered(kept, term, 0, None, KEPT_PEER_AT, ROWS)


Y_MATE, Z_MATE, Z_SIDE = range(3)
Y_OWN_PART, Y_SIDE_PART, Z_OWN_PART, Z_PEER_PART, PEER_PART = range(5)
Y_PEER, Y_OWN, Y_SIDE, PEER_Y, Z_PEER = range(5)


def middle_kernel(
    kept, y_peer, strips, y_mate, z_mate, y_side, z_side, mate_terms,
    peer_y, from_side, factor_own, mate_factor,
    finished, partial, ready,
):
    def keep(at, parts):
        ready[at, 0], ready[at, 1] = parts

    y_to_mate, y_own = split(y_mate[0]), split(y_mate[1])
    z_to_mate, z_own = split(z_mate[0]), split(z_mate[1])
    y_to_peer, z_to_peer = split(y_peer[...]), split(peer_part(strips))
    y_to_side, z_to_side = split(y_side[...]), split(z_side[...])
    f_own = split(factor_own[...])
    keep(Y_OWN, y_own)
    keep(Y_SIDE, y_to_side)
    keep(Y_PEER, y_to_peer)
    keep(Z_PEER, z_to_peer)
    keep(PEER_Y, split(peer_y[...]))

    total = products((z_own, y_to_side), (z_to_side, split(from_side[0])))
    f_side = split(filtered(kept, total, SIDE, -0.5))
    partial[PEER_PART] = products((z_own, y_to_peer))
    partial[Y_SIDE_PART] = products((y_own, f_side))
    partial[Y_OWN_PART] = mate_terms[M_Y_OWN] + products((y_own, f_own))
    partial[Z_PEER_PART] = products((f_own, z_to_peer))
    partial[Z_OWN_PART] = mate_terms[M_Z_OWN] + products((f_own, z_own))
    value = mate_terms[M_Y_MATE] + products((y_to_mate, split(mate_factor[...])))
    finished[Y_MATE] = filtered(kept, value, MATE)
    value = mate_terms[M_Z_MATE] + products((f_own, z_to_mate))
    finished[Z_MATE] = filtered(kept, value, MATE)
    value = products((f_own, z_to_side), (f_side, split(from_side[1])))
    finished[Z_SIDE] = filtered(kept, value, SIDE)


class Writer:
    def __init__(self, slots, kept, result, sems):
        self.slots, self.kept, self.result, self.sems = slots, kept, result, sems
        self.started = []
        self.held = 0

    def write(self, source, out, region):
        size = out.shape[1]
        for i in range(ROWS):
            for j in range(ROWS):
                rows, cols = quarter(i, j, size)
                slot = self.slots[i * SLOTS + region * ROWS + j, 0]
                copy = pltpu.make_async_copy(
                    source.at[rows, cols],
                    out.at[i, :, pl.ds(pl.multiple_of(slot * size, size), size)],
                    self.sems.at[len(self.started)],
                )
                copy.start()
                self.started.append(copy)

    def finish(self, value, out, region):
        place = self.result.at[self.held]
        self.held += 1
        place[...] = filtered(self.kept, value, region)
        self.write(place, out, region)

    def wait(self):
        for copy in self.started:
            copy.wait()


def peer_kernel(
    slots, kept, finished, partial, ready, from_peer, peer_spread,
    sqrt_next, inverse_next, y_peer_part, result, sems,
):
    def held(at):
        return ready[at, 0], ready[at, 1]

    writer = Writer(slots, kept, result, sems)
    writer.write(finished.at[Y_MATE], sqrt_next, MATE)
    writer.write(finished.at[Z_MATE], inverse_next, MATE)
    writer.write(finished.at[Z_SIDE], inverse_next, SIDE)
    peer_y_own = split(own_part(from_peer[Y_BESIDE], peer_spread[0]))
    peer_z_own = split(own_part(from_peer[Z_BESIDE], peer_spread[1]))
    peer_z_peer = split(peer_part(from_peer))
    total = partial[PEER_PART] + products((held(Z_PEER), peer_y_own))
    f_peer = split(filtered(kept, total, PEER, -0.5))
    total = products((peer_z_own, held(PEER_Y)), (peer_z_peer, held(Y_OWN)))
    peer_f_peer = split(filtered(kept, total, 0, -0.5, KEPT_PEER_AT, ROWS))
    value = partial[Z_PEER_PART] + products((f_peer, peer_z_own))
    writer.finish(value, inverse_next, PEER)
    value = partial[Z_OWN_PART] + products((f_peer, peer_z_peer))
    writer.finish(value, inverse_next, OWN)
    value = partial[Y_OWN_PART] + products((held(Y_PEER), peer_f_peer))
    writer.finish(value, sqrt_next, OWN)
    y_peer_part[...] = filtered(kept, products((held(Y_OWN), f_peer)), PEER)
    writer.wait()


def side_kernel(slots, kept, partial, ready, factor, unfinished, sqrt_next, result, sems):
    left = (ready[Y_SIDE, 0], ready[Y_SIDE, 1])
    value = partial[Y_SIDE_PART] + products((left, split(factor[...])))
    writer = Writer(slots, kept, result, sems)
    writer.finish(value, sqrt_next, SIDE)
    writer.wait()


def last_kernel(slots, part, term, unfinished, sqrt_next, result, sems):
    size = sqrt_next.shape[1]
    copies = []
    blocks = [(i, j) for i in range(ROWS) for j in range(ROWS)]
    starts = [slots[i * SLOTS + PEER * ROWS + j, 0] * size for i, j in blocks]
    for at, (i, j) in enumerate(blocks):
        rows, cols = quarter(i, j, size)
        result[at] = part[rows, cols] + term[rows, cols]
        out = sqrt_next.at[i, :, pl.ds(pl.multiple_of(starts[at], size), size)]
        copies.append(pltpu.make_async_copy(result.at[at], out, sems.at[at]))
        copies[at].start()
    for copy in copies:
        copy.wait()


def call(
    kernel, outs, operands, micros=0, scratch=(), hbm_in=(), any_in=(), hbm_out=(), in_place=None
):
    def spec(space=pltpu.VMEM):
        return pl.BlockSpec(memory_space=space)

    operands = [
        pltpu.with_memory_space_constraint(array, pltpu.HBM) if at in hbm_in else array
        for at, array in enumerate(operands)
    ]
    return pl.pallas_call(
        kernel,
        out_shape=outs,
        in_specs=[
            spec(pltpu.HBM if at in hbm_in else pl.ANY if at in any_in else pltpu.VMEM)
            for at in range(len(operands))
        ],
        out_specs=tuple(
            spec(pltpu.HBM if at in hbm_out else pltpu.VMEM) for at in range(len(outs))
        ),
        scratch_shapes=scratch,
        input_output_aliases={} if in_place is None else {in_place: 0},
        compiler_params=pltpu.CompilerParams(vmem_limit_bytes=VMEM_LIMIT),
        cost_estimate=pl.CostEstimate(
            flops=int(micros * PEAK), bytes_accessed=0, transcendentals=0
        ),
    )(*operands)


def local(sqrt_iterate, inverse_iterate, pattern, keep_mask, row_order):
    rows_dev, block, width = sqrt_iterate.shape
    row_devices, col_devices = lax.axis_size("row"), lax.axis_size("col")
    assert rows_dev == ROWS and width == SLOTS * block and pattern.shape[1] == SLOTS
    assert row_devices > 3 and row_devices % 2 == 0 and col_devices > 2
    size = ROWS * block

    def to_mate(value):
        return lax.ppermute(value, "row", [(i, i ^ 1) for i in range(row_devices)])

    def to_peer(value):
        route = [(i, (i + (1 if i % 2 else -1)) % row_devices) for i in range(row_devices)]
        return lax.ppermute(value, "row", route)

    def to_side(value):
        route = [((i + 1) % col_devices, i) for i in range(col_devices)]
        return lax.ppermute(value, "col", route)

    def shape(*dims, dtype=jnp.float32):
        return jax.ShapeDtypeStruct(dims, dtype)

    one, pair = shape(size, size), shape(2, size, size)
    whole = to_mate(sqrt_iterate)
    (diagonal,) = call(
        diagonal_kernel,
        (shape(2 * ROWS, block, block),),
        (sqrt_iterate, inverse_iterate),
        scratch=[pltpu.SemaphoreType.DMA((2,))],
        hbm_in=range(2),
    )
    peer_diagonal = to_peer(diagonal)
    slots, kept, y_peer, strips, y_mate, z_mate, y_side, z_side, own_pair = call(
        functools.partial(pack_kernel, row_devices, col_devices),
        (
            shape(SLOT_LINES, block, dtype=jnp.int32), shape(KEPT_LINES, block),
            one, shape(ROWS + 2, block, size), pair, pair, one, one, pair,
        ),
        (pattern.T, keep_mask.T, row_order, sqrt_iterate, inverse_iterate, diagonal),
        scratch=[
            pltpu.SMEM(pattern.T.shape, jnp.int32),
            pltpu.SMEM(keep_mask.T.shape, jnp.int32),
            pltpu.SMEM(row_order.shape, jnp.int32),
            pltpu.VMEM(sqrt_iterate.shape, jnp.float32),
            pltpu.VMEM(inverse_iterate.shape, jnp.float32),
            pltpu.SemaphoreType.DMA((5,)),
        ],
        hbm_in=range(5),
        any_in=(5,),
    )
    peer_y = to_peer(y_peer)
    from_peer = to_peer(strips)
    mate_z = to_mate(z_mate)
    from_side = to_side(own_pair)
    (mate_y,) = call(unpack_kernel, (pair,), (slots, whole), micros=5)
    (peer_spread,) = call(
        spread_kernel, (pair,), (peer_diagonal, mate_y), any_in=(1,), micros=10
    )
    (mate_terms,) = call(
        mate_kernel,
        (shape(5, size, size),),
        (kept, y_mate, z_mate, mate_y, mate_z, peer_spread),
        any_in=(5,),
    )
    factor_own, peer_term = call(
        factor_own_kernel, (one, one), (kept, mate_terms, strips, peer_y), micros=5
    )
    mate_factor = to_mate(factor_own)
    term = to_peer(peer_term)
    side_factor = to_side(factor_own)
    finished, partial, ready = call(
        middle_kernel,
        (
            shape(3, size, size), shape(5, size, size),
            shape(5, 2, size, size, dtype=jnp.bfloat16),
        ),
        (
            kept, y_peer, strips, y_mate, z_mate, y_side, z_side, mate_terms,
            peer_y, from_side, factor_own, mate_factor,
        ),
    )
    output = shape(rows_dev, block, width)

    def writing(blocks):
        return [
            pltpu.VMEM((blocks, size, size), jnp.float32),
            pltpu.SemaphoreType.DMA((24,)),
        ]

    sqrt_next, inverse_next, y_peer_part = call(
        peer_kernel,
        (output, output, one),
        (slots, kept, finished, partial, ready, from_peer, peer_spread),
        scratch=writing(3),
        hbm_out=(0, 1),
    )
    (sqrt_next,) = call(
        side_kernel,
        (output,),
        (slots, kept, partial, ready, side_factor, sqrt_next),
        scratch=writing(1),
        hbm_in=(5,),
        hbm_out=(0,),
        in_place=5,
    )
    (sqrt_next,) = call(
        last_kernel,
        (output,),
        (slots, y_peer_part, term, sqrt_next),
        scratch=[
            pltpu.VMEM((ROWS * ROWS, block, block), jnp.float32),
            pltpu.SemaphoreType.DMA((ROWS * ROWS,)),
        ],
        hbm_in=(3,),
        hbm_out=(0,),
        in_place=3,
    )
    return sqrt_next, inverse_next


def solution(mesh):
    rows = P(("row", "col"), None, None)
    return jax.shard_map(
        local,
        mesh=mesh,
        in_specs=(rows, rows, P(), P(), P()),
        out_specs=(rows, rows),
        check_vma=False,
    )
```

```python
import functools

import jax
import jax.numpy as jnp
from jax import lax
from jax.experimental import pallas as pl
from jax.experimental.pallas import tpu as pltpu
from jax.sharding import PartitionSpec as P

PEER, OWN, MATE, SIDE = range(4)
ROWS = 2
SLOTS = 8
KEPT_PEER_AT, KEPT_MATE_AT, KEPT_LINES = 16, 20, 24
LARGEST = float(jnp.finfo(jnp.bfloat16).max)
VMEM_LIMIT = 24 * 2**20
PEAK = 1.153e9


def split(value):
    clipped = jnp.clip(value, -LARGEST, LARGEST)
    high = clipped.astype(jnp.bfloat16)
    low = (value - high.astype(jnp.float32)).astype(jnp.bfloat16)
    return high, low


def products(*pairs):
    left = [part for (high, low), _ in pairs for part in (high, low, high)]
    right = [part for _, (high, low) in pairs for part in (high, high, low)]
    return jnp.dot(
        jnp.concatenate(left, axis=1),
        jnp.concatenate(right, axis=0),
        preferred_element_type=jnp.float32,
    )


def filtered(kept, value, region, scale=None, base=0, width=SLOTS):
    size = value.shape[0] // ROWS
    rows = []
    for i in range(ROWS):
        row = []
        for j in range(ROWS):
            at = base + i * width + region * ROWS + j
            flag = kept[at:at + 1, :]
            if scale is not None:
                flag = flag * scale
            row.append(value[i * size:(i + 1) * size, j * size:(j + 1) * size] * flag)
        rows.append(jnp.concatenate(row, axis=1))
    return jnp.concatenate(rows, axis=0)


def neighbours(row_devices, col_devices, order):
    row = lax.axis_index("row")
    col = lax.axis_index("col")
    odd = lax.rem(row, 2)

    def first(row_of, col_of):
        return (lax.rem(row_of, row_devices) * col_devices + lax.rem(col_of, col_devices)) * ROWS

    starts = (
        first(row + row_devices - 1 + 2 * odd, col),
        first(row, col),
        first(row + 1 - 2 * odd, col),
        first(row, col + 1),
    )
    return starts, [order[start + j] for start in starts for j in range(ROWS)]


def find_slots(pattern, stored, wanted):
    slots = [jnp.int32(0)] * len(wanted)
    for k in range(SLOTS):
        label = pattern[k, stored]
        slots = [jnp.where(label == want, k, slot) for want, slot in zip(wanted, slots)]
    return slots


def look_up(row_devices, col_devices, pattern, keep, order, slots, kept):
    starts, labels = neighbours(row_devices, col_devices, order)
    own_labels = labels[OWN * ROWS:(OWN + 1) * ROWS]

    def write_flags(stored, found, line):
        for j, slot in enumerate(found):
            flag = ((slot == 0) | (keep[slot, stored] == 1)).astype(jnp.float32)
            kept[line + j:line + j + 1, :] = jnp.full((1, kept.shape[1]), flag)

    result = []
    for i in range(ROWS):
        found = find_slots(pattern, starts[OWN] + i, labels)
        result.append(found)
        for j, slot in enumerate(found):
            line = i * SLOTS + j
            slots[line:line + 1, :] = jnp.full((1, slots.shape[1]), slot)
        write_flags(starts[OWN] + i, found, i * SLOTS)
        for region, line in ((PEER, KEPT_PEER_AT), (MATE, KEPT_MATE_AT)):
            stored = starts[region] + i
            write_flags(stored, find_slots(pattern, stored, own_labels), line + i * ROWS)
    return result


def quarter(i, j, size):
    return slice(i * size, (i + 1) * size), slice(j * size, (j + 1) * size)


def gather(slot_of, source, places):
    size = source.shape[1]
    for region, region_places in places.items():
        for i in range(ROWS):
            for j in range(ROWS):
                start = pl.multiple_of(slot_of(i, region * ROWS + j) * size, size)
                block = source[i, :, pl.ds(start, size)]
                for place in region_places:
                    place(i, j, size, block)


def into(out):
    def place(i, j, size, block):
        rows, cols = quarter(i, j, size)
        out[rows, cols] = block

    return place


def strip_peer(out):
    def place(i, j, size, block):
        out[i, :, j * size:(j + 1) * size] = block

    return place


def strip_own(out, at):
    def place(i, j, size, block):
        if i != j:
            out[at, :, i * size:(i + 1) * size] = block

    return place


Y_BESIDE, Z_BESIDE = ROWS, ROWS + 1


def peer_part(strips):
    return jnp.concatenate([strips[i] for i in range(ROWS)], axis=0)


def own_part(beside, spread):
    size = beside.shape[0]
    return jnp.concatenate(
        [
            jnp.concatenate([spread[:size, :size], beside[:, :size]], axis=1),
            jnp.concatenate([beside[:, size:], spread[size:, size:]], axis=1),
        ],
        axis=0,
    )


def diagonal_kernel(sqrt_iterate, inverse_iterate, diagonal, sems):
    size = sqrt_iterate.shape[1]
    copies = [
        pltpu.make_async_copy(
            source.at[:, :, pl.ds(0, size)], diagonal.at[pl.ds(at * ROWS, ROWS)], sems.at[at]
        )
        for at, source in enumerate((sqrt_iterate, inverse_iterate))
    ]
    for copy in copies:
        copy.start()
    for copy in copies:
        copy.wait()


def pack_kernel(
    row_devices, col_devices, pattern, keep, order, sqrt_iterate, inverse_iterate, after,
    slots, kept, y_peer, strips, mate, y_side, z_side, to_side,
    pattern_here, keep_here, order_here, sems,
):
    copies = [
        pltpu.make_async_copy(source, here, sems.at[at])
        for at, (source, here) in enumerate((
            (order, order_here), (pattern, pattern_here), (keep, keep_here),
        ))
    ]
    for copy in copies:
        copy.start()
    for copy in copies:
        copy.wait()
    found = look_up(
        row_devices, col_devices, pattern_here, keep_here, order_here, slots, kept
    )

    def slot_of(i, j):
        return found[i][j]

    places = {
        PEER: (into(y_peer),),
        OWN: (strip_own(strips, Y_BESIDE), into(mate.at[1]), into(to_side.at[0])),
        MATE: (into(mate.at[0]),),
        SIDE: (into(y_side),),
    }
    gather(slot_of, sqrt_iterate, places)
    places = {
        PEER: (strip_peer(strips),),
        OWN: (strip_own(strips, Z_BESIDE), into(mate.at[3]), into(to_side.at[1])),
        MATE: (into(mate.at[2]),),
        SIDE: (into(z_side),),
    }
    gather(slot_of, inverse_iterate, places)


def spread_kernel(diagonal, spread):
    size = diagonal.shape[1]
    for at in range(2):
        for i in range(ROWS):
            for j in range(ROWS):
                rows, cols = quarter(i, j, size)
                block = diagonal[at * ROWS + i]
                spread[at, rows, cols] = block if i == j else jnp.zeros_like(block)


M_OWN, M_Y_OWN, M_Y_MATE, M_Z_OWN, M_Z_MATE = range(5)


def mate_kernel(kept, mate, from_mate, after, mate_terms):
    y_to_mate, y_own, z_to_mate, z_own = (split(mate[at]) for at in range(4))
    mate_y_mate, mate_y_own, mate_z_mate, mate_z_own = (split(from_mate[at]) for at in range(4))
    mate_terms[M_OWN] = products((z_own, y_own), (z_to_mate, mate_y_mate))
    total = products((z_own, y_to_mate), (z_to_mate, mate_y_own))
    f_mate = split(filtered(kept, total, MATE, -0.5))
    total = products((mate_z_own, mate_y_mate), (mate_z_mate, y_own))
    mate_f_mate = split(filtered(kept, total, 0, -0.5, KEPT_MATE_AT, ROWS))
    mate_terms[M_Y_OWN] = products((y_to_mate, mate_f_mate))
    mate_terms[M_Y_MATE] = products((y_own, f_mate))
    mate_terms[M_Z_OWN] = products((f_mate, mate_z_mate))
    mate_terms[M_Z_MATE] = products((f_mate, mate_z_own))


def factor_own_kernel(kept, mate_terms, strips, peer_y, factor_own, peer_term):
    peer_y_peer = split(peer_y[...])
    total = mate_terms[M_OWN] + products((split(peer_part(strips)), peer_y_peer))
    rows = lax.broadcasted_iota(jnp.int32, total.shape, 0)
    cols = lax.broadcasted_iota(jnp.int32, total.shape, 1)
    factor = jnp.where(rows == cols, 1.5, 0.0) + filtered(kept, total, OWN, -0.5)
    factor_own[...] = factor
    term = products((peer_y_peer, split(factor)))
    peer_term[...] = filtered(kept, term, 0, None, KEPT_PEER_AT, ROWS)


Y_MATE, Z_MATE, Z_SIDE = range(3)
Y_OWN_PART, Y_SIDE_PART, Z_OWN_PART, Z_PEER_PART, PEER_PART = range(5)
Y_PEER, Y_OWN, Y_SIDE, PEER_Y, Z_PEER = range(5)


def middle_kernel(
    kept, y_peer, strips, mate, y_side, z_side, mate_terms,
    peer_y, from_side, factor_own, mate_factor,
    finished, partial, ready,
):
    def keep(at, parts):
        ready[at, 0], ready[at, 1] = parts

    y_to_mate, y_own, z_to_mate, z_own = (split(mate[at]) for at in range(4))
    y_to_peer, z_to_peer = split(y_peer[...]), split(peer_part(strips))
    y_to_side, z_to_side = split(y_side[...]), split(z_side[...])
    f_own = split(factor_own[...])
    keep(Y_OWN, y_own)
    keep(Y_SIDE, y_to_side)
    keep(Y_PEER, y_to_peer)
    keep(Z_PEER, z_to_peer)
    keep(PEER_Y, split(peer_y[...]))

    total = products((z_own, y_to_side), (z_to_side, split(from_side[0])))
    f_side = split(filtered(kept, total, SIDE, -0.5))
    partial[PEER_PART] = products((z_own, y_to_peer))
    partial[Y_SIDE_PART] = products((y_own, f_side))
    partial[Y_OWN_PART] = mate_terms[M_Y_OWN] + products((y_own, f_own))
    partial[Z_PEER_PART] = products((f_own, z_to_peer))
    partial[Z_OWN_PART] = mate_terms[M_Z_OWN] + products((f_own, z_own))
    value = mate_terms[M_Y_MATE] + products((y_to_mate, split(mate_factor[...])))
    finished[Y_MATE] = filtered(kept, value, MATE)
    value = mate_terms[M_Z_MATE] + products((f_own, z_to_mate))
    finished[Z_MATE] = filtered(kept, value, MATE)
    value = products((f_own, z_to_side), (f_side, split(from_side[1])))
    finished[Z_SIDE] = filtered(kept, value, SIDE)


class Writer:
    def __init__(self, slots, kept, result, sems):
        self.slots, self.kept, self.result, self.sems = slots, kept, result, sems
        self.started = []
        self.held = 0

    def write(self, source, out, region):
        size = out.shape[1]
        for i in range(ROWS):
            for j in range(ROWS):
                rows, cols = quarter(i, j, size)
                slot = self.slots[i * SLOTS + region * ROWS + j, 0]
                copy = pltpu.make_async_copy(
                    source.at[rows, cols],
                    out.at[i, :, pl.ds(pl.multiple_of(slot * size, size), size)],
                    self.sems.at[len(self.started)],
                )
                copy.start()
                self.started.append(copy)

    def finish(self, value, out, region):
        place = self.result.at[self.held]
        self.held += 1
        place[...] = filtered(self.kept, value, region)
        self.write(place, out, region)

    def wait(self):
        for copy in self.started:
            copy.wait()


def peer_kernel(
    slots, kept, finished, partial, ready, from_peer, peer_spread,
    sqrt_next, inverse_next, y_peer_part, result, sems,
):
    def held(at):
        return ready[at, 0], ready[at, 1]

    writer = Writer(slots, kept, result, sems)
    writer.write(finished.at[Y_MATE], sqrt_next, MATE)
    writer.write(finished.at[Z_MATE], inverse_next, MATE)
    writer.write(finished.at[Z_SIDE], inverse_next, SIDE)
    peer_y_own = split(own_part(from_peer[Y_BESIDE], peer_spread[0]))
    peer_z_own = split(own_part(from_peer[Z_BESIDE], peer_spread[1]))
    peer_z_peer = split(peer_part(from_peer))
    total = partial[PEER_PART] + products((held(Z_PEER), peer_y_own))
    f_peer = split(filtered(kept, total, PEER, -0.5))
    total = products((peer_z_own, held(PEER_Y)), (peer_z_peer, held(Y_OWN)))
    peer_f_peer = split(filtered(kept, total, 0, -0.5, KEPT_PEER_AT, ROWS))
    value = partial[Z_PEER_PART] + products((f_peer, peer_z_own))
    writer.finish(value, inverse_next, PEER)
    value = partial[Z_OWN_PART] + products((f_peer, peer_z_peer))
    writer.finish(value, inverse_next, OWN)
    value = partial[Y_OWN_PART] + products((held(Y_PEER), peer_f_peer))
    writer.finish(value, sqrt_next, OWN)
    y_peer_part[...] = filtered(kept, products((held(Y_OWN), f_peer)), PEER)
    writer.wait()


def side_kernel(slots, kept, partial, ready, factor, unfinished, sqrt_next, result, sems):
    left = (ready[Y_SIDE, 0], ready[Y_SIDE, 1])
    value = partial[Y_SIDE_PART] + products((left, split(factor[...])))
    writer = Writer(slots, kept, result, sems)
    writer.finish(value, sqrt_next, SIDE)
    writer.wait()


def last_kernel(slots, part, term, unfinished, sqrt_next, result, sems):
    size = sqrt_next.shape[1]
    copies = []
    blocks = [(i, j) for i in range(ROWS) for j in range(ROWS)]
    starts = [slots[i * SLOTS + PEER * ROWS + j, 0] * size for i, j in blocks]
    for at, (i, j) in enumerate(blocks):
        rows, cols = quarter(i, j, size)
        result[at] = part[rows, cols] + term[rows, cols]
        out = sqrt_next.at[i, :, pl.ds(pl.multiple_of(starts[at], size), size)]
        copies.append(pltpu.make_async_copy(result.at[at], out, sems.at[at]))
        copies[at].start()
    for copy in copies:
        copy.wait()


def call(
    kernel, outs, operands, micros=0, scratch=(), hbm_in=(), any_in=(), hbm_out=(), in_place=None
):
    def spec(space=pltpu.VMEM):
        return pl.BlockSpec(memory_space=space)

    operands = [
        pltpu.with_memory_space_constraint(array, pltpu.HBM) if at in hbm_in else array
        for at, array in enumerate(operands)
    ]
    return pl.pallas_call(
        kernel,
        out_shape=outs,
        in_specs=[
            spec(pltpu.HBM if at in hbm_in else pl.ANY if at in any_in else pltpu.VMEM)
            for at in range(len(operands))
        ],
        out_specs=tuple(
            spec(pltpu.HBM if at in hbm_out else pltpu.VMEM) for at in range(len(outs))
        ),
        scratch_shapes=scratch,
        input_output_aliases={} if in_place is None else {in_place: 0},
        compiler_params=pltpu.CompilerParams(vmem_limit_bytes=VMEM_LIMIT),
        cost_estimate=pl.CostEstimate(
            flops=int(micros * PEAK), bytes_accessed=0, transcendentals=0
        ),
    )(*operands)


def local(sqrt_iterate, inverse_iterate, pattern, keep_mask, row_order):
    rows_dev, block, width = sqrt_iterate.shape
    row_devices, col_devices = lax.axis_size("row"), lax.axis_size("col")
    assert rows_dev == ROWS and width == SLOTS * block and pattern.shape[1] == SLOTS
    assert row_devices > 3 and row_devices % 2 == 0 and col_devices > 2
    size = ROWS * block

    def to_mate(value):
        return lax.ppermute(value, "row", [(i, i ^ 1) for i in range(row_devices)])

    def to_peer(value):
        route = [(i, (i + (1 if i % 2 else -1)) % row_devices) for i in range(row_devices)]
        return lax.ppermute(value, "row", route)

    def to_side(value):
        route = [((i + 1) % col_devices, i) for i in range(col_devices)]
        return lax.ppermute(value, "col", route)

    def shape(*dims, dtype=jnp.float32):
        return jax.ShapeDtypeStruct(dims, dtype)

    one, pair = shape(size, size), shape(2, size, size)
    (diagonal,) = call(
        diagonal_kernel,
        (shape(2 * ROWS, block, block),),
        (sqrt_iterate, inverse_iterate),
        scratch=[pltpu.SemaphoreType.DMA((2,))],
        hbm_in=range(2),
    )
    peer_diagonal = to_peer(diagonal)
    slots, kept, y_peer, strips, mate, y_side, z_side, own_pair = call(
        functools.partial(pack_kernel, row_devices, col_devices),
        (
            shape(ROWS * SLOTS, block, dtype=jnp.int32), shape(KEPT_LINES, block),
            one, shape(ROWS + 2, block, size), shape(4, size, size), one, one, pair,
        ),
        (pattern.T, keep_mask.T, row_order, sqrt_iterate, inverse_iterate, diagonal),
        scratch=[
            pltpu.SMEM(pattern.T.shape, jnp.int32),
            pltpu.SMEM(keep_mask.T.shape, jnp.int32),
            pltpu.SMEM(row_order.shape, jnp.int32),
            pltpu.SemaphoreType.DMA((3,)),
        ],
        hbm_in=range(3),
        any_in=(5,),
    )
    peer_y = to_peer(y_peer)
    from_peer = to_peer(strips)
    from_mate = to_mate(mate)
    from_side = to_side(own_pair)
    (peer_spread,) = call(spread_kernel, (pair,), (peer_diagonal,), micros=10)
    (mate_terms,) = call(
        mate_kernel,
        (shape(5, size, size),),
        (kept, mate, from_mate, peer_spread),
        any_in=(3,),
    )
    factor_own, peer_term = call(
        factor_own_kernel, (one, one), (kept, mate_terms, strips, peer_y), micros=5
    )
    mate_factor = to_mate(factor_own)
    term = to_peer(peer_term)
    side_factor = to_side(factor_own)
    finished, partial, ready = call(
        middle_kernel,
        (
            shape(3, size, size), shape(5, size, size),
            shape(5, 2, size, size, dtype=jnp.bfloat16),
        ),
        (
            kept, y_peer, strips, mate, y_side, z_side, mate_terms,
            peer_y, from_side, factor_own, mate_factor,
        ),
    )
    output = shape(rows_dev, block, width)

    def writing(blocks):
        return [
            pltpu.VMEM((blocks, size, size), jnp.float32),
            pltpu.SemaphoreType.DMA((24,)),
        ]

    sqrt_next, inverse_next, y_peer_part = call(
        peer_kernel,
        (output, output, one),
        (slots, kept, finished, partial, ready, from_peer, peer_spread),
        scratch=writing(3),
        hbm_out=(0, 1),
    )
    (sqrt_next,) = call(
        side_kernel,
        (output,),
        (slots, kept, partial, ready, side_factor, sqrt_next),
        scratch=writing(1),
        hbm_in=(5,),
        hbm_out=(0,),
        in_place=5,
    )
    (sqrt_next,) = call(
        last_kernel,
        (output,),
        (slots, y_peer_part, term, sqrt_next),
        scratch=[
            pltpu.VMEM((ROWS * ROWS, block, block), jnp.float32),
            pltpu.SemaphoreType.DMA((ROWS * ROWS,)),
        ],
        hbm_in=(3,),
        hbm_out=(0,),
        in_place=3,
    )
    return sqrt_next, inverse_next


def solution(mesh):
    rows = P(("row", "col"), None, None)
    return jax.shard_map(
        local,
        mesh=mesh,
        in_specs=(rows, rows, P(), P(), P()),
        out_specs=(rows, rows),
        check_vma=False,
    )
```

```python
import functools

import jax
import jax.numpy as jnp
from jax import lax
from jax.experimental import pallas as pl
from jax.experimental.pallas import tpu as pltpu
from jax.sharding import PartitionSpec as P

PEER, OWN, MATE, SIDE = range(4)
ROWS = 2
SLOTS = 8
KEPT_PEER_AT, KEPT_MATE_AT, KEPT_LINES = 16, 20, 24
LARGEST = float(jnp.finfo(jnp.bfloat16).max)
VMEM_LIMIT = 24 * 2**20
PEAK = 1.153e9


def split(value):
    clipped = jnp.clip(value, -LARGEST, LARGEST)
    high = clipped.astype(jnp.bfloat16)
    low = (value - high.astype(jnp.float32)).astype(jnp.bfloat16)
    return high, low


def products(*pairs):
    left = [part for (high, low), _ in pairs for part in (high, low, high)]
    right = [part for _, (high, low) in pairs for part in (high, high, low)]
    return jnp.dot(
        jnp.concatenate(left, axis=1),
        jnp.concatenate(right, axis=0),
        preferred_element_type=jnp.float32,
    )


def filtered(kept, value, region, scale=None, base=0, width=SLOTS):
    size = value.shape[0] // ROWS
    rows = []
    for i in range(ROWS):
        row = []
        for j in range(ROWS):
            at = base + i * width + region * ROWS + j
            flag = kept[at:at + 1, :]
            if scale is not None:
                flag = flag * scale
            row.append(value[i * size:(i + 1) * size, j * size:(j + 1) * size] * flag)
        rows.append(jnp.concatenate(row, axis=1))
    return jnp.concatenate(rows, axis=0)


def neighbours(row_devices, col_devices, order):
    row = lax.axis_index("row")
    col = lax.axis_index("col")
    odd = lax.rem(row, 2)

    def first(row_of, col_of):
        return (lax.rem(row_of, row_devices) * col_devices + lax.rem(col_of, col_devices)) * ROWS

    starts = (
        first(row + row_devices - 1 + 2 * odd, col),
        first(row, col),
        first(row + 1 - 2 * odd, col),
        first(row, col + 1),
    )
    return starts, [order[start + j] for start in starts for j in range(ROWS)]


def find_slots(pattern, stored, wanted):
    slots = [jnp.int32(0)] * len(wanted)
    for k in range(SLOTS):
        label = pattern[k, stored]
        slots = [jnp.where(label == want, k, slot) for want, slot in zip(wanted, slots)]
    return slots


def look_up(row_devices, col_devices, pattern, keep, order, slots, kept):
    starts, labels = neighbours(row_devices, col_devices, order)
    own_labels = labels[OWN * ROWS:(OWN + 1) * ROWS]

    def write_flags(stored, found, line):
        for j, slot in enumerate(found):
            flag = ((slot == 0) | (keep[slot, stored] == 1)).astype(jnp.float32)
            kept[line + j:line + j + 1, :] = jnp.full((1, kept.shape[1]), flag)

    result = []
    for i in range(ROWS):
        found = find_slots(pattern, starts[OWN] + i, labels)
        result.append(found)
        for j, slot in enumerate(found):
            line = i * SLOTS + j
            slots[line:line + 1, :] = jnp.full((1, slots.shape[1]), slot)
        write_flags(starts[OWN] + i, found, i * SLOTS)
        for region, line in ((PEER, KEPT_PEER_AT), (MATE, KEPT_MATE_AT)):
            stored = starts[region] + i
            write_flags(stored, find_slots(pattern, stored, own_labels), line + i * ROWS)
    return result


def quarter(i, j, size):
    return slice(i * size, (i + 1) * size), slice(j * size, (j + 1) * size)


def gather(slot_of, source, places):
    size = source.shape[1]
    for region, region_places in places.items():
        for i in range(ROWS):
            for j in range(ROWS):
                start = pl.multiple_of(slot_of(i, region * ROWS + j) * size, size)
                block = source[i, :, pl.ds(start, size)]
                for place in region_places:
                    place(i, j, size, block)


def into(out):
    def place(i, j, size, block):
        rows, cols = quarter(i, j, size)
        out[rows, cols] = block

    return place


def strip_peer(out):
    def place(i, j, size, block):
        out[i, :, j * size:(j + 1) * size] = block

    return place


def strip_own(out, at):
    def place(i, j, size, block):
        if i != j:
            out[at, :, i * size:(i + 1) * size] = block

    return place


Y_BESIDE, Z_BESIDE = ROWS, ROWS + 1


def peer_part(strips):
    return jnp.concatenate([strips[i] for i in range(ROWS)], axis=0)


def own_part(beside, spread):
    size = beside.shape[0]
    return jnp.concatenate(
        [
            jnp.concatenate([spread[:size, :size], beside[:, :size]], axis=1),
            jnp.concatenate([beside[:, size:], spread[size:, size:]], axis=1),
        ],
        axis=0,
    )


def diagonal_kernel(sqrt_iterate, inverse_iterate, diagonal, sems):
    size = sqrt_iterate.shape[1]
    copies = [
        pltpu.make_async_copy(
            source.at[:, :, pl.ds(0, size)], diagonal.at[pl.ds(at * ROWS, ROWS)], sems.at[at]
        )
        for at, source in enumerate((sqrt_iterate, inverse_iterate))
    ]
    for copy in copies:
        copy.start()
    for copy in copies:
        copy.wait()


def pack_kernel(
    row_devices, col_devices, pattern, keep, order, sqrt_iterate, inverse_iterate, after,
    slots, kept, y_peer, strips, mate, y_side, z_side, to_side,
    pattern_here, keep_here, order_here, sqrt_here, inverse_here, sems,
):
    copies = [
        pltpu.make_async_copy(source, here, sems.at[at])
        for at, (source, here) in enumerate((
            (order, order_here), (pattern, pattern_here), (keep, keep_here),
            (sqrt_iterate, sqrt_here), (inverse_iterate, inverse_here),
        ))
    ]
    for copy in copies:
        copy.start()
    for copy in copies[:3]:
        copy.wait()
    found = look_up(
        row_devices, col_devices, pattern_here, keep_here, order_here, slots, kept
    )

    def slot_of(i, j):
        return found[i][j]

    copies[3].wait()
    places = {
        PEER: (into(y_peer),),
        OWN: (strip_own(strips, Y_BESIDE), into(mate.at[1]), into(to_side.at[0])),
        MATE: (into(mate.at[0]),),
        SIDE: (into(y_side),),
    }
    gather(slot_of, sqrt_here, places)
    copies[4].wait()
    places = {
        PEER: (strip_peer(strips),),
        OWN: (strip_own(strips, Z_BESIDE), into(mate.at[3]), into(to_side.at[1])),
        MATE: (into(mate.at[2]),),
        SIDE: (into(z_side),),
    }
    gather(slot_of, inverse_here, places)


def greet_kernel(greeting):
    greeting[...] = jnp.zeros_like(greeting)


def heard_kernel(greeting, heard):
    heard[...] = greeting[...]


def spread_kernel(diagonal, after, spread):
    size = diagonal.shape[1]
    for at in range(2):
        for i in range(ROWS):
            for j in range(ROWS):
                rows, cols = quarter(i, j, size)
                block = diagonal[at * ROWS + i]
                spread[at, rows, cols] = block if i == j else jnp.zeros_like(block)


M_OWN, M_Y_OWN, M_Y_MATE, M_Z_OWN, M_Z_MATE = range(5)


def mate_kernel(kept, mate, from_mate, after, mate_terms):
    y_to_mate, y_own, z_to_mate, z_own = (split(mate[at]) for at in range(4))
    mate_y_mate, mate_y_own, mate_z_mate, mate_z_own = (split(from_mate[at]) for at in range(4))
    mate_terms[M_OWN] = products((z_own, y_own), (z_to_mate, mate_y_mate))
    total = products((z_own, y_to_mate), (z_to_mate, mate_y_own))
    f_mate = split(filtered(kept, total, MATE, -0.5))
    total = products((mate_z_own, mate_y_mate), (mate_z_mate, y_own))
    mate_f_mate = split(filtered(kept, total, 0, -0.5, KEPT_MATE_AT, ROWS))
    mate_terms[M_Y_OWN] = products((y_to_mate, mate_f_mate))
    mate_terms[M_Y_MATE] = products((y_own, f_mate))
    mate_terms[M_Z_OWN] = products((f_mate, mate_z_mate))
    mate_terms[M_Z_MATE] = products((f_mate, mate_z_own))


def factor_own_kernel(kept, mate_terms, strips, peer_y, factor_own, peer_term):
    peer_y_peer = split(peer_y[...])
    total = mate_terms[M_OWN] + products((split(peer_part(strips)), peer_y_peer))
    rows = lax.broadcasted_iota(jnp.int32, total.shape, 0)
    cols = lax.broadcasted_iota(jnp.int32, total.shape, 1)
    factor = jnp.where(rows == cols, 1.5, 0.0) + filtered(kept, total, OWN, -0.5)
    factor_own[...] = factor
    term = products((peer_y_peer, split(factor)))
    peer_term[...] = filtered(kept, term, 0, None, KEPT_PEER_AT, ROWS)


Y_MATE, Z_MATE, Z_SIDE = range(3)
Y_OWN_PART, Y_SIDE_PART, Z_OWN_PART, Z_PEER_PART, PEER_PART = range(5)
Y_PEER, Y_OWN, Y_SIDE, PEER_Y, Z_PEER = range(5)


def middle_kernel(
    kept, y_peer, strips, mate, y_side, z_side, mate_terms,
    peer_y, from_side, factor_own, mate_factor,
    finished, partial, ready,
):
    def keep(at, parts):
        ready[at, 0], ready[at, 1] = parts

    y_to_mate, y_own, z_to_mate, z_own = (split(mate[at]) for at in range(4))
    y_to_peer, z_to_peer = split(y_peer[...]), split(peer_part(strips))
    y_to_side, z_to_side = split(y_side[...]), split(z_side[...])
    f_own = split(factor_own[...])
    keep(Y_OWN, y_own)
    keep(Y_SIDE, y_to_side)
    keep(Y_PEER, y_to_peer)
    keep(Z_PEER, z_to_peer)
    keep(PEER_Y, split(peer_y[...]))

    total = products((z_own, y_to_side), (z_to_side, split(from_side[0])))
    f_side = split(filtered(kept, total, SIDE, -0.5))
    partial[PEER_PART] = products((z_own, y_to_peer))
    partial[Y_SIDE_PART] = products((y_own, f_side))
    partial[Y_OWN_PART] = mate_terms[M_Y_OWN] + products((y_own, f_own))
    partial[Z_PEER_PART] = products((f_own, z_to_peer))
    partial[Z_OWN_PART] = mate_terms[M_Z_OWN] + products((f_own, z_own))
    value = mate_terms[M_Y_MATE] + products((y_to_mate, split(mate_factor[...])))
    finished[Y_MATE] = filtered(kept, value, MATE)
    value = mate_terms[M_Z_MATE] + products((f_own, z_to_mate))
    finished[Z_MATE] = filtered(kept, value, MATE)
    value = products((f_own, z_to_side), (f_side, split(from_side[1])))
    finished[Z_SIDE] = filtered(kept, value, SIDE)


class Writer:
    def __init__(self, slots, kept, result, sems):
        self.slots, self.kept, self.result, self.sems = slots, kept, result, sems
        self.started = []
        self.held = 0

    def write(self, source, out, region):
        size = out.shape[1]
        for i in range(ROWS):
            for j in range(ROWS):
                rows, cols = quarter(i, j, size)
                slot = self.slots[i * SLOTS + region * ROWS + j, 0]
                copy = pltpu.make_async_copy(
                    source.at[rows, cols],
                    out.at[i, :, pl.ds(pl.multiple_of(slot * size, size), size)],
                    self.sems.at[len(self.started)],
                )
                copy.start()
                self.started.append(copy)

    def finish(self, value, out, region):
        place = self.result.at[self.held]
        self.held += 1
        place[...] = filtered(self.kept, value, region)
        self.write(place, out, region)

    def wait(self):
        for copy in self.started:
            copy.wait()


def peer_kernel(
    slots, kept, finished, partial, ready, from_peer, peer_spread,
    sqrt_next, inverse_next, y_peer_part, result, sems,
):
    def held(at):
        return ready[at, 0], ready[at, 1]

    writer = Writer(slots, kept, result, sems)
    writer.write(finished.at[Y_MATE], sqrt_next, MATE)
    writer.write(finished.at[Z_MATE], inverse_next, MATE)
    writer.write(finished.at[Z_SIDE], inverse_next, SIDE)
    peer_y_own = split(own_part(from_peer[Y_BESIDE], peer_spread[0]))
    peer_z_own = split(own_part(from_peer[Z_BESIDE], peer_spread[1]))
    peer_z_peer = split(peer_part(from_peer))
    total = partial[PEER_PART] + products((held(Z_PEER), peer_y_own))
    f_peer = split(filtered(kept, total, PEER, -0.5))
    total = products((peer_z_own, held(PEER_Y)), (peer_z_peer, held(Y_OWN)))
    peer_f_peer = split(filtered(kept, total, 0, -0.5, KEPT_PEER_AT, ROWS))
    value = partial[Z_PEER_PART] + products((f_peer, peer_z_own))
    writer.finish(value, inverse_next, PEER)
    value = partial[Z_OWN_PART] + products((f_peer, peer_z_peer))
    writer.finish(value, inverse_next, OWN)
    value = partial[Y_OWN_PART] + products((held(Y_PEER), peer_f_peer))
    writer.finish(value, sqrt_next, OWN)
    y_peer_part[...] = filtered(kept, products((held(Y_OWN), f_peer)), PEER)
    writer.wait()


def side_kernel(slots, kept, partial, ready, factor, unfinished, sqrt_next, result, sems):
    left = (ready[Y_SIDE, 0], ready[Y_SIDE, 1])
    value = partial[Y_SIDE_PART] + products((left, split(factor[...])))
    writer = Writer(slots, kept, result, sems)
    writer.finish(value, sqrt_next, SIDE)
    writer.wait()


def last_kernel(slots, part, term, unfinished, sqrt_next, result, sems):
    size = sqrt_next.shape[1]
    copies = []
    blocks = [(i, j) for i in range(ROWS) for j in range(ROWS)]
    starts = [slots[i * SLOTS + PEER * ROWS + j, 0] * size for i, j in blocks]
    for at, (i, j) in enumerate(blocks):
        rows, cols = quarter(i, j, size)
        result[at] = part[rows, cols] + term[rows, cols]
        out = sqrt_next.at[i, :, pl.ds(pl.multiple_of(starts[at], size), size)]
        copies.append(pltpu.make_async_copy(result.at[at], out, sems.at[at]))
        copies[at].start()
    for copy in copies:
        copy.wait()


def call(
    kernel, outs, operands, micros=0, scratch=(), hbm_in=(), any_in=(), hbm_out=(), in_place=None
):
    def spec(space=pltpu.VMEM):
        return pl.BlockSpec(memory_space=space)

    operands = [
        pltpu.with_memory_space_constraint(array, pltpu.HBM) if at in hbm_in else array
        for at, array in enumerate(operands)
    ]
    return pl.pallas_call(
        kernel,
        out_shape=outs,
        in_specs=[
            spec(pltpu.HBM if at in hbm_in else pl.ANY if at in any_in else pltpu.VMEM)
            for at in range(len(operands))
        ],
        out_specs=tuple(
            spec(pltpu.HBM if at in hbm_out else pltpu.VMEM) for at in range(len(outs))
        ),
        scratch_shapes=scratch,
        input_output_aliases={} if in_place is None else {in_place: 0},
        compiler_params=pltpu.CompilerParams(vmem_limit_bytes=VMEM_LIMIT),
        cost_estimate=pl.CostEstimate(
            flops=int(micros * PEAK), bytes_accessed=0, transcendentals=0
        ),
    )(*operands)


def local(sqrt_iterate, inverse_iterate, pattern, keep_mask, row_order):
    rows_dev, block, width = sqrt_iterate.shape
    row_devices, col_devices = lax.axis_size("row"), lax.axis_size("col")
    assert rows_dev == ROWS and width == SLOTS * block and pattern.shape[1] == SLOTS
    assert row_devices > 3 and row_devices % 2 == 0 and col_devices > 2
    size = ROWS * block

    def to_mate(value):
        return lax.ppermute(value, "row", [(i, i ^ 1) for i in range(row_devices)])

    def to_peer(value):
        route = [(i, (i + (1 if i % 2 else -1)) % row_devices) for i in range(row_devices)]
        return lax.ppermute(value, "row", route)

    def to_side(value):
        route = [((i + 1) % col_devices, i) for i in range(col_devices)]
        return lax.ppermute(value, "col", route)

    def shape(*dims, dtype=jnp.float32):
        return jax.ShapeDtypeStruct(dims, dtype)

    one, pair = shape(size, size), shape(2, size, size)
    (greeting,) = call(greet_kernel, (shape(8, block),), ())
    peer_greeting = to_peer(greeting)
    (diagonal,) = call(
        diagonal_kernel,
        (shape(2 * ROWS, block, block),),
        (sqrt_iterate, inverse_iterate),
        scratch=[pltpu.SemaphoreType.DMA((2,))],
        hbm_in=range(2),
    )
    peer_diagonal = to_peer(diagonal)
    slots, kept, y_peer, strips, mate, y_side, z_side, own_pair = call(
        functools.partial(pack_kernel, row_devices, col_devices),
        (
            shape(ROWS * SLOTS, block, dtype=jnp.int32), shape(KEPT_LINES, block),
            one, shape(ROWS + 2, block, size), shape(4, size, size), one, one, pair,
        ),
        (pattern.T, keep_mask.T, row_order, sqrt_iterate, inverse_iterate, diagonal),
        scratch=[
            pltpu.SMEM(pattern.T.shape, jnp.int32),
            pltpu.SMEM(keep_mask.T.shape, jnp.int32),
            pltpu.SMEM(row_order.shape, jnp.int32),
            pltpu.VMEM(sqrt_iterate.shape, jnp.float32),
            pltpu.VMEM(inverse_iterate.shape, jnp.float32),
            pltpu.SemaphoreType.DMA((5,)),
        ],
        hbm_in=range(5),
        any_in=(5,),
    )
    peer_y = to_peer(y_peer)
    from_peer = to_peer(strips)
    from_mate = to_mate(mate)
    from_side = to_side(own_pair)
    (heard,) = call(heard_kernel, (shape(8, block),), (peer_greeting,), micros=5)
    (peer_spread,) = call(
        spread_kernel, (pair,), (peer_diagonal, heard), any_in=(1,), micros=10
    )
    (mate_terms,) = call(
        mate_kernel,
        (shape(5, size, size),),
        (kept, mate, from_mate, peer_spread),
        any_in=(3,),
    )
    factor_own, peer_term = call(
        factor_own_kernel, (one, one), (kept, mate_terms, strips, peer_y), micros=5
    )
    mate_factor = to_mate(factor_own)
    term = to_peer(peer_term)
    side_factor = to_side(factor_own)
    finished, partial, ready = call(
        middle_kernel,
        (
            shape(3, size, size), shape(5, size, size),
            shape(5, 2, size, size, dtype=jnp.bfloat16),
        ),
        (
            kept, y_peer, strips, mate, y_side, z_side, mate_terms,
            peer_y, from_side, factor_own, mate_factor,
        ),
    )
    output = shape(rows_dev, block, width)

    def writing(blocks):
        return [
            pltpu.VMEM((blocks, size, size), jnp.float32),
            pltpu.SemaphoreType.DMA((24,)),
        ]

    sqrt_next, inverse_next, y_peer_part = call(
        peer_kernel,
        (output, output, one),
        (slots, kept, finished, partial, ready, from_peer, peer_spread),
        scratch=writing(3),
        hbm_out=(0, 1),
    )
    (sqrt_next,) = call(
        side_kernel,
        (output,),
        (slots, kept, partial, ready, side_factor, sqrt_next),
        scratch=writing(1),
        hbm_in=(5,),
        hbm_out=(0,),
        in_place=5,
    )
    (sqrt_next,) = call(
        last_kernel,
        (output,),
        (slots, y_peer_part, term, sqrt_next),
        scratch=[
            pltpu.VMEM((ROWS * ROWS, block, block), jnp.float32),
            pltpu.SemaphoreType.DMA((ROWS * ROWS,)),
        ],
        hbm_in=(3,),
        hbm_out=(0,),
        in_place=3,
    )
    return sqrt_next, inverse_next


def solution(mesh):
    rows = P(("row", "col"), None, None)
    return jax.shard_map(
        local,
        mesh=mesh,
        in_specs=(rows, rows, P(), P(), P()),
        out_specs=(rows, rows),
        check_vma=False,
    )
```

```python
import functools

import jax
import jax.numpy as jnp
from jax import lax
from jax.experimental import pallas as pl
from jax.experimental.pallas import tpu as pltpu
from jax.sharding import PartitionSpec as P

PEER, OWN, MATE, SIDE = range(4)
ROWS = 2
SLOTS = 8
KEPT_PEER_AT, KEPT_MATE_AT, KEPT_LINES = 16, 20, 24
LARGEST = float(jnp.finfo(jnp.bfloat16).max)
VMEM_LIMIT = 24 * 2**20
PEAK = 1.153e9


def split(value):
    clipped = jnp.clip(value, -LARGEST, LARGEST)
    high = clipped.astype(jnp.bfloat16)
    low = (value - high.astype(jnp.float32)).astype(jnp.bfloat16)
    return high, low


def products(*pairs):
    left = [part for (high, low), _ in pairs for part in (high, low, high)]
    right = [part for _, (high, low) in pairs for part in (high, high, low)]
    return jnp.dot(
        jnp.concatenate(left, axis=1),
        jnp.concatenate(right, axis=0),
        preferred_element_type=jnp.float32,
    )


def filtered(kept, value, region, scale=None, base=0, width=SLOTS):
    size = value.shape[0] // ROWS
    rows = []
    for i in range(ROWS):
        row = []
        for j in range(ROWS):
            at = base + i * width + region * ROWS + j
            flag = kept[at:at + 1, :]
            if scale is not None:
                flag = flag * scale
            row.append(value[i * size:(i + 1) * size, j * size:(j + 1) * size] * flag)
        rows.append(jnp.concatenate(row, axis=1))
    return jnp.concatenate(rows, axis=0)


def neighbours(row_devices, col_devices, order):
    row = lax.axis_index("row")
    col = lax.axis_index("col")
    odd = lax.rem(row, 2)

    def first(row_of, col_of):
        return (lax.rem(row_of, row_devices) * col_devices + lax.rem(col_of, col_devices)) * ROWS

    starts = (
        first(row + row_devices - 1 + 2 * odd, col),
        first(row, col),
        first(row + 1 - 2 * odd, col),
        first(row, col + 1),
    )
    return starts, [order[start + j] for start in starts for j in range(ROWS)]


def find_slots(pattern, stored, wanted):
    slots = [jnp.int32(0)] * len(wanted)
    for k in range(SLOTS):
        label = pattern[k, stored]
        slots = [jnp.where(label == want, k, slot) for want, slot in zip(wanted, slots)]
    return slots


def look_up(row_devices, col_devices, pattern, keep, order, slots, kept):
    starts, labels = neighbours(row_devices, col_devices, order)
    own_labels = labels[OWN * ROWS:(OWN + 1) * ROWS]

    def write_flags(stored, found, line):
        for j, slot in enumerate(found):
            flag = ((slot == 0) | (keep[slot, stored] == 1)).astype(jnp.float32)
            kept[line + j:line + j + 1, :] = jnp.full((1, kept.shape[1]), flag)

    result = []
    for i in range(ROWS):
        found = find_slots(pattern, starts[OWN] + i, labels)
        result.append(found)
        for j, slot in enumerate(found):
            line = i * SLOTS + j
            slots[line:line + 1, :] = jnp.full((1, slots.shape[1]), slot)
        write_flags(starts[OWN] + i, found, i * SLOTS)
        for region, line in ((PEER, KEPT_PEER_AT), (MATE, KEPT_MATE_AT)):
            stored = starts[region] + i
            write_flags(stored, find_slots(pattern, stored, own_labels), line + i * ROWS)
    return result


def quarter(i, j, size):
    return slice(i * size, (i + 1) * size), slice(j * size, (j + 1) * size)


def gather(slot_of, source, places):
    size = source.shape[1]
    for region, region_places in places.items():
        for i in range(ROWS):
            for j in range(ROWS):
                start = pl.multiple_of(slot_of(i, region * ROWS + j) * size, size)
                block = source[i, :, pl.ds(start, size)]
                for place in region_places:
                    place(i, j, size, block)


def into(out):
    def place(i, j, size, block):
        rows, cols = quarter(i, j, size)
        out[rows, cols] = block

    return place


def strip_peer(out):
    def place(i, j, size, block):
        out[i, :, j * size:(j + 1) * size] = block

    return place


def strip_own(out, at):
    def place(i, j, size, block):
        if i != j:
            out[at, :, i * size:(i + 1) * size] = block

    return place


Y_BESIDE, Z_BESIDE = ROWS, ROWS + 1


def peer_part(strips):
    return jnp.concatenate([strips[i] for i in range(ROWS)], axis=0)


def own_part(beside, spread):
    size = beside.shape[0]
    return jnp.concatenate(
        [
            jnp.concatenate([spread[:size, :size], beside[:, :size]], axis=1),
            jnp.concatenate([beside[:, size:], spread[size:, size:]], axis=1),
        ],
        axis=0,
    )


def diagonal_kernel(sqrt_iterate, inverse_iterate, diagonal, sems):
    size = sqrt_iterate.shape[1]
    half = size // 2
    copies = []
    for source in (sqrt_iterate, inverse_iterate):
        for i in range(ROWS):
            block = len(copies) // 2
            for rows in (pl.ds(0, half), pl.ds(half, half)):
                copies.append(
                    pltpu.make_async_copy(
                        source.at[i, rows, pl.ds(0, size)],
                        diagonal.at[block, rows],
                        sems.at[len(copies)],
                    )
                )
                copies[-1].start()
    for copy in copies:
        copy.wait()


def pack_kernel(
    row_devices, col_devices, pattern, keep, order, sqrt_iterate, inverse_iterate, after,
    slots, kept, y_peer, strips, mate, y_side, z_side, to_side,
    pattern_here, keep_here, order_here, sqrt_here, inverse_here, sems,
):
    copies = [
        pltpu.make_async_copy(source, here, sems.at[at])
        for at, (source, here) in enumerate((
            (order, order_here), (pattern, pattern_here), (keep, keep_here),
            (sqrt_iterate, sqrt_here), (inverse_iterate, inverse_here),
        ))
    ]
    for copy in copies:
        copy.start()
    for copy in copies[:3]:
        copy.wait()
    found = look_up(
        row_devices, col_devices, pattern_here, keep_here, order_here, slots, kept
    )

    def slot_of(i, j):
        return found[i][j]

    copies[3].wait()
    places = {
        PEER: (into(y_peer),),
        OWN: (strip_own(strips, Y_BESIDE), into(mate.at[1]), into(to_side.at[0])),
        MATE: (into(mate.at[0]),),
        SIDE: (into(y_side),),
    }
    gather(slot_of, sqrt_here, places)
    copies[4].wait()
    places = {
        PEER: (strip_peer(strips),),
        OWN: (strip_own(strips, Z_BESIDE), into(mate.at[3]), into(to_side.at[1])),
        MATE: (into(mate.at[2]),),
        SIDE: (into(z_side),),
    }
    gather(slot_of, inverse_here, places)


def spread_kernel(diagonal, spread):
    size = diagonal.shape[1]
    for at in range(2):
        for i in range(ROWS):
            for j in range(ROWS):
                rows, cols = quarter(i, j, size)
                block = diagonal[at * ROWS + i]
                spread[at, rows, cols] = block if i == j else jnp.zeros_like(block)


M_OWN, M_Y_OWN, M_Y_MATE, M_Z_OWN, M_Z_MATE = range(5)


def mate_kernel(kept, mate, from_mate, after, mate_terms):
    y_to_mate, y_own, z_to_mate, z_own = (split(mate[at]) for at in range(4))
    mate_y_mate, mate_y_own, mate_z_mate, mate_z_own = (split(from_mate[at]) for at in range(4))
    mate_terms[M_OWN] = products((z_own, y_own), (z_to_mate, mate_y_mate))
    total = products((z_own, y_to_mate), (z_to_mate, mate_y_own))
    f_mate = split(filtered(kept, total, MATE, -0.5))
    total = products((mate_z_own, mate_y_mate), (mate_z_mate, y_own))
    mate_f_mate = split(filtered(kept, total, 0, -0.5, KEPT_MATE_AT, ROWS))
    mate_terms[M_Y_OWN] = products((y_to_mate, mate_f_mate))
    mate_terms[M_Y_MATE] = products((y_own, f_mate))
    mate_terms[M_Z_OWN] = products((f_mate, mate_z_mate))
    mate_terms[M_Z_MATE] = products((f_mate, mate_z_own))


def factor_own_kernel(kept, mate_terms, strips, peer_y, factor_own, peer_term):
    peer_y_peer = split(peer_y[...])
    total = mate_terms[M_OWN] + products((split(peer_part(strips)), peer_y_peer))
    rows = lax.broadcasted_iota(jnp.int32, total.shape, 0)
    cols = lax.broadcasted_iota(jnp.int32, total.shape, 1)
    factor = jnp.where(rows == cols, 1.5, 0.0) + filtered(kept, total, OWN, -0.5)
    factor_own[...] = factor
    term = products((peer_y_peer, split(factor)))
    peer_term[...] = filtered(kept, term, 0, None, KEPT_PEER_AT, ROWS)


Y_MATE, Z_MATE, Z_SIDE = range(3)
Y_OWN_PART, Y_SIDE_PART, Z_OWN_PART, Z_PEER_PART, PEER_PART = range(5)
Y_PEER, Y_OWN, Y_SIDE, PEER_Y, Z_PEER = range(5)


def middle_kernel(
    kept, y_peer, strips, mate, y_side, z_side, mate_terms,
    peer_y, from_side, factor_own, mate_factor,
    finished, partial, ready,
):
    def keep(at, parts):
        ready[at, 0], ready[at, 1] = parts

    y_to_mate, y_own, z_to_mate, z_own = (split(mate[at]) for at in range(4))
    y_to_peer, z_to_peer = split(y_peer[...]), split(peer_part(strips))
    y_to_side, z_to_side = split(y_side[...]), split(z_side[...])
    f_own = split(factor_own[...])
    keep(Y_OWN, y_own)
    keep(Y_SIDE, y_to_side)
    keep(Y_PEER, y_to_peer)
    keep(Z_PEER, z_to_peer)
    keep(PEER_Y, split(peer_y[...]))

    total = products((z_own, y_to_side), (z_to_side, split(from_side[0])))
    f_side = split(filtered(kept, total, SIDE, -0.5))
    partial[PEER_PART] = products((z_own, y_to_peer))
    partial[Y_SIDE_PART] = products((y_own, f_side))
    partial[Y_OWN_PART] = mate_terms[M_Y_OWN] + products((y_own, f_own))
    partial[Z_PEER_PART] = products((f_own, z_to_peer))
    partial[Z_OWN_PART] = mate_terms[M_Z_OWN] + products((f_own, z_own))
    value = mate_terms[M_Y_MATE] + products((y_to_mate, split(mate_factor[...])))
    finished[Y_MATE] = filtered(kept, value, MATE)
    value = mate_terms[M_Z_MATE] + products((f_own, z_to_mate))
    finished[Z_MATE] = filtered(kept, value, MATE)
    value = products((f_own, z_to_side), (f_side, split(from_side[1])))
    finished[Z_SIDE] = filtered(kept, value, SIDE)


class Writer:
    def __init__(self, slots, kept, result, sems):
        self.slots, self.kept, self.result, self.sems = slots, kept, result, sems
        self.started = []
        self.held = 0

    def write(self, source, out, region):
        size = out.shape[1]
        for i in range(ROWS):
            for j in range(ROWS):
                rows, cols = quarter(i, j, size)
                slot = self.slots[i * SLOTS + region * ROWS + j, 0]
                copy = pltpu.make_async_copy(
                    source.at[rows, cols],
                    out.at[i, :, pl.ds(pl.multiple_of(slot * size, size), size)],
                    self.sems.at[len(self.started)],
                )
                copy.start()
                self.started.append(copy)

    def finish(self, value, out, region):
        place = self.result.at[self.held]
        self.held += 1
        place[...] = filtered(self.kept, value, region)
        self.write(place, out, region)

    def wait(self):
        for copy in self.started:
            copy.wait()


def peer_kernel(
    slots, kept, finished, partial, ready, from_peer, peer_spread,
    sqrt_next, inverse_next, y_peer_part, result, sems,
):
    def held(at):
        return ready[at, 0], ready[at, 1]

    writer = Writer(slots, kept, result, sems)
    writer.write(finished.at[Y_MATE], sqrt_next, MATE)
    writer.write(finished.at[Z_MATE], inverse_next, MATE)
    writer.write(finished.at[Z_SIDE], inverse_next, SIDE)
    peer_y_own = split(own_part(from_peer[Y_BESIDE], peer_spread[0]))
    peer_z_own = split(own_part(from_peer[Z_BESIDE], peer_spread[1]))
    peer_z_peer = split(peer_part(from_peer))
    total = partial[PEER_PART] + products((held(Z_PEER), peer_y_own))
    f_peer = split(filtered(kept, total, PEER, -0.5))
    total = products((peer_z_own, held(PEER_Y)), (peer_z_peer, held(Y_OWN)))
    peer_f_peer = split(filtered(kept, total, 0, -0.5, KEPT_PEER_AT, ROWS))
    value = partial[Z_PEER_PART] + products((f_peer, peer_z_own))
    writer.finish(value, inverse_next, PEER)
    value = partial[Z_OWN_PART] + products((f_peer, peer_z_peer))
    writer.finish(value, inverse_next, OWN)
    value = partial[Y_OWN_PART] + products((held(Y_PEER), peer_f_peer))
    writer.finish(value, sqrt_next, OWN)
    y_peer_part[...] = filtered(kept, products((held(Y_OWN), f_peer)), PEER)
    writer.wait()


def side_kernel(slots, kept, partial, ready, factor, unfinished, sqrt_next, result, sems):
    left = (ready[Y_SIDE, 0], ready[Y_SIDE, 1])
    value = partial[Y_SIDE_PART] + products((left, split(factor[...])))
    writer = Writer(slots, kept, result, sems)
    writer.finish(value, sqrt_next, SIDE)
    writer.wait()


def last_kernel(slots, part, term, unfinished, sqrt_next, result, sems):
    size = sqrt_next.shape[1]
    copies = []
    blocks = [(i, j) for i in range(ROWS) for j in range(ROWS)]
    starts = [slots[i * SLOTS + PEER * ROWS + j, 0] * size for i, j in blocks]
    for at, (i, j) in enumerate(blocks):
        rows, cols = quarter(i, j, size)
        result[at] = part[rows, cols] + term[rows, cols]
        for half in (pl.ds(0, size // 2), pl.ds(size // 2, size // 2)):
            out = sqrt_next.at[i, half, pl.ds(pl.multiple_of(starts[at], size), size)]
            copies.append(
                pltpu.make_async_copy(result.at[at, half], out, sems.at[len(copies)])
            )
            copies[-1].start()
    for copy in copies:
        copy.wait()


def call(
    kernel, outs, operands, micros=0, scratch=(), hbm_in=(), any_in=(), hbm_out=(), in_place=None
):
    def spec(space=pltpu.VMEM):
        return pl.BlockSpec(memory_space=space)

    operands = [
        pltpu.with_memory_space_constraint(array, pltpu.HBM) if at in hbm_in else array
        for at, array in enumerate(operands)
    ]
    return pl.pallas_call(
        kernel,
        out_shape=outs,
        in_specs=[
            spec(pltpu.HBM if at in hbm_in else pl.ANY if at in any_in else pltpu.VMEM)
            for at in range(len(operands))
        ],
        out_specs=tuple(
            spec(pltpu.HBM if at in hbm_out else pltpu.VMEM) for at in range(len(outs))
        ),
        scratch_shapes=scratch,
        input_output_aliases={} if in_place is None else {in_place: 0},
        compiler_params=pltpu.CompilerParams(vmem_limit_bytes=VMEM_LIMIT),
        cost_estimate=pl.CostEstimate(
            flops=int(micros * PEAK), bytes_accessed=0, transcendentals=0
        ),
    )(*operands)


def local(sqrt_iterate, inverse_iterate, pattern, keep_mask, row_order):
    rows_dev, block, width = sqrt_iterate.shape
    row_devices, col_devices = lax.axis_size("row"), lax.axis_size("col")
    assert rows_dev == ROWS and width == SLOTS * block and pattern.shape[1] == SLOTS
    assert row_devices > 3 and row_devices % 2 == 0 and col_devices > 2
    size = ROWS * block

    def to_mate(value):
        return lax.ppermute(value, "row", [(i, i ^ 1) for i in range(row_devices)])

    def to_peer(value):
        route = [(i, (i + (1 if i % 2 else -1)) % row_devices) for i in range(row_devices)]
        return lax.ppermute(value, "row", route)

    def to_side(value):
        route = [((i + 1) % col_devices, i) for i in range(col_devices)]
        return lax.ppermute(value, "col", route)

    def shape(*dims, dtype=jnp.float32):
        return jax.ShapeDtypeStruct(dims, dtype)

    one, pair = shape(size, size), shape(2, size, size)
    (diagonal,) = call(
        diagonal_kernel,
        (shape(2 * ROWS, block, block),),
        (sqrt_iterate, inverse_iterate),
        scratch=[pltpu.SemaphoreType.DMA((4 * ROWS,))],
        hbm_in=range(2),
    )
    peer_diagonal = to_peer(diagonal)
    slots, kept, y_peer, strips, mate, y_side, z_side, own_pair = call(
        functools.partial(pack_kernel, row_devices, col_devices),
        (
            shape(ROWS * SLOTS, block, dtype=jnp.int32), shape(KEPT_LINES, block),
            one, shape(ROWS + 2, block, size), shape(4, size, size), one, one, pair,
        ),
        (pattern.T, keep_mask.T, row_order, sqrt_iterate, inverse_iterate, diagonal),
        scratch=[
            pltpu.SMEM(pattern.T.shape, jnp.int32),
            pltpu.SMEM(keep_mask.T.shape, jnp.int32),
            pltpu.SMEM(row_order.shape, jnp.int32),
            pltpu.VMEM(sqrt_iterate.shape, jnp.float32),
            pltpu.VMEM(inverse_iterate.shape, jnp.float32),
            pltpu.SemaphoreType.DMA((5,)),
        ],
        hbm_in=range(5),
        any_in=(5,),
    )
    peer_y = to_peer(y_peer)
    from_peer = to_peer(strips)
    from_mate = to_mate(mate)
    from_side = to_side(own_pair)
    (peer_spread,) = call(spread_kernel, (pair,), (peer_diagonal,), micros=10)
    (mate_terms,) = call(
        mate_kernel,
        (shape(5, size, size),),
        (kept, mate, from_mate, peer_spread),
        any_in=(3,),
    )
    factor_own, peer_term = call(
        factor_own_kernel, (one, one), (kept, mate_terms, strips, peer_y), micros=5
    )
    mate_factor = to_mate(factor_own)
    term = to_peer(peer_term)
    side_factor = to_side(factor_own)
    finished, partial, ready = call(
        middle_kernel,
        (
            shape(3, size, size), shape(5, size, size),
            shape(5, 2, size, size, dtype=jnp.bfloat16),
        ),
        (
            kept, y_peer, strips, mate, y_side, z_side, mate_terms,
            peer_y, from_side, factor_own, mate_factor,
        ),
    )
    output = shape(rows_dev, block, width)

    def writing(blocks):
        return [
            pltpu.VMEM((blocks, size, size), jnp.float32),
            pltpu.SemaphoreType.DMA((24,)),
        ]

    sqrt_next, inverse_next, y_peer_part = call(
        peer_kernel,
        (output, output, one),
        (slots, kept, finished, partial, ready, from_peer, peer_spread),
        scratch=writing(3),
        hbm_out=(0, 1),
    )
    (sqrt_next,) = call(
        side_kernel,
        (output,),
        (slots, kept, partial, ready, side_factor, sqrt_next),
        scratch=writing(1),
        hbm_in=(5,),
        hbm_out=(0,),
        in_place=5,
    )
    (sqrt_next,) = call(
        last_kernel,
        (output,),
        (slots, y_peer_part, term, sqrt_next),
        scratch=[
            pltpu.VMEM((ROWS * ROWS, block, block), jnp.float32),
            pltpu.SemaphoreType.DMA((2 * ROWS * ROWS,)),
        ],
        hbm_in=(3,),
        hbm_out=(0,),
        in_place=3,
    )
    return sqrt_next, inverse_next


def solution(mesh):
    rows = P(("row", "col"), None, None)
    return jax.shard_map(
        local,
        mesh=mesh,
        in_specs=(rows, rows, P(), P(), P()),
        out_specs=(rows, rows),
        check_vma=False,
    )
```

```python
import functools

import jax
import jax.numpy as jnp
from jax import lax
from jax.experimental import pallas as pl
from jax.experimental.pallas import tpu as pltpu
from jax.sharding import PartitionSpec as P

PEER, OWN, MATE, SIDE = range(4)
ROWS = 2
SLOTS = 8
KEPT_PEER_AT, KEPT_MATE_AT, KEPT_LINES = 16, 20, 24
LARGEST = float(jnp.finfo(jnp.bfloat16).max)
VMEM_LIMIT = 24 * 2**20
PEAK = 1.153e9


def split(value):
    clipped = jnp.clip(value, -LARGEST, LARGEST)
    high = clipped.astype(jnp.bfloat16)
    low = (value - high.astype(jnp.float32)).astype(jnp.bfloat16)
    return high, low


def products(*pairs):
    left = [part for (high, low), _ in pairs for part in (high, low, high)]
    right = [part for _, (high, low) in pairs for part in (high, high, low)]
    return jnp.dot(
        jnp.concatenate(left, axis=1),
        jnp.concatenate(right, axis=0),
        preferred_element_type=jnp.float32,
    )


def filtered(kept, value, region, scale=None, base=0, width=SLOTS):
    size = value.shape[0] // ROWS
    rows = []
    for i in range(ROWS):
        row = []
        for j in range(ROWS):
            at = base + i * width + region * ROWS + j
            flag = kept[at:at + 1, :]
            if scale is not None:
                flag = flag * scale
            row.append(value[i * size:(i + 1) * size, j * size:(j + 1) * size] * flag)
        rows.append(jnp.concatenate(row, axis=1))
    return jnp.concatenate(rows, axis=0)


def neighbours(row_devices, col_devices, order):
    row = lax.axis_index("row")
    col = lax.axis_index("col")
    odd = lax.rem(row, 2)

    def first(row_of, col_of):
        return (lax.rem(row_of, row_devices) * col_devices + lax.rem(col_of, col_devices)) * ROWS

    starts = (
        first(row + row_devices - 1 + 2 * odd, col),
        first(row, col),
        first(row + 1 - 2 * odd, col),
        first(row, col + 1),
    )
    return starts, [order[start + j] for start in starts for j in range(ROWS)]


def find_slots(pattern, stored, wanted):
    slots = [jnp.int32(0)] * len(wanted)
    for k in range(SLOTS):
        label = pattern[k, stored]
        slots = [jnp.where(label == want, k, slot) for want, slot in zip(wanted, slots)]
    return slots


def look_up(row_devices, col_devices, pattern, keep, order, slots, kept):
    starts, labels = neighbours(row_devices, col_devices, order)
    own_labels = labels[OWN * ROWS:(OWN + 1) * ROWS]

    def write_flags(stored, found, line):
        for j, slot in enumerate(found):
            flag = ((slot == 0) | (keep[slot, stored] == 1)).astype(jnp.float32)
            kept[line + j:line + j + 1, :] = jnp.full((1, kept.shape[1]), flag)

    result = []
    for i in range(ROWS):
        found = find_slots(pattern, starts[OWN] + i, labels)
        result.append(found)
        for j, slot in enumerate(found):
            line = i * SLOTS + j
            slots[line:line + 1, :] = jnp.full((1, slots.shape[1]), slot)
        write_flags(starts[OWN] + i, found, i * SLOTS)
        for region, line in ((PEER, KEPT_PEER_AT), (MATE, KEPT_MATE_AT)):
            stored = starts[region] + i
            write_flags(stored, find_slots(pattern, stored, own_labels), line + i * ROWS)
    return result


def quarter(i, j, size):
    return slice(i * size, (i + 1) * size), slice(j * size, (j + 1) * size)


def gather(slot_of, source, places):
    size = source.shape[1]
    for region, region_places in places.items():
        for i in range(ROWS):
            for j in range(ROWS):
                start = pl.multiple_of(slot_of(i, region * ROWS + j) * size, size)
                block = source[i, :, pl.ds(start, size)]
                for place in region_places:
                    place(i, j, size, block)


def into(out):
    def place(i, j, size, block):
        rows, cols = quarter(i, j, size)
        out[rows, cols] = block

    return place


def strip_peer(out):
    def place(i, j, size, block):
        out[i, :, j * size:(j + 1) * size] = block

    return place


def strip_own(out, at):
    def place(i, j, size, block):
        if i != j:
            out[at, :, i * size:(i + 1) * size] = block

    return place


Y_BESIDE, Z_BESIDE = ROWS, ROWS + 1


def peer_part(strips):
    return jnp.concatenate([strips[i] for i in range(ROWS)], axis=0)


def own_part(beside, spread):
    size = beside.shape[0]
    return jnp.concatenate(
        [
            jnp.concatenate([spread[:size, :size], beside[:, :size]], axis=1),
            jnp.concatenate([beside[:, size:], spread[size:, size:]], axis=1),
        ],
        axis=0,
    )


def diagonal_kernel(sqrt_iterate, inverse_iterate, diagonal, sems):
    size = sqrt_iterate.shape[1]
    half = size // 2
    copies = []
    for source in (sqrt_iterate, inverse_iterate):
        for i in range(ROWS):
            block = len(copies) // 2
            for rows in (pl.ds(0, half), pl.ds(half, half)):
                copies.append(
                    pltpu.make_async_copy(
                        source.at[i, rows, pl.ds(0, size)],
                        diagonal.at[block, rows],
                        sems.at[len(copies)],
                    )
                )
                copies[-1].start()
    for copy in copies:
        copy.wait()


def pack_kernel(
    row_devices, col_devices, pattern, keep, order, sqrt_iterate, inverse_iterate, after,
    slots, kept, y_peer, strips, mate, y_side, z_side, to_side,
    pattern_here, keep_here, order_here, sqrt_here, inverse_here, sems,
):
    copies = [
        pltpu.make_async_copy(source, here, sems.at[at])
        for at, (source, here) in enumerate((
            (order, order_here), (pattern, pattern_here), (keep, keep_here),
            (sqrt_iterate, sqrt_here), (inverse_iterate, inverse_here),
        ))
    ]
    for copy in copies:
        copy.start()
    for copy in copies[:3]:
        copy.wait()
    found = look_up(
        row_devices, col_devices, pattern_here, keep_here, order_here, slots, kept
    )

    def slot_of(i, j):
        return found[i][j]

    copies[3].wait()
    places = {
        PEER: (into(y_peer),),
        OWN: (strip_own(strips, Y_BESIDE), into(mate.at[1]), into(to_side.at[0])),
        MATE: (into(mate.at[0]),),
        SIDE: (into(y_side),),
    }
    gather(slot_of, sqrt_here, places)
    copies[4].wait()
    places = {
        PEER: (strip_peer(strips),),
        OWN: (strip_own(strips, Z_BESIDE), into(mate.at[3]), into(to_side.at[1])),
        MATE: (into(mate.at[2]),),
        SIDE: (into(z_side),),
    }
    gather(slot_of, inverse_here, places)


def spread_kernel(diagonal, spread):
    size = diagonal.shape[1]
    for at in range(2):
        for i in range(ROWS):
            for j in range(ROWS):
                rows, cols = quarter(i, j, size)
                block = diagonal[at * ROWS + i]
                spread[at, rows, cols] = block if i == j else jnp.zeros_like(block)


M_OWN, M_Y_OWN, M_Y_MATE, M_Z_OWN, M_Z_MATE = range(5)


def mate_kernel(kept, mate, from_mate, after, mate_terms):
    y_to_mate, y_own, z_to_mate, z_own = (split(mate[at]) for at in range(4))
    mate_y_mate, mate_y_own, mate_z_mate, mate_z_own = (split(from_mate[at]) for at in range(4))
    mate_terms[M_OWN] = products((z_own, y_own), (z_to_mate, mate_y_mate))
    total = products((z_own, y_to_mate), (z_to_mate, mate_y_own))
    f_mate = split(filtered(kept, total, MATE, -0.5))
    total = products((mate_z_own, mate_y_mate), (mate_z_mate, y_own))
    mate_f_mate = split(filtered(kept, total, 0, -0.5, KEPT_MATE_AT, ROWS))
    mate_terms[M_Y_OWN] = products((y_to_mate, mate_f_mate))
    mate_terms[M_Y_MATE] = products((y_own, f_mate))
    mate_terms[M_Z_OWN] = products((f_mate, mate_z_mate))
    mate_terms[M_Z_MATE] = products((f_mate, mate_z_own))


def factor_own_kernel(kept, mate_terms, strips, peer_y, factor_own, *peer_term):
    peer_y_peer = split(peer_y[...])
    total = mate_terms[M_OWN] + products((split(peer_part(strips)), peer_y_peer))
    rows = lax.broadcasted_iota(jnp.int32, total.shape, 0)
    cols = lax.broadcasted_iota(jnp.int32, total.shape, 1)
    factor = jnp.where(rows == cols, 1.5, 0.0) + filtered(kept, total, OWN, -0.5)
    factor_own[...] = factor
    term = products((peer_y_peer, split(factor)))
    term = filtered(kept, term, 0, None, KEPT_PEER_AT, ROWS)
    size = term.shape[0] // ROWS
    for i, place in enumerate(peer_term):
        place[...] = term[i * size:(i + 1) * size]


Y_MATE, Z_MATE, Z_SIDE = range(3)
Y_OWN_PART, Y_SIDE_PART, Z_OWN_PART, Z_PEER_PART, PEER_PART = range(5)
Y_PEER, Y_OWN, Y_SIDE, PEER_Y, Z_PEER = range(5)


def middle_kernel(
    kept, y_peer, strips, mate, y_side, z_side, mate_terms,
    peer_y, from_side, factor_own, mate_factor,
    finished, partial, ready,
):
    def keep(at, parts):
        ready[at, 0], ready[at, 1] = parts

    y_to_mate, y_own, z_to_mate, z_own = (split(mate[at]) for at in range(4))
    y_to_peer, z_to_peer = split(y_peer[...]), split(peer_part(strips))
    y_to_side, z_to_side = split(y_side[...]), split(z_side[...])
    f_own = split(factor_own[...])
    keep(Y_OWN, y_own)
    keep(Y_SIDE, y_to_side)
    keep(Y_PEER, y_to_peer)
    keep(Z_PEER, z_to_peer)
    keep(PEER_Y, split(peer_y[...]))

    total = products((z_own, y_to_side), (z_to_side, split(from_side[0])))
    f_side = split(filtered(kept, total, SIDE, -0.5))
    partial[PEER_PART] = products((z_own, y_to_peer))
    partial[Y_SIDE_PART] = products((y_own, f_side))
    partial[Y_OWN_PART] = mate_terms[M_Y_OWN] + products((y_own, f_own))
    partial[Z_PEER_PART] = products((f_own, z_to_peer))
    partial[Z_OWN_PART] = mate_terms[M_Z_OWN] + products((f_own, z_own))
    value = mate_terms[M_Y_MATE] + products((y_to_mate, split(mate_factor[...])))
    finished[Y_MATE] = filtered(kept, value, MATE)
    value = mate_terms[M_Z_MATE] + products((f_own, z_to_mate))
    finished[Z_MATE] = filtered(kept, value, MATE)
    value = products((f_own, z_to_side), (f_side, split(from_side[1])))
    finished[Z_SIDE] = filtered(kept, value, SIDE)


class Writer:
    def __init__(self, slots, kept, result, sems):
        self.slots, self.kept, self.result, self.sems = slots, kept, result, sems
        self.started = []
        self.held = 0

    def write(self, source, out, region):
        size = out.shape[1]
        for i in range(ROWS):
            for j in range(ROWS):
                rows, cols = quarter(i, j, size)
                slot = self.slots[i * SLOTS + region * ROWS + j, 0]
                copy = pltpu.make_async_copy(
                    source.at[rows, cols],
                    out.at[i, :, pl.ds(pl.multiple_of(slot * size, size), size)],
                    self.sems.at[len(self.started)],
                )
                copy.start()
                self.started.append(copy)

    def finish(self, value, out, region):
        place = self.result.at[self.held]
        self.held += 1
        place[...] = filtered(self.kept, value, region)
        self.write(place, out, region)

    def wait(self):
        for copy in self.started:
            copy.wait()


def peer_kernel(
    slots, kept, finished, partial, ready, from_peer, peer_spread,
    sqrt_next, inverse_next, y_peer_part, result, sems,
):
    def held(at):
        return ready[at, 0], ready[at, 1]

    writer = Writer(slots, kept, result, sems)
    writer.write(finished.at[Y_MATE], sqrt_next, MATE)
    writer.write(finished.at[Z_MATE], inverse_next, MATE)
    writer.write(finished.at[Z_SIDE], inverse_next, SIDE)
    peer_y_own = split(own_part(from_peer[Y_BESIDE], peer_spread[0]))
    peer_z_own = split(own_part(from_peer[Z_BESIDE], peer_spread[1]))
    peer_z_peer = split(peer_part(from_peer))
    total = partial[PEER_PART] + products((held(Z_PEER), peer_y_own))
    f_peer = split(filtered(kept, total, PEER, -0.5))
    total = products((peer_z_own, held(PEER_Y)), (peer_z_peer, held(Y_OWN)))
    peer_f_peer = split(filtered(kept, total, 0, -0.5, KEPT_PEER_AT, ROWS))
    value = partial[Z_PEER_PART] + products((f_peer, peer_z_own))
    writer.finish(value, inverse_next, PEER)
    value = partial[Z_OWN_PART] + products((f_peer, peer_z_peer))
    writer.finish(value, inverse_next, OWN)
    value = partial[Y_OWN_PART] + products((held(Y_PEER), peer_f_peer))
    writer.finish(value, sqrt_next, OWN)
    y_peer_part[...] = filtered(kept, products((held(Y_OWN), f_peer)), PEER)
    writer.wait()


def side_kernel(slots, kept, partial, ready, factor, unfinished, sqrt_next, result, sems):
    left = (ready[Y_SIDE, 0], ready[Y_SIDE, 1])
    value = partial[Y_SIDE_PART] + products((left, split(factor[...])))
    writer = Writer(slots, kept, result, sems)
    writer.finish(value, sqrt_next, SIDE)
    writer.wait()


def last_kernel(i, slots, part, term, unfinished, sqrt_next, result, sems):
    size = sqrt_next.shape[1]
    copies = []
    starts = [slots[i * SLOTS + PEER * ROWS + j, 0] * size for j in range(ROWS)]
    for j in range(ROWS):
        rows, cols = quarter(i, j, size)
        result[j] = part[rows, cols] + term[:, cols]
        out = sqrt_next.at[i, :, pl.ds(pl.multiple_of(starts[j], size), size)]
        copies.append(pltpu.make_async_copy(result.at[j], out, sems.at[j]))
        copies[j].start()
    for copy in copies:
        copy.wait()


def call(
    kernel, outs, operands, micros=0, scratch=(), hbm_in=(), any_in=(), hbm_out=(), in_place=None
):
    def spec(space=pltpu.VMEM):
        return pl.BlockSpec(memory_space=space)

    operands = [
        pltpu.with_memory_space_constraint(array, pltpu.HBM) if at in hbm_in else array
        for at, array in enumerate(operands)
    ]
    return pl.pallas_call(
        kernel,
        out_shape=outs,
        in_specs=[
            spec(pltpu.HBM if at in hbm_in else pl.ANY if at in any_in else pltpu.VMEM)
            for at in range(len(operands))
        ],
        out_specs=tuple(
            spec(pltpu.HBM if at in hbm_out else pltpu.VMEM) for at in range(len(outs))
        ),
        scratch_shapes=scratch,
        input_output_aliases={} if in_place is None else {in_place: 0},
        compiler_params=pltpu.CompilerParams(vmem_limit_bytes=VMEM_LIMIT),
        cost_estimate=pl.CostEstimate(
            flops=int(micros * PEAK), bytes_accessed=0, transcendentals=0
        ),
    )(*operands)


def local(sqrt_iterate, inverse_iterate, pattern, keep_mask, row_order):
    rows_dev, block, width = sqrt_iterate.shape
    row_devices, col_devices = lax.axis_size("row"), lax.axis_size("col")
    assert rows_dev == ROWS and width == SLOTS * block and pattern.shape[1] == SLOTS
    assert row_devices > 3 and row_devices % 2 == 0 and col_devices > 2
    size = ROWS * block

    def to_mate(value):
        return lax.ppermute(value, "row", [(i, i ^ 1) for i in range(row_devices)])

    def to_peer(value):
        route = [(i, (i + (1 if i % 2 else -1)) % row_devices) for i in range(row_devices)]
        return lax.ppermute(value, "row", route)

    def to_side(value):
        route = [((i + 1) % col_devices, i) for i in range(col_devices)]
        return lax.ppermute(value, "col", route)

    def shape(*dims, dtype=jnp.float32):
        return jax.ShapeDtypeStruct(dims, dtype)

    one, pair = shape(size, size), shape(2, size, size)
    (diagonal,) = call(
        diagonal_kernel,
        (shape(2 * ROWS, block, block),),
        (sqrt_iterate, inverse_iterate),
        scratch=[pltpu.SemaphoreType.DMA((4 * ROWS,))],
        hbm_in=range(2),
    )
    peer_diagonal = to_peer(diagonal)
    slots, kept, y_peer, strips, mate, y_side, z_side, own_pair = call(
        functools.partial(pack_kernel, row_devices, col_devices),
        (
            shape(ROWS * SLOTS, block, dtype=jnp.int32), shape(KEPT_LINES, block),
            one, shape(ROWS + 2, block, size), shape(4, size, size), one, one, pair,
        ),
        (pattern.T, keep_mask.T, row_order, sqrt_iterate, inverse_iterate, diagonal),
        scratch=[
            pltpu.SMEM(pattern.T.shape, jnp.int32),
            pltpu.SMEM(keep_mask.T.shape, jnp.int32),
            pltpu.SMEM(row_order.shape, jnp.int32),
            pltpu.VMEM(sqrt_iterate.shape, jnp.float32),
            pltpu.VMEM(inverse_iterate.shape, jnp.float32),
            pltpu.SemaphoreType.DMA((5,)),
        ],
        hbm_in=range(5),
        any_in=(5,),
    )
    peer_y = to_peer(y_peer)
    from_peer = to_peer(strips)
    from_mate = to_mate(mate)
    from_side = to_side(own_pair)
    (peer_spread,) = call(spread_kernel, (pair,), (peer_diagonal,), micros=10)
    (mate_terms,) = call(
        mate_kernel,
        (shape(5, size, size),),
        (kept, mate, from_mate, peer_spread),
        any_in=(3,),
    )
    factor_own, *peer_term = call(
        factor_own_kernel, (one, *[shape(block, size)] * ROWS), (kept, mate_terms, strips, peer_y), micros=5
    )
    mate_factor = to_mate(factor_own)
    term = [to_peer(value) for value in peer_term]
    side_factor = to_side(factor_own)
    finished, partial, ready = call(
        middle_kernel,
        (
            shape(3, size, size), shape(5, size, size),
            shape(5, 2, size, size, dtype=jnp.bfloat16),
        ),
        (
            kept, y_peer, strips, mate, y_side, z_side, mate_terms,
            peer_y, from_side, factor_own, mate_factor,
        ),
    )
    output = shape(rows_dev, block, width)

    def writing(blocks):
        return [
            pltpu.VMEM((blocks, size, size), jnp.float32),
            pltpu.SemaphoreType.DMA((24,)),
        ]

    sqrt_next, inverse_next, y_peer_part = call(
        peer_kernel,
        (output, output, one),
        (slots, kept, finished, partial, ready, from_peer, peer_spread),
        scratch=writing(3),
        hbm_out=(0, 1),
    )
    (sqrt_next,) = call(
        side_kernel,
        (output,),
        (slots, kept, partial, ready, side_factor, sqrt_next),
        scratch=writing(1),
        hbm_in=(5,),
        hbm_out=(0,),
        in_place=5,
    )
    for i in range(ROWS):
        (sqrt_next,) = call(
            functools.partial(last_kernel, i),
            (output,),
            (slots, y_peer_part, term[i], sqrt_next),
            scratch=[
                pltpu.VMEM((ROWS, block, block), jnp.float32),
                pltpu.SemaphoreType.DMA((ROWS,)),
            ],
            hbm_in=(3,),
            hbm_out=(0,),
            in_place=3,
        )
    return sqrt_next, inverse_next


def solution(mesh):
    rows = P(("row", "col"), None, None)
    return jax.shard_map(
        local,
        mesh=mesh,
        in_specs=(rows, rows, P(), P(), P()),
        out_specs=(rows, rows),
        check_vma=False,
    )
```

```python
import functools

import jax
import jax.numpy as jnp
from jax import lax
from jax.experimental import pallas as pl
from jax.experimental.pallas import tpu as pltpu
from jax.sharding import PartitionSpec as P

PEER, OWN, MATE, SIDE = range(4)
ROWS = 2
SLOTS = 8
KEPT_PEER_AT, KEPT_MATE_AT, KEPT_LINES = 16, 20, 24
LARGEST = float(jnp.finfo(jnp.bfloat16).max)
VMEM_LIMIT = 24 * 2**20
PEAK = 1.153e9


def split(value):
    clipped = jnp.clip(value, -LARGEST, LARGEST)
    high = clipped.astype(jnp.bfloat16)
    low = (value - high.astype(jnp.float32)).astype(jnp.bfloat16)
    return high, low


def products(*pairs):
    left = [part for (high, low), _ in pairs for part in (high, low, high)]
    right = [part for _, (high, low) in pairs for part in (high, high, low)]
    return jnp.dot(
        jnp.concatenate(left, axis=1),
        jnp.concatenate(right, axis=0),
        preferred_element_type=jnp.float32,
    )


def filtered(kept, value, region, scale=None, base=0, width=SLOTS):
    size = value.shape[0] // ROWS
    rows = []
    for i in range(ROWS):
        row = []
        for j in range(ROWS):
            at = base + i * width + region * ROWS + j
            flag = kept[at:at + 1, :]
            if scale is not None:
                flag = flag * scale
            row.append(value[i * size:(i + 1) * size, j * size:(j + 1) * size] * flag)
        rows.append(jnp.concatenate(row, axis=1))
    return jnp.concatenate(rows, axis=0)


def neighbours(row_devices, col_devices, order):
    row = lax.axis_index("row")
    col = lax.axis_index("col")
    odd = lax.rem(row, 2)

    def first(row_of, col_of):
        return (lax.rem(row_of, row_devices) * col_devices + lax.rem(col_of, col_devices)) * ROWS

    starts = (
        first(row + row_devices - 1 + 2 * odd, col),
        first(row, col),
        first(row + 1 - 2 * odd, col),
        first(row, col + 1),
    )
    return starts, [order[start + j] for start in starts for j in range(ROWS)]


def find_slots(pattern, stored, wanted):
    slots = [jnp.int32(0)] * len(wanted)
    for k in range(SLOTS):
        label = pattern[k, stored]
        slots = [jnp.where(label == want, k, slot) for want, slot in zip(wanted, slots)]
    return slots


def look_up(row_devices, col_devices, pattern, keep, order, slots, kept):
    starts, labels = neighbours(row_devices, col_devices, order)
    own_labels = labels[OWN * ROWS:(OWN + 1) * ROWS]

    def write_flags(stored, found, line):
        for j, slot in enumerate(found):
            flag = ((slot == 0) | (keep[slot, stored] == 1)).astype(jnp.float32)
            kept[line + j:line + j + 1, :] = jnp.full((1, kept.shape[1]), flag)

    result = []
    for i in range(ROWS):
        found = find_slots(pattern, starts[OWN] + i, labels)
        result.append(found)
        for j, slot in enumerate(found):
            line = i * SLOTS + j
            slots[line:line + 1, :] = jnp.full((1, slots.shape[1]), slot)
        write_flags(starts[OWN] + i, found, i * SLOTS)
        for region, line in ((PEER, KEPT_PEER_AT), (MATE, KEPT_MATE_AT)):
            stored = starts[region] + i
            write_flags(stored, find_slots(pattern, stored, own_labels), line + i * ROWS)
    return result


def quarter(i, j, size):
    return slice(i * size, (i + 1) * size), slice(j * size, (j + 1) * size)


def gather(slot_of, source, places):
    size = source.shape[1]
    for region, region_places in places.items():
        for i in range(ROWS):
            for j in range(ROWS):
                start = pl.multiple_of(slot_of(i, region * ROWS + j) * size, size)
                block = source[i, :, pl.ds(start, size)]
                for place in region_places:
                    place(i, j, size, block)


def into(out):
    def place(i, j, size, block):
        rows, cols = quarter(i, j, size)
        out[rows, cols] = block

    return place


def strip_whole(out, at):
    def place(i, j, size, block):
        out[at + i, :, j * size:(j + 1) * size] = block

    return place


def strip_own(out, at):
    def place(i, j, size, block):
        if i != j:
            out[at, :, i * size:(i + 1) * size] = block

    return place


Y_BESIDE, Z_OWN, STRIPS = ROWS, ROWS + 1, 2 * ROWS + 1


def whole_part(strips, at=0):
    return jnp.concatenate([strips[at + i] for i in range(ROWS)], axis=0)


def own_part(beside, spread):
    size = beside.shape[0]
    return jnp.concatenate(
        [
            jnp.concatenate([spread[:size, :size], beside[:, :size]], axis=1),
            jnp.concatenate([beside[:, size:], spread[size:, size:]], axis=1),
        ],
        axis=0,
    )


def diagonal_kernel(sqrt_iterate, diagonal, sems):
    size = sqrt_iterate.shape[1]
    half = size // 2
    copies = []
    for i in range(ROWS):
        for rows in (pl.ds(0, half), pl.ds(half, half)):
            copies.append(
                pltpu.make_async_copy(
                    sqrt_iterate.at[i, rows, pl.ds(0, size)],
                    diagonal.at[i, rows],
                    sems.at[len(copies)],
                )
            )
            copies[-1].start()
    for copy in copies:
        copy.wait()


def pack_kernel(
    row_devices, col_devices, pattern, keep, order, sqrt_iterate, inverse_iterate, after,
    slots, kept, y_peer, strips, mate, y_side, z_side, to_side,
    pattern_here, keep_here, order_here, sqrt_here, inverse_here, sems,
):
    copies = [
        pltpu.make_async_copy(source, here, sems.at[at])
        for at, (source, here) in enumerate((
            (order, order_here), (pattern, pattern_here), (keep, keep_here),
            (sqrt_iterate, sqrt_here), (inverse_iterate, inverse_here),
        ))
    ]
    for copy in copies:
        copy.start()
    for copy in copies[:3]:
        copy.wait()
    found = look_up(
        row_devices, col_devices, pattern_here, keep_here, order_here, slots, kept
    )

    def slot_of(i, j):
        return found[i][j]

    copies[3].wait()
    places = {
        PEER: (into(y_peer),),
        OWN: (strip_own(strips, Y_BESIDE), into(mate.at[1]), into(to_side.at[0])),
        MATE: (into(mate.at[0]),),
        SIDE: (into(y_side),),
    }
    gather(slot_of, sqrt_here, places)
    copies[4].wait()
    places = {
        PEER: (strip_whole(strips, 0),),
        OWN: (strip_whole(strips, Z_OWN), into(mate.at[3]), into(to_side.at[1])),
        MATE: (into(mate.at[2]),),
        SIDE: (into(z_side),),
    }
    gather(slot_of, inverse_here, places)


def spread_kernel(diagonal, spread):
    size = diagonal.shape[1]
    for i in range(ROWS):
        for j in range(ROWS):
            rows, cols = quarter(i, j, size)
            spread[rows, cols] = diagonal[i] if i == j else jnp.zeros_like(diagonal[i])


M_OWN, M_Y_OWN, M_Y_MATE, M_Z_OWN, M_Z_MATE = range(5)


def mate_kernel(kept, mate, from_mate, after, mate_terms):
    y_to_mate, y_own, z_to_mate, z_own = (split(mate[at]) for at in range(4))
    mate_y_mate, mate_y_own, mate_z_mate, mate_z_own = (split(from_mate[at]) for at in range(4))
    mate_terms[M_OWN] = products((z_own, y_own), (z_to_mate, mate_y_mate))
    total = products((z_own, y_to_mate), (z_to_mate, mate_y_own))
    f_mate = split(filtered(kept, total, MATE, -0.5))
    total = products((mate_z_own, mate_y_mate), (mate_z_mate, y_own))
    mate_f_mate = split(filtered(kept, total, 0, -0.5, KEPT_MATE_AT, ROWS))
    mate_terms[M_Y_OWN] = products((y_to_mate, mate_f_mate))
    mate_terms[M_Y_MATE] = products((y_own, f_mate))
    mate_terms[M_Z_OWN] = products((f_mate, mate_z_mate))
    mate_terms[M_Z_MATE] = products((f_mate, mate_z_own))


def factor_own_kernel(kept, mate_terms, strips, peer_y, factor_own, *peer_term):
    peer_y_peer = split(peer_y[...])
    total = mate_terms[M_OWN] + products((split(whole_part(strips)), peer_y_peer))
    rows = lax.broadcasted_iota(jnp.int32, total.shape, 0)
    cols = lax.broadcasted_iota(jnp.int32, total.shape, 1)
    factor = jnp.where(rows == cols, 1.5, 0.0) + filtered(kept, total, OWN, -0.5)
    factor_own[...] = factor
    term = products((peer_y_peer, split(factor)))
    term = filtered(kept, term, 0, None, KEPT_PEER_AT, ROWS)
    size = term.shape[0] // ROWS
    for i, place in enumerate(peer_term):
        place[...] = term[i * size:(i + 1) * size]


Y_MATE, Z_MATE, Z_SIDE = range(3)
Y_OWN_PART, Y_SIDE_PART, Z_OWN_PART, Z_PEER_PART, PEER_PART = range(5)
Y_PEER, Y_OWN, Y_SIDE, PEER_Y, Z_PEER = range(5)


def middle_kernel(
    kept, y_peer, strips, mate, y_side, z_side, mate_terms,
    peer_y, from_side, factor_own, mate_factor,
    finished, partial, ready,
):
    def keep(at, parts):
        ready[at, 0], ready[at, 1] = parts

    y_to_mate, y_own, z_to_mate, z_own = (split(mate[at]) for at in range(4))
    y_to_peer, z_to_peer = split(y_peer[...]), split(whole_part(strips))
    y_to_side, z_to_side = split(y_side[...]), split(z_side[...])
    f_own = split(factor_own[...])
    keep(Y_OWN, y_own)
    keep(Y_SIDE, y_to_side)
    keep(Y_PEER, y_to_peer)
    keep(Z_PEER, z_to_peer)
    keep(PEER_Y, split(peer_y[...]))

    total = products((z_own, y_to_side), (z_to_side, split(from_side[0])))
    f_side = split(filtered(kept, total, SIDE, -0.5))
    partial[PEER_PART] = products((z_own, y_to_peer))
    partial[Y_SIDE_PART] = products((y_own, f_side))
    partial[Y_OWN_PART] = mate_terms[M_Y_OWN] + products((y_own, f_own))
    partial[Z_PEER_PART] = products((f_own, z_to_peer))
    partial[Z_OWN_PART] = mate_terms[M_Z_OWN] + products((f_own, z_own))
    value = mate_terms[M_Y_MATE] + products((y_to_mate, split(mate_factor[...])))
    finished[Y_MATE] = filtered(kept, value, MATE)
    value = mate_terms[M_Z_MATE] + products((f_own, z_to_mate))
    finished[Z_MATE] = filtered(kept, value, MATE)
    value = products((f_own, z_to_side), (f_side, split(from_side[1])))
    finished[Z_SIDE] = filtered(kept, value, SIDE)


class Writer:
    def __init__(self, slots, kept, result, sems):
        self.slots, self.kept, self.result, self.sems = slots, kept, result, sems
        self.started = []
        self.held = 0

    def write(self, source, out, region):
        size = out.shape[1]
        for i in range(ROWS):
            for j in range(ROWS):
                rows, cols = quarter(i, j, size)
                slot = self.slots[i * SLOTS + region * ROWS + j, 0]
                copy = pltpu.make_async_copy(
                    source.at[rows, cols],
                    out.at[i, :, pl.ds(pl.multiple_of(slot * size, size), size)],
                    self.sems.at[len(self.started)],
                )
                copy.start()
                self.started.append(copy)

    def finish(self, value, out, region):
        place = self.result.at[self.held]
        self.held += 1
        place[...] = filtered(self.kept, value, region)
        self.write(place, out, region)

    def wait(self):
        for copy in self.started:
            copy.wait()


def peer_kernel(
    slots, kept, finished, partial, ready, from_peer, peer_spread,
    sqrt_next, inverse_next, y_peer_part, result, sems,
):
    def held(at):
        return ready[at, 0], ready[at, 1]

    writer = Writer(slots, kept, result, sems)
    writer.write(finished.at[Y_MATE], sqrt_next, MATE)
    writer.write(finished.at[Z_MATE], inverse_next, MATE)
    writer.write(finished.at[Z_SIDE], inverse_next, SIDE)
    peer_y_own = split(own_part(from_peer[Y_BESIDE], peer_spread))
    peer_z_own = split(whole_part(from_peer, Z_OWN))
    peer_z_peer = split(whole_part(from_peer))
    total = partial[PEER_PART] + products((held(Z_PEER), peer_y_own))
    f_peer = split(filtered(kept, total, PEER, -0.5))
    total = products((peer_z_own, held(PEER_Y)), (peer_z_peer, held(Y_OWN)))
    peer_f_peer = split(filtered(kept, total, 0, -0.5, KEPT_PEER_AT, ROWS))
    value = partial[Z_PEER_PART] + products((f_peer, peer_z_own))
    writer.finish(value, inverse_next, PEER)
    value = partial[Z_OWN_PART] + products((f_peer, peer_z_peer))
    writer.finish(value, inverse_next, OWN)
    value = partial[Y_OWN_PART] + products((held(Y_PEER), peer_f_peer))
    writer.finish(value, sqrt_next, OWN)
    y_peer_part[...] = filtered(kept, products((held(Y_OWN), f_peer)), PEER)
    writer.wait()


def side_kernel(slots, kept, partial, ready, factor, unfinished, sqrt_next, result, sems):
    left = (ready[Y_SIDE, 0], ready[Y_SIDE, 1])
    value = partial[Y_SIDE_PART] + products((left, split(factor[...])))
    writer = Writer(slots, kept, result, sems)
    writer.finish(value, sqrt_next, SIDE)
    writer.wait()


def last_kernel(i, slots, part, term, unfinished, sqrt_next, result, sems):
    size = sqrt_next.shape[1]
    copies = []
    starts = [slots[i * SLOTS + PEER * ROWS + j, 0] * size for j in range(ROWS)]
    for j in range(ROWS):
        rows, cols = quarter(i, j, size)
        result[j] = part[rows, cols] + term[:, cols]
        out = sqrt_next.at[i, :, pl.ds(pl.multiple_of(starts[j], size), size)]
        copies.append(pltpu.make_async_copy(result.at[j], out, sems.at[j]))
        copies[j].start()
    for copy in copies:
        copy.wait()


def call(
    kernel, outs, operands, micros=0, scratch=(), hbm_in=(), any_in=(), hbm_out=(), in_place=None
):
    def spec(space=pltpu.VMEM):
        return pl.BlockSpec(memory_space=space)

    operands = [
        pltpu.with_memory_space_constraint(array, pltpu.HBM) if at in hbm_in else array
        for at, array in enumerate(operands)
    ]
    return pl.pallas_call(
        kernel,
        out_shape=outs,
        in_specs=[
            spec(pltpu.HBM if at in hbm_in else pl.ANY if at in any_in else pltpu.VMEM)
            for at in range(len(operands))
        ],
        out_specs=tuple(
            spec(pltpu.HBM if at in hbm_out else pltpu.VMEM) for at in range(len(outs))
        ),
        scratch_shapes=scratch,
        input_output_aliases={} if in_place is None else {in_place: 0},
        compiler_params=pltpu.CompilerParams(vmem_limit_bytes=VMEM_LIMIT),
        cost_estimate=pl.CostEstimate(
            flops=int(micros * PEAK), bytes_accessed=0, transcendentals=0
        ),
    )(*operands)


def local(sqrt_iterate, inverse_iterate, pattern, keep_mask, row_order):
    rows_dev, block, width = sqrt_iterate.shape
    row_devices, col_devices = lax.axis_size("row"), lax.axis_size("col")
    assert rows_dev == ROWS and width == SLOTS * block and pattern.shape[1] == SLOTS
    assert row_devices > 3 and row_devices % 2 == 0 and col_devices > 2
    size = ROWS * block

    def to_mate(value):
        return lax.ppermute(value, "row", [(i, i ^ 1) for i in range(row_devices)])

    def to_peer(value):
        route = [(i, (i + (1 if i % 2 else -1)) % row_devices) for i in range(row_devices)]
        return lax.ppermute(value, "row", route)

    def to_side(value):
        route = [((i + 1) % col_devices, i) for i in range(col_devices)]
        return lax.ppermute(value, "col", route)

    def shape(*dims, dtype=jnp.float32):
        return jax.ShapeDtypeStruct(dims, dtype)

    one, pair = shape(size, size), shape(2, size, size)
    (diagonal,) = call(
        diagonal_kernel,
        (shape(ROWS, block, block),),
        (sqrt_iterate,),
        scratch=[pltpu.SemaphoreType.DMA((2 * ROWS,))],
        hbm_in=(0,),
    )
    peer_diagonal = to_peer(diagonal)
    slots, kept, y_peer, strips, mate, y_side, z_side, own_pair = call(
        functools.partial(pack_kernel, row_devices, col_devices),
        (
            shape(ROWS * SLOTS, block, dtype=jnp.int32), shape(KEPT_LINES, block),
            one, shape(STRIPS, block, size), shape(4, size, size), one, one, pair,
        ),
        (pattern.T, keep_mask.T, row_order, sqrt_iterate, inverse_iterate, diagonal),
        scratch=[
            pltpu.SMEM(pattern.T.shape, jnp.int32),
            pltpu.SMEM(keep_mask.T.shape, jnp.int32),
            pltpu.SMEM(row_order.shape, jnp.int32),
            pltpu.VMEM(sqrt_iterate.shape, jnp.float32),
            pltpu.VMEM(inverse_iterate.shape, jnp.float32),
            pltpu.SemaphoreType.DMA((5,)),
        ],
        hbm_in=range(5),
        any_in=(5,),
    )
    peer_y = to_peer(y_peer)
    from_peer = to_peer(strips)
    from_mate = to_mate(mate)
    from_side = to_side(own_pair)
    (peer_spread,) = call(spread_kernel, (one,), (peer_diagonal,), micros=10)
    (mate_terms,) = call(
        mate_kernel,
        (shape(5, size, size),),
        (kept, mate, from_mate, peer_spread),
        any_in=(3,),
    )
    factor_own, *peer_term = call(
        factor_own_kernel, (one, *[shape(block, size)] * ROWS), (kept, mate_terms, strips, peer_y), micros=5
    )
    mate_factor = to_mate(factor_own)
    term = [to_peer(value) for value in peer_term]
    side_factor = to_side(factor_own)
    finished, partial, ready = call(
        middle_kernel,
        (
            shape(3, size, size), shape(5, size, size),
            shape(5, 2, size, size, dtype=jnp.bfloat16),
        ),
        (
            kept, y_peer, strips, mate, y_side, z_side, mate_terms,
            peer_y, from_side, factor_own, mate_factor,
        ),
    )
    output = shape(rows_dev, block, width)

    def writing(blocks):
        return [
            pltpu.VMEM((blocks, size, size), jnp.float32),
            pltpu.SemaphoreType.DMA((24,)),
        ]

    sqrt_next, inverse_next, y_peer_part = call(
        peer_kernel,
        (output, output, one),
        (slots, kept, finished, partial, ready, from_peer, peer_spread),
        scratch=writing(3),
        hbm_out=(0, 1),
    )
    (sqrt_next,) = call(
        side_kernel,
        (output,),
        (slots, kept, partial, ready, side_factor, sqrt_next),
        scratch=writing(1),
        hbm_in=(5,),
        hbm_out=(0,),
        in_place=5,
    )
    for i in range(ROWS):
        (sqrt_next,) = call(
            functools.partial(last_kernel, i),
            (output,),
            (slots, y_peer_part, term[i], sqrt_next),
            scratch=[
                pltpu.VMEM((ROWS, block, block), jnp.float32),
                pltpu.SemaphoreType.DMA((ROWS,)),
            ],
            hbm_in=(3,),
            hbm_out=(0,),
            in_place=3,
        )
    return sqrt_next, inverse_next


def solution(mesh):
    rows = P(("row", "col"), None, None)
    return jax.shard_map(
        local,
        mesh=mesh,
        in_specs=(rows, rows, P(), P(), P()),
        out_specs=(rows, rows),
        check_vma=False,
    )
```

```python
import functools

import jax
import jax.numpy as jnp
from jax import lax
from jax.experimental import pallas as pl
from jax.experimental.pallas import tpu as pltpu
from jax.sharding import PartitionSpec as P

PEER, OWN, MATE, SIDE = range(4)
ROWS = 2
SLOTS = 8
KEPT_PEER_AT, KEPT_MATE_AT, KEPT_LINES = 16, 20, 24
LARGEST = float(jnp.finfo(jnp.bfloat16).max)
VMEM_LIMIT = 24 * 2**20
PEAK = 1.153e9


def split(value):
    clipped = jnp.clip(value, -LARGEST, LARGEST)
    high = clipped.astype(jnp.bfloat16)
    low = (value - high.astype(jnp.float32)).astype(jnp.bfloat16)
    return high, low


def products(*pairs):
    left = [part for (high, low), _ in pairs for part in (high, low, high)]
    right = [part for _, (high, low) in pairs for part in (high, high, low)]
    return jnp.dot(
        jnp.concatenate(left, axis=1),
        jnp.concatenate(right, axis=0),
        preferred_element_type=jnp.float32,
    )


def filtered(kept, value, region, scale=None, base=0, width=SLOTS):
    size = value.shape[0] // ROWS
    rows = []
    for i in range(ROWS):
        row = []
        for j in range(ROWS):
            at = base + i * width + region * ROWS + j
            flag = kept[at:at + 1, :]
            if scale is not None:
                flag = flag * scale
            row.append(value[i * size:(i + 1) * size, j * size:(j + 1) * size] * flag)
        rows.append(jnp.concatenate(row, axis=1))
    return jnp.concatenate(rows, axis=0)


def neighbours(row_devices, col_devices, order):
    row = lax.axis_index("row")
    col = lax.axis_index("col")
    odd = lax.rem(row, 2)

    def first(row_of, col_of):
        return (lax.rem(row_of, row_devices) * col_devices + lax.rem(col_of, col_devices)) * ROWS

    starts = (
        first(row + row_devices - 1 + 2 * odd, col),
        first(row, col),
        first(row + 1 - 2 * odd, col),
        first(row, col + 1),
    )
    return starts, [order[start + j] for start in starts for j in range(ROWS)]


def find_slots(pattern, stored, wanted):
    slots = [jnp.int32(0)] * len(wanted)
    for k in range(SLOTS):
        label = pattern[k, stored]
        slots = [jnp.where(label == want, k, slot) for want, slot in zip(wanted, slots)]
    return slots


def look_up(row_devices, col_devices, pattern, keep, order, slots, kept):
    starts, labels = neighbours(row_devices, col_devices, order)
    own_labels = labels[OWN * ROWS:(OWN + 1) * ROWS]

    def write_flags(stored, found, line):
        for j, slot in enumerate(found):
            flag = ((slot == 0) | (keep[slot, stored] == 1)).astype(jnp.float32)
            kept[line + j:line + j + 1, :] = jnp.full((1, kept.shape[1]), flag)

    result = []
    for i in range(ROWS):
        found = find_slots(pattern, starts[OWN] + i, labels)
        result.append(found)
        for j, slot in enumerate(found):
            line = i * SLOTS + j
            slots[line:line + 1, :] = jnp.full((1, slots.shape[1]), slot)
        write_flags(starts[OWN] + i, found, i * SLOTS)
        for region, line in ((PEER, KEPT_PEER_AT), (MATE, KEPT_MATE_AT)):
            stored = starts[region] + i
            write_flags(stored, find_slots(pattern, stored, own_labels), line + i * ROWS)
    return result


def quarter(i, j, size):
    return slice(i * size, (i + 1) * size), slice(j * size, (j + 1) * size)


def gather(slot_of, source, places):
    size = source.shape[1]
    for region, region_places in places.items():
        for i in range(ROWS):
            for j in range(ROWS):
                start = pl.multiple_of(slot_of(i, region * ROWS + j) * size, size)
                block = source[i, :, pl.ds(start, size)]
                for place in region_places:
                    place(i, j, size, block)


def into(out):
    def place(i, j, size, block):
        rows, cols = quarter(i, j, size)
        out[rows, cols] = block

    return place


def strip_peer(out):
    def place(i, j, size, block):
        out[i, :, j * size:(j + 1) * size] = block

    return place


def strip_own(out, at):
    def place(i, j, size, block):
        if i != j:
            out[at, :, i * size:(i + 1) * size] = block

    return place


Y_BESIDE, Z_BESIDE = ROWS, ROWS + 1


def peer_part(strips):
    return jnp.concatenate([strips[i] for i in range(ROWS)], axis=0)


def own_part(beside, spread):
    size = beside.shape[0]
    return jnp.concatenate(
        [
            jnp.concatenate([spread[:size, :size], beside[:, :size]], axis=1),
            jnp.concatenate([beside[:, size:], spread[size:, size:]], axis=1),
        ],
        axis=0,
    )


def diagonal_kernel(sqrt_iterate, inverse_iterate, diagonal, sems):
    size = sqrt_iterate.shape[1]
    half = size // 2
    copies = []
    for source in (sqrt_iterate, inverse_iterate):
        for i in range(ROWS):
            block = len(copies) // 2
            for rows in (pl.ds(0, half), pl.ds(half, half)):
                copies.append(
                    pltpu.make_async_copy(
                        source.at[i, rows, pl.ds(0, size)],
                        diagonal.at[block, rows],
                        sems.at[len(copies)],
                    )
                )
                copies[-1].start()
    for copy in copies:
        copy.wait()


def pack_kernel(
    row_devices, col_devices, pattern, keep, order, sqrt_iterate, inverse_iterate, after,
    slots, kept, y_peer, strips, mate, y_side, z_side, to_side,
    pattern_here, keep_here, order_here, sqrt_here, inverse_here, sems,
):
    copies = [
        pltpu.make_async_copy(source, here, sems.at[at])
        for at, (source, here) in enumerate((
            (order, order_here), (pattern, pattern_here), (keep, keep_here),
            (sqrt_iterate, sqrt_here), (inverse_iterate, inverse_here),
        ))
    ]
    for copy in copies:
        copy.start()
    for copy in copies[:3]:
        copy.wait()
    found = look_up(
        row_devices, col_devices, pattern_here, keep_here, order_here, slots, kept
    )

    def slot_of(i, j):
        return found[i][j]

    copies[3].wait()
    places = {
        PEER: (into(y_peer),),
        OWN: (strip_own(strips, Y_BESIDE), into(mate.at[1]), into(to_side.at[0])),
        MATE: (into(mate.at[0]),),
        SIDE: (into(y_side),),
    }
    gather(slot_of, sqrt_here, places)
    copies[4].wait()
    places = {
        PEER: (strip_peer(strips),),
        OWN: (strip_own(strips, Z_BESIDE), into(mate.at[3]), into(to_side.at[1])),
        MATE: (into(mate.at[2]),),
        SIDE: (into(z_side),),
    }
    gather(slot_of, inverse_here, places)


def spread_kernel(diagonal, spread):
    size = diagonal.shape[1]
    for at in range(2):
        for i in range(ROWS):
            for j in range(ROWS):
                rows, cols = quarter(i, j, size)
                block = diagonal[at * ROWS + i]
                spread[at, rows, cols] = block if i == j else jnp.zeros_like(block)


M_OWN, M_Y_OWN, M_Y_MATE, M_Z_OWN, M_Z_MATE = range(5)


def mate_kernel(kept, mate, from_mate, after, mate_terms):
    y_to_mate, y_own, z_to_mate, z_own = (split(mate[at]) for at in range(4))
    mate_y_mate, mate_y_own, mate_z_mate, mate_z_own = (split(from_mate[at]) for at in range(4))
    mate_terms[M_OWN] = products((z_own, y_own), (z_to_mate, mate_y_mate))
    total = products((z_own, y_to_mate), (z_to_mate, mate_y_own))
    f_mate = split(filtered(kept, total, MATE, -0.5))
    total = products((mate_z_own, mate_y_mate), (mate_z_mate, y_own))
    mate_f_mate = split(filtered(kept, total, 0, -0.5, KEPT_MATE_AT, ROWS))
    mate_terms[M_Y_OWN] = products((y_to_mate, mate_f_mate))
    mate_terms[M_Y_MATE] = products((y_own, f_mate))
    mate_terms[M_Z_OWN] = products((f_mate, mate_z_mate))
    mate_terms[M_Z_MATE] = products((f_mate, mate_z_own))


def factor_own_kernel(kept, mate_terms, strips, peer_y, factor_own, *peer_term):
    peer_y_peer = split(peer_y[...])
    total = mate_terms[M_OWN] + products((split(peer_part(strips)), peer_y_peer))
    rows = lax.broadcasted_iota(jnp.int32, total.shape, 0)
    cols = lax.broadcasted_iota(jnp.int32, total.shape, 1)
    factor = jnp.where(rows == cols, 1.5, 0.0) + filtered(kept, total, OWN, -0.5)
    factor_own[...] = factor
    term = products((peer_y_peer, split(factor)))
    term = filtered(kept, term, 0, None, KEPT_PEER_AT, ROWS)
    size = term.shape[0] // ROWS
    for i, place in enumerate(peer_term):
        place[...] = term[i * size:(i + 1) * size]


Y_MATE, Z_MATE, Z_SIDE = range(3)
Y_OWN_PART, Y_SIDE_PART, Z_OWN_PART, Z_PEER_PART, PEER_PART = range(5)
Y_PEER, Y_OWN, Y_SIDE, PEER_Y, Z_PEER = range(5)


def middle_kernel(
    kept, y_peer, strips, mate, y_side, z_side, mate_terms,
    peer_y, from_side, factor_own, mate_factor,
    finished, partial, ready,
):
    def keep(at, parts):
        ready[at, 0], ready[at, 1] = parts

    y_to_mate, y_own, z_to_mate, z_own = (split(mate[at]) for at in range(4))
    y_to_peer, z_to_peer = split(y_peer[...]), split(peer_part(strips))
    y_to_side, z_to_side = split(y_side[...]), split(z_side[...])
    f_own = split(factor_own[...])
    keep(Y_OWN, y_own)
    keep(Y_SIDE, y_to_side)
    keep(Y_PEER, y_to_peer)
    keep(Z_PEER, z_to_peer)
    keep(PEER_Y, split(peer_y[...]))

    total = products((z_own, y_to_side), (z_to_side, split(from_side[0])))
    f_side = split(filtered(kept, total, SIDE, -0.5))
    partial[PEER_PART] = products((z_own, y_to_peer))
    partial[Y_SIDE_PART] = products((y_own, f_side))
    partial[Y_OWN_PART] = mate_terms[M_Y_OWN] + products((y_own, f_own))
    partial[Z_PEER_PART] = products((f_own, z_to_peer))
    partial[Z_OWN_PART] = mate_terms[M_Z_OWN] + products((f_own, z_own))
    value = mate_terms[M_Y_MATE] + products((y_to_mate, split(mate_factor[...])))
    finished[Y_MATE] = filtered(kept, value, MATE)
    value = mate_terms[M_Z_MATE] + products((f_own, z_to_mate))
    finished[Z_MATE] = filtered(kept, value, MATE)
    value = products((f_own, z_to_side), (f_side, split(from_side[1])))
    finished[Z_SIDE] = filtered(kept, value, SIDE)


class Writer:
    def __init__(self, slots, kept, result, sems):
        self.slots, self.kept, self.result, self.sems = slots, kept, result, sems
        self.started = []
        self.held = 0

    def write(self, source, out, region):
        size = out.shape[1]
        for i in range(ROWS):
            for j in range(ROWS):
                rows, cols = quarter(i, j, size)
                slot = self.slots[i * SLOTS + region * ROWS + j, 0]
                copy = pltpu.make_async_copy(
                    source.at[rows, cols],
                    out.at[i, :, pl.ds(pl.multiple_of(slot * size, size), size)],
                    self.sems.at[len(self.started)],
                )
                copy.start()
                self.started.append(copy)

    def finish(self, value, out, region):
        place = self.result.at[self.held]
        self.held += 1
        place[...] = filtered(self.kept, value, region)
        self.write(place, out, region)

    def wait(self):
        for copy in self.started:
            copy.wait()


def peer_kernel(
    slots, kept, finished, partial, ready, from_peer, peer_spread,
    sqrt_next, inverse_next, y_peer_part, result, sems,
):
    def held(at):
        return ready[at, 0], ready[at, 1]

    writer = Writer(slots, kept, result, sems)
    writer.write(finished.at[Y_MATE], sqrt_next, MATE)
    writer.write(finished.at[Z_MATE], inverse_next, MATE)
    writer.write(finished.at[Z_SIDE], inverse_next, SIDE)
    peer_y_own = split(own_part(from_peer[Y_BESIDE], peer_spread[0]))
    peer_z_own = split(own_part(from_peer[Z_BESIDE], peer_spread[1]))
    peer_z_peer = split(peer_part(from_peer))
    total = partial[PEER_PART] + products((held(Z_PEER), peer_y_own))
    f_peer = split(filtered(kept, total, PEER, -0.5))
    total = products((peer_z_own, held(PEER_Y)), (peer_z_peer, held(Y_OWN)))
    peer_f_peer = split(filtered(kept, total, 0, -0.5, KEPT_PEER_AT, ROWS))
    value = partial[Z_PEER_PART] + products((f_peer, peer_z_own))
    writer.finish(value, inverse_next, PEER)
    value = partial[Z_OWN_PART] + products((f_peer, peer_z_peer))
    writer.finish(value, inverse_next, OWN)
    value = partial[Y_OWN_PART] + products((held(Y_PEER), peer_f_peer))
    writer.finish(value, sqrt_next, OWN)
    y_peer_part[...] = filtered(kept, products((held(Y_OWN), f_peer)), PEER)
    writer.wait()


def side_kernel(slots, kept, partial, ready, factor, unfinished, sqrt_next, result, sems):
    left = (ready[Y_SIDE, 0], ready[Y_SIDE, 1])
    value = partial[Y_SIDE_PART] + products((left, split(factor[...])))
    writer = Writer(slots, kept, result, sems)
    writer.finish(value, sqrt_next, SIDE)
    writer.wait()


def last_kernel(i, slots, part, term, unfinished, sqrt_next, result, sems):
    size = sqrt_next.shape[1]
    copies = []
    starts = [slots[i * SLOTS + PEER * ROWS + j, 0] * size for j in range(ROWS)]
    for j in range(ROWS):
        rows, cols = quarter(i, j, size)
        result[j] = part[rows, cols] + term[:, cols]
        out = sqrt_next.at[i, :, pl.ds(pl.multiple_of(starts[j], size), size)]
        copies.append(pltpu.make_async_copy(result.at[j], out, sems.at[j]))
        copies[j].start()
    for copy in copies:
        copy.wait()


def call(
    kernel, outs, operands, micros=0, scratch=(), hbm_in=(), any_in=(), hbm_out=(), in_place=None
):
    def spec(space=pltpu.VMEM):
        return pl.BlockSpec(memory_space=space)

    operands = [
        pltpu.with_memory_space_constraint(array, pltpu.HBM) if at in hbm_in else array
        for at, array in enumerate(operands)
    ]
    return pl.pallas_call(
        kernel,
        out_shape=outs,
        in_specs=[
            spec(pltpu.HBM if at in hbm_in else pl.ANY if at in any_in else pltpu.VMEM)
            for at in range(len(operands))
        ],
        out_specs=tuple(
            spec(pltpu.HBM if at in hbm_out else pltpu.VMEM) for at in range(len(outs))
        ),
        scratch_shapes=scratch,
        input_output_aliases={} if in_place is None else {in_place: 0},
        compiler_params=pltpu.CompilerParams(vmem_limit_bytes=VMEM_LIMIT),
        cost_estimate=pl.CostEstimate(
            flops=int(micros * PEAK), bytes_accessed=0, transcendentals=0
        ),
    )(*operands)


def local(sqrt_iterate, inverse_iterate, pattern, keep_mask, row_order):
    rows_dev, block, width = sqrt_iterate.shape
    row_devices, col_devices = lax.axis_size("row"), lax.axis_size("col")
    assert rows_dev == ROWS and width == SLOTS * block and pattern.shape[1] == SLOTS
    assert row_devices > 3 and row_devices % 2 == 0 and col_devices > 2
    size = ROWS * block

    def to_mate(value):
        return lax.ppermute(value, "row", [(i, i ^ 1) for i in range(row_devices)])

    def to_peer(value):
        route = [(i, (i + (1 if i % 2 else -1)) % row_devices) for i in range(row_devices)]
        return lax.ppermute(value, "row", route)

    def to_side(value):
        route = [((i + 1) % col_devices, i) for i in range(col_devices)]
        return lax.ppermute(value, "col", route)

    def shape(*dims, dtype=jnp.float32):
        return jax.ShapeDtypeStruct(dims, dtype)

    one, pair = shape(size, size), shape(2, size, size)
    (diagonal,) = call(
        diagonal_kernel,
        (pltpu.HBM((2 * ROWS, block, block), jnp.float32),),
        (sqrt_iterate, inverse_iterate),
        scratch=[pltpu.SemaphoreType.DMA((4 * ROWS,))],
        hbm_in=range(2),
        hbm_out=(0,),
    )
    peer_diagonal = to_peer(diagonal)
    slots, kept, y_peer, strips, mate, y_side, z_side, own_pair = call(
        functools.partial(pack_kernel, row_devices, col_devices),
        (
            shape(ROWS * SLOTS, block, dtype=jnp.int32), shape(KEPT_LINES, block),
            one, shape(ROWS + 2, block, size), shape(4, size, size), one, one, pair,
        ),
        (pattern.T, keep_mask.T, row_order, sqrt_iterate, inverse_iterate, diagonal),
        scratch=[
            pltpu.SMEM(pattern.T.shape, jnp.int32),
            pltpu.SMEM(keep_mask.T.shape, jnp.int32),
            pltpu.SMEM(row_order.shape, jnp.int32),
            pltpu.VMEM(sqrt_iterate.shape, jnp.float32),
            pltpu.VMEM(inverse_iterate.shape, jnp.float32),
            pltpu.SemaphoreType.DMA((5,)),
        ],
        hbm_in=range(6),
    )
    peer_y = to_peer(y_peer)
    from_peer = to_peer(strips)
    from_mate = to_mate(mate)
    from_side = to_side(own_pair)
    (peer_spread,) = call(spread_kernel, (pair,), (peer_diagonal,), micros=10)
    (mate_terms,) = call(
        mate_kernel,
        (shape(5, size, size),),
        (kept, mate, from_mate, peer_spread),
        any_in=(3,),
    )
    factor_own, *peer_term = call(
        factor_own_kernel, (one, *[shape(block, size)] * ROWS), (kept, mate_terms, strips, peer_y), micros=5
    )
    mate_factor = to_mate(factor_own)
    term = [to_peer(value) for value in peer_term]
    side_factor = to_side(factor_own)
    finished, partial, ready = call(
        middle_kernel,
        (
            shape(3, size, size), shape(5, size, size),
            shape(5, 2, size, size, dtype=jnp.bfloat16),
        ),
        (
            kept, y_peer, strips, mate, y_side, z_side, mate_terms,
            peer_y, from_side, factor_own, mate_factor,
        ),
    )
    output = shape(rows_dev, block, width)

    def writing(blocks):
        return [
            pltpu.VMEM((blocks, size, size), jnp.float32),
            pltpu.SemaphoreType.DMA((24,)),
        ]

    sqrt_next, inverse_next, y_peer_part = call(
        peer_kernel,
        (output, output, one),
        (slots, kept, finished, partial, ready, from_peer, peer_spread),
        scratch=writing(3),
        hbm_out=(0, 1),
    )
    (sqrt_next,) = call(
        side_kernel,
        (output,),
        (slots, kept, partial, ready, side_factor, sqrt_next),
        scratch=writing(1),
        hbm_in=(5,),
        hbm_out=(0,),
        in_place=5,
    )
    for i in range(ROWS):
        (sqrt_next,) = call(
            functools.partial(last_kernel, i),
            (output,),
            (slots, y_peer_part, term[i], sqrt_next),
            scratch=[
                pltpu.VMEM((ROWS, block, block), jnp.float32),
                pltpu.SemaphoreType.DMA((ROWS,)),
            ],
            hbm_in=(3,),
            hbm_out=(0,),
            in_place=3,
        )
    return sqrt_next, inverse_next


def solution(mesh):
    rows = P(("row", "col"), None, None)
    return jax.shard_map(
        local,
        mesh=mesh,
        in_specs=(rows, rows, P(), P(), P()),
        out_specs=(rows, rows),
        check_vma=False,
    )
```

```python
import functools

import jax
import jax.numpy as jnp
from jax import lax
from jax.experimental import pallas as pl
from jax.experimental.pallas import tpu as pltpu
from jax.sharding import PartitionSpec as P

PEER, OWN, MATE, SIDE = range(4)
ROWS = 2
SLOTS = 8
PIECES = 4
KEPT_PEER_AT, KEPT_MATE_AT, KEPT_LINES = 16, 20, 24
LARGEST = float(jnp.finfo(jnp.bfloat16).max)
VMEM_LIMIT = 24 * 2**20
PEAK = 1.153e9


def split(value):
    clipped = jnp.clip(value, -LARGEST, LARGEST)
    high = clipped.astype(jnp.bfloat16)
    low = (value - high.astype(jnp.float32)).astype(jnp.bfloat16)
    return high, low


def products(*pairs):
    left = [part for (high, low), _ in pairs for part in (high, low, high)]
    right = [part for _, (high, low) in pairs for part in (high, high, low)]
    return jnp.dot(
        jnp.concatenate(left, axis=1),
        jnp.concatenate(right, axis=0),
        preferred_element_type=jnp.float32,
    )


def filtered(kept, value, region, scale=None, base=0, width=SLOTS):
    size = value.shape[0] // ROWS
    rows = []
    for i in range(ROWS):
        row = []
        for j in range(ROWS):
            at = base + i * width + region * ROWS + j
            flag = kept[at:at + 1, :]
            if scale is not None:
                flag = flag * scale
            row.append(value[i * size:(i + 1) * size, j * size:(j + 1) * size] * flag)
        rows.append(jnp.concatenate(row, axis=1))
    return jnp.concatenate(rows, axis=0)


def neighbours(row_devices, col_devices, order):
    row = lax.axis_index("row")
    col = lax.axis_index("col")
    odd = lax.rem(row, 2)

    def first(row_of, col_of):
        return (lax.rem(row_of, row_devices) * col_devices + lax.rem(col_of, col_devices)) * ROWS

    starts = (
        first(row + row_devices - 1 + 2 * odd, col),
        first(row, col),
        first(row + 1 - 2 * odd, col),
        first(row, col + 1),
    )
    return starts, [order[start + j] for start in starts for j in range(ROWS)]


def find_slots(pattern, stored, wanted):
    slots = [jnp.int32(0)] * len(wanted)
    for k in range(SLOTS):
        label = pattern[k, stored]
        slots = [jnp.where(label == want, k, slot) for want, slot in zip(wanted, slots)]
    return slots


def look_up(row_devices, col_devices, pattern, keep, order, slots, kept):
    starts, labels = neighbours(row_devices, col_devices, order)
    own_labels = labels[OWN * ROWS:(OWN + 1) * ROWS]

    def write_flags(stored, found, line):
        for j, slot in enumerate(found):
            flag = ((slot == 0) | (keep[slot, stored] == 1)).astype(jnp.float32)
            kept[line + j:line + j + 1, :] = jnp.full((1, kept.shape[1]), flag)

    result = []
    for i in range(ROWS):
        found = find_slots(pattern, starts[OWN] + i, labels)
        result.append(found)
        for j, slot in enumerate(found):
            line = i * SLOTS + j
            slots[line:line + 1, :] = jnp.full((1, slots.shape[1]), slot)
        write_flags(starts[OWN] + i, found, i * SLOTS)
        for region, line in ((PEER, KEPT_PEER_AT), (MATE, KEPT_MATE_AT)):
            stored = starts[region] + i
            write_flags(stored, find_slots(pattern, stored, own_labels), line + i * ROWS)
    return result


def quarter(i, j, size):
    return slice(i * size, (i + 1) * size), slice(j * size, (j + 1) * size)


def gather(slot_of, source, places):
    size = source.shape[1]
    for region, region_places in places.items():
        for i in range(ROWS):
            for j in range(ROWS):
                start = pl.multiple_of(slot_of(i, region * ROWS + j) * size, size)
                block = source[i, :, pl.ds(start, size)]
                for place in region_places:
                    place(i, j, size, block)


def into(out):
    def place(i, j, size, block):
        rows, cols = quarter(i, j, size)
        out[rows, cols] = block

    return place


def strip_peer(out):
    def place(i, j, size, block):
        out[i, :, j * size:(j + 1) * size] = block

    return place


def strip_own(out, at):
    def place(i, j, size, block):
        if i != j:
            out[at, :, i * size:(i + 1) * size] = block

    return place


Y_BESIDE, Z_BESIDE = ROWS, ROWS + 1


def peer_part(strips):
    return jnp.concatenate([strips[i] for i in range(ROWS)], axis=0)


def own_part(beside, spread):
    size = beside.shape[0]
    return jnp.concatenate(
        [
            jnp.concatenate([spread[:size, :size], beside[:, :size]], axis=1),
            jnp.concatenate([beside[:, size:], spread[size:, size:]], axis=1),
        ],
        axis=0,
    )


def diagonal_kernel(sqrt_iterate, inverse_iterate, diagonal, sems):
    size = sqrt_iterate.shape[1]
    height = size // PIECES
    copies = []
    for source in (sqrt_iterate, inverse_iterate):
        for i in range(ROWS):
            block = len(copies) // PIECES
            for piece in range(PIECES):
                rows = pl.ds(piece * height, height)
                copies.append(
                    pltpu.make_async_copy(
                        source.at[i, rows, pl.ds(0, size)],
                        diagonal.at[block, rows],
                        sems.at[len(copies)],
                    )
                )
                copies[-1].start()
    for copy in copies:
        copy.wait()


def pack_kernel(
    row_devices, col_devices, pattern, keep, order, sqrt_iterate, inverse_iterate, after,
    slots, kept, y_peer, strips, mate, y_side, z_side, to_side,
    pattern_here, keep_here, order_here, sqrt_here, inverse_here, sems,
):
    copies = [
        pltpu.make_async_copy(source, here, sems.at[at])
        for at, (source, here) in enumerate((
            (order, order_here), (pattern, pattern_here), (keep, keep_here),
            (sqrt_iterate, sqrt_here), (inverse_iterate, inverse_here),
        ))
    ]
    for copy in copies:
        copy.start()
    for copy in copies[:3]:
        copy.wait()
    found = look_up(
        row_devices, col_devices, pattern_here, keep_here, order_here, slots, kept
    )

    def slot_of(i, j):
        return found[i][j]

    copies[3].wait()
    places = {
        PEER: (into(y_peer),),
        OWN: (strip_own(strips, Y_BESIDE), into(mate.at[1]), into(to_side.at[0])),
        MATE: (into(mate.at[0]),),
        SIDE: (into(y_side),),
    }
    gather(slot_of, sqrt_here, places)
    copies[4].wait()
    places = {
        PEER: (strip_peer(strips),),
        OWN: (strip_own(strips, Z_BESIDE), into(mate.at[3]), into(to_side.at[1])),
        MATE: (into(mate.at[2]),),
        SIDE: (into(z_side),),
    }
    gather(slot_of, inverse_here, places)


def spread_kernel(diagonal, spread):
    size = diagonal.shape[1]
    for at in range(2):
        for i in range(ROWS):
            for j in range(ROWS):
                rows, cols = quarter(i, j, size)
                block = diagonal[at * ROWS + i]
                spread[at, rows, cols] = block if i == j else jnp.zeros_like(block)


M_OWN, M_Y_OWN, M_Y_MATE, M_Z_OWN, M_Z_MATE = range(5)


def mate_kernel(kept, mate, from_mate, after, mate_terms):
    y_to_mate, y_own, z_to_mate, z_own = (split(mate[at]) for at in range(4))
    mate_y_mate, mate_y_own, mate_z_mate, mate_z_own = (split(from_mate[at]) for at in range(4))
    mate_terms[M_OWN] = products((z_own, y_own), (z_to_mate, mate_y_mate))
    total = products((z_own, y_to_mate), (z_to_mate, mate_y_own))
    f_mate = split(filtered(kept, total, MATE, -0.5))
    total = products((mate_z_own, mate_y_mate), (mate_z_mate, y_own))
    mate_f_mate = split(filtered(kept, total, 0, -0.5, KEPT_MATE_AT, ROWS))
    mate_terms[M_Y_OWN] = products((y_to_mate, mate_f_mate))
    mate_terms[M_Y_MATE] = products((y_own, f_mate))
    mate_terms[M_Z_OWN] = products((f_mate, mate_z_mate))
    mate_terms[M_Z_MATE] = products((f_mate, mate_z_own))


def factor_own_kernel(kept, mate_terms, strips, peer_y, factor_own, *peer_term):
    peer_y_peer = split(peer_y[...])
    total = mate_terms[M_OWN] + products((split(peer_part(strips)), peer_y_peer))
    rows = lax.broadcasted_iota(jnp.int32, total.shape, 0)
    cols = lax.broadcasted_iota(jnp.int32, total.shape, 1)
    factor = jnp.where(rows == cols, 1.5, 0.0) + filtered(kept, total, OWN, -0.5)
    factor_own[...] = factor
    term = products((peer_y_peer, split(factor)))
    term = filtered(kept, term, 0, None, KEPT_PEER_AT, ROWS)
    size = term.shape[0] // ROWS
    for i, place in enumerate(peer_term):
        place[...] = term[i * size:(i + 1) * size]


Y_MATE, Z_MATE, Z_SIDE = range(3)
Y_OWN_PART, Y_SIDE_PART, Z_OWN_PART, Z_PEER_PART, PEER_PART = range(5)
Y_PEER, Y_OWN, Y_SIDE, PEER_Y, Z_PEER = range(5)


def middle_kernel(
    kept, y_peer, strips, mate, y_side, z_side, mate_terms,
    peer_y, from_side, factor_own, mate_factor,
    finished, partial, ready,
):
    def keep(at, parts):
        ready[at, 0], ready[at, 1] = parts

    y_to_mate, y_own, z_to_mate, z_own = (split(mate[at]) for at in range(4))
    y_to_peer, z_to_peer = split(y_peer[...]), split(peer_part(strips))
    y_to_side, z_to_side = split(y_side[...]), split(z_side[...])
    f_own = split(factor_own[...])
    keep(Y_OWN, y_own)
    keep(Y_SIDE, y_to_side)
    keep(Y_PEER, y_to_peer)
    keep(Z_PEER, z_to_peer)
    keep(PEER_Y, split(peer_y[...]))

    total = products((z_own, y_to_side), (z_to_side, split(from_side[0])))
    f_side = split(filtered(kept, total, SIDE, -0.5))
    partial[PEER_PART] = products((z_own, y_to_peer))
    partial[Y_SIDE_PART] = products((y_own, f_side))
    partial[Y_OWN_PART] = mate_terms[M_Y_OWN] + products((y_own, f_own))
    partial[Z_PEER_PART] = products((f_own, z_to_peer))
    partial[Z_OWN_PART] = mate_terms[M_Z_OWN] + products((f_own, z_own))
    value = mate_terms[M_Y_MATE] + products((y_to_mate, split(mate_factor[...])))
    finished[Y_MATE] = filtered(kept, value, MATE)
    value = mate_terms[M_Z_MATE] + products((f_own, z_to_mate))
    finished[Z_MATE] = filtered(kept, value, MATE)
    value = products((f_own, z_to_side), (f_side, split(from_side[1])))
    finished[Z_SIDE] = filtered(kept, value, SIDE)


class Writer:
    def __init__(self, slots, kept, result, sems):
        self.slots, self.kept, self.result, self.sems = slots, kept, result, sems
        self.started = []
        self.held = 0

    def write(self, source, out, region):
        size = out.shape[1]
        for i in range(ROWS):
            for j in range(ROWS):
                rows, cols = quarter(i, j, size)
                slot = self.slots[i * SLOTS + region * ROWS + j, 0]
                copy = pltpu.make_async_copy(
                    source.at[rows, cols],
                    out.at[i, :, pl.ds(pl.multiple_of(slot * size, size), size)],
                    self.sems.at[len(self.started)],
                )
                copy.start()
                self.started.append(copy)

    def finish(self, value, out, region):
        place = self.result.at[self.held]
        self.held += 1
        place[...] = filtered(self.kept, value, region)
        self.write(place, out, region)

    def wait(self):
        for copy in self.started:
            copy.wait()


def peer_kernel(
    slots, kept, finished, partial, ready, from_peer, peer_spread,
    sqrt_next, inverse_next, y_peer_part, result, sems,
):
    def held(at):
        return ready[at, 0], ready[at, 1]

    writer = Writer(slots, kept, result, sems)
    writer.write(finished.at[Y_MATE], sqrt_next, MATE)
    writer.write(finished.at[Z_MATE], inverse_next, MATE)
    writer.write(finished.at[Z_SIDE], inverse_next, SIDE)
    peer_y_own = split(own_part(from_peer[Y_BESIDE], peer_spread[0]))
    peer_z_own = split(own_part(from_peer[Z_BESIDE], peer_spread[1]))
    peer_z_peer = split(peer_part(from_peer))
    total = partial[PEER_PART] + products((held(Z_PEER), peer_y_own))
    f_peer = split(filtered(kept, total, PEER, -0.5))
    total = products((peer_z_own, held(PEER_Y)), (peer_z_peer, held(Y_OWN)))
    peer_f_peer = split(filtered(kept, total, 0, -0.5, KEPT_PEER_AT, ROWS))
    value = partial[Z_PEER_PART] + products((f_peer, peer_z_own))
    writer.finish(value, inverse_next, PEER)
    value = partial[Z_OWN_PART] + products((f_peer, peer_z_peer))
    writer.finish(value, inverse_next, OWN)
    value = partial[Y_OWN_PART] + products((held(Y_PEER), peer_f_peer))
    writer.finish(value, sqrt_next, OWN)
    y_peer_part[...] = filtered(kept, products((held(Y_OWN), f_peer)), PEER)
    writer.wait()


def side_kernel(slots, kept, partial, ready, factor, unfinished, sqrt_next, result, sems):
    left = (ready[Y_SIDE, 0], ready[Y_SIDE, 1])
    value = partial[Y_SIDE_PART] + products((left, split(factor[...])))
    writer = Writer(slots, kept, result, sems)
    writer.finish(value, sqrt_next, SIDE)
    writer.wait()


def last_kernel(i, slots, part, term, unfinished, sqrt_next, result, sems):
    size = sqrt_next.shape[1]
    copies = []
    starts = [slots[i * SLOTS + PEER * ROWS + j, 0] * size for j in range(ROWS)]
    for j in range(ROWS):
        rows, cols = quarter(i, j, size)
        result[j] = part[rows, cols] + term[:, cols]
        out = sqrt_next.at[i, :, pl.ds(pl.multiple_of(starts[j], size), size)]
        copies.append(pltpu.make_async_copy(result.at[j], out, sems.at[j]))
        copies[j].start()
    for copy in copies:
        copy.wait()


def call(
    kernel, outs, operands, micros=0, scratch=(), hbm_in=(), any_in=(), hbm_out=(), in_place=None
):
    def spec(space=pltpu.VMEM):
        return pl.BlockSpec(memory_space=space)

    operands = [
        pltpu.with_memory_space_constraint(array, pltpu.HBM) if at in hbm_in else array
        for at, array in enumerate(operands)
    ]
    return pl.pallas_call(
        kernel,
        out_shape=outs,
        in_specs=[
            spec(pltpu.HBM if at in hbm_in else pl.ANY if at in any_in else pltpu.VMEM)
            for at in range(len(operands))
        ],
        out_specs=tuple(
            spec(pltpu.HBM if at in hbm_out else pltpu.VMEM) for at in range(len(outs))
        ),
        scratch_shapes=scratch,
        input_output_aliases={} if in_place is None else {in_place: 0},
        compiler_params=pltpu.CompilerParams(vmem_limit_bytes=VMEM_LIMIT),
        cost_estimate=pl.CostEstimate(
            flops=int(micros * PEAK), bytes_accessed=0, transcendentals=0
        ),
    )(*operands)


def local(sqrt_iterate, inverse_iterate, pattern, keep_mask, row_order):
    rows_dev, block, width = sqrt_iterate.shape
    row_devices, col_devices = lax.axis_size("row"), lax.axis_size("col")
    assert rows_dev == ROWS and width == SLOTS * block and pattern.shape[1] == SLOTS
    assert row_devices > 3 and row_devices % 2 == 0 and col_devices > 2
    size = ROWS * block

    def to_mate(value):
        return lax.ppermute(value, "row", [(i, i ^ 1) for i in range(row_devices)])

    def to_peer(value):
        route = [(i, (i + (1 if i % 2 else -1)) % row_devices) for i in range(row_devices)]
        return lax.ppermute(value, "row", route)

    def to_side(value):
        route = [((i + 1) % col_devices, i) for i in range(col_devices)]
        return lax.ppermute(value, "col", route)

    def shape(*dims, dtype=jnp.float32):
        return jax.ShapeDtypeStruct(dims, dtype)

    one, pair = shape(size, size), shape(2, size, size)
    (diagonal,) = call(
        diagonal_kernel,
        (shape(2 * ROWS, block, block),),
        (sqrt_iterate, inverse_iterate),
        scratch=[pltpu.SemaphoreType.DMA((2 * ROWS * PIECES,))],
        hbm_in=range(2),
    )
    peer_diagonal = to_peer(diagonal)
    slots, kept, y_peer, strips, mate, y_side, z_side, own_pair = call(
        functools.partial(pack_kernel, row_devices, col_devices),
        (
            shape(ROWS * SLOTS, block, dtype=jnp.int32), shape(KEPT_LINES, block),
            one, shape(ROWS + 2, block, size), shape(4, size, size), one, one, pair,
        ),
        (pattern.T, keep_mask.T, row_order, sqrt_iterate, inverse_iterate, diagonal),
        scratch=[
            pltpu.SMEM(pattern.T.shape, jnp.int32),
            pltpu.SMEM(keep_mask.T.shape, jnp.int32),
            pltpu.SMEM(row_order.shape, jnp.int32),
            pltpu.VMEM(sqrt_iterate.shape, jnp.float32),
            pltpu.VMEM(inverse_iterate.shape, jnp.float32),
            pltpu.SemaphoreType.DMA((5,)),
        ],
        hbm_in=range(5),
        any_in=(5,),
    )
    peer_y = to_peer(y_peer)
    from_peer = to_peer(strips)
    from_mate = to_mate(mate)
    from_side = to_side(own_pair)
    (peer_spread,) = call(spread_kernel, (pair,), (peer_diagonal,), micros=10)
    (mate_terms,) = call(
        mate_kernel,
        (shape(5, size, size),),
        (kept, mate, from_mate, peer_spread),
        any_in=(3,),
    )
    factor_own, *peer_term = call(
        factor_own_kernel, (one, *[shape(block, size)] * ROWS), (kept, mate_terms, strips, peer_y), micros=5
    )
    mate_factor = to_mate(factor_own)
    term = [to_peer(value) for value in peer_term]
    side_factor = to_side(factor_own)
    finished, partial, ready = call(
        middle_kernel,
        (
            shape(3, size, size), shape(5, size, size),
            shape(5, 2, size, size, dtype=jnp.bfloat16),
        ),
        (
            kept, y_peer, strips, mate, y_side, z_side, mate_terms,
            peer_y, from_side, factor_own, mate_factor,
        ),
    )
    output = shape(rows_dev, block, width)

    def writing(blocks):
        return [
            pltpu.VMEM((blocks, size, size), jnp.float32),
            pltpu.SemaphoreType.DMA((24,)),
        ]

    sqrt_next, inverse_next, y_peer_part = call(
        peer_kernel,
        (output, output, one),
        (slots, kept, finished, partial, ready, from_peer, peer_spread),
        scratch=writing(3),
        hbm_out=(0, 1),
    )
    (sqrt_next,) = call(
        side_kernel,
        (output,),
        (slots, kept, partial, ready, side_factor, sqrt_next),
        scratch=writing(1),
        hbm_in=(5,),
        hbm_out=(0,),
        in_place=5,
    )
    for i in range(ROWS):
        (sqrt_next,) = call(
            functools.partial(last_kernel, i),
            (output,),
            (slots, y_peer_part, term[i], sqrt_next),
            scratch=[
                pltpu.VMEM((ROWS, block, block), jnp.float32),
                pltpu.SemaphoreType.DMA((ROWS,)),
            ],
            hbm_in=(3,),
            hbm_out=(0,),
            in_place=3,
        )
    return sqrt_next, inverse_next


def solution(mesh):
    rows = P(("row", "col"), None, None)
    return jax.shard_map(
        local,
        mesh=mesh,
        in_specs=(rows, rows, P(), P(), P()),
        out_specs=(rows, rows),
        check_vma=False,
    )
```

```python
import functools

import jax
import jax.numpy as jnp
from jax import lax
from jax.experimental import pallas as pl
from jax.experimental.pallas import tpu as pltpu
from jax.sharding import PartitionSpec as P

PEER, OWN, MATE, SIDE = range(4)
ROWS = 2
SLOTS = 8
KEPT_PEER_AT, KEPT_MATE_AT, KEPT_LINES = 16, 20, 24
LARGEST = float(jnp.finfo(jnp.bfloat16).max)
VMEM_LIMIT = 24 * 2**20
PEAK = 1.153e9


def split(value):
    clipped = jnp.clip(value, -LARGEST, LARGEST)
    high = clipped.astype(jnp.bfloat16)
    low = (value - high.astype(jnp.float32)).astype(jnp.bfloat16)
    return high, low


def products(*pairs):
    left = [part for (high, low), _ in pairs for part in (high, low, high)]
    right = [part for _, (high, low) in pairs for part in (high, high, low)]
    return jnp.dot(
        jnp.concatenate(left, axis=1),
        jnp.concatenate(right, axis=0),
        preferred_element_type=jnp.float32,
    )


def filtered(kept, value, region, scale=None, base=0, width=SLOTS):
    size = value.shape[0] // ROWS
    rows = []
    for i in range(ROWS):
        row = []
        for j in range(ROWS):
            at = base + i * width + region * ROWS + j
            flag = kept[at:at + 1, :]
            if scale is not None:
                flag = flag * scale
            row.append(value[i * size:(i + 1) * size, j * size:(j + 1) * size] * flag)
        rows.append(jnp.concatenate(row, axis=1))
    return jnp.concatenate(rows, axis=0)


def neighbours(row_devices, col_devices, order):
    row = lax.axis_index("row")
    col = lax.axis_index("col")
    odd = lax.rem(row, 2)

    def first(row_of, col_of):
        return (lax.rem(row_of, row_devices) * col_devices + lax.rem(col_of, col_devices)) * ROWS

    starts = (
        first(row + row_devices - 1 + 2 * odd, col),
        first(row, col),
        first(row + 1 - 2 * odd, col),
        first(row, col + 1),
    )
    return starts, [order[start + j] for start in starts for j in range(ROWS)]


def find_slots(pattern, stored, wanted):
    slots = [jnp.int32(0)] * len(wanted)
    for k in range(SLOTS):
        label = pattern[k, stored]
        slots = [jnp.where(label == want, k, slot) for want, slot in zip(wanted, slots)]
    return slots


def look_up(row_devices, col_devices, pattern, keep, order, slots, kept):
    starts, labels = neighbours(row_devices, col_devices, order)
    own_labels = labels[OWN * ROWS:(OWN + 1) * ROWS]

    def write_flags(stored, found, line):
        for j, slot in enumerate(found):
            flag = ((slot == 0) | (keep[slot, stored] == 1)).astype(jnp.float32)
            kept[line + j:line + j + 1, :] = jnp.full((1, kept.shape[1]), flag)

    result = []
    for i in range(ROWS):
        found = find_slots(pattern, starts[OWN] + i, labels)
        result.append(found)
        for j, slot in enumerate(found):
            line = i * SLOTS + j
            slots[line:line + 1, :] = jnp.full((1, slots.shape[1]), slot)
        write_flags(starts[OWN] + i, found, i * SLOTS)
        for region, line in ((PEER, KEPT_PEER_AT), (MATE, KEPT_MATE_AT)):
            stored = starts[region] + i
            write_flags(stored, find_slots(pattern, stored, own_labels), line + i * ROWS)
    return result


def quarter(i, j, size):
    return slice(i * size, (i + 1) * size), slice(j * size, (j + 1) * size)


def gather(slot_of, source, places):
    size = source.shape[1]
    for region, region_places in places.items():
        for i in range(ROWS):
            for j in range(ROWS):
                start = pl.multiple_of(slot_of(i, region * ROWS + j) * size, size)
                block = source[i, :, pl.ds(start, size)]
                for place in region_places:
                    place(i, j, size, block)


def into(out):
    def place(i, j, size, block):
        rows, cols = quarter(i, j, size)
        out[rows, cols] = block

    return place


def strip_peer(out):
    def place(i, j, size, block):
        out[i, :, j * size:(j + 1) * size] = block

    return place


def strip_own(out, at):
    def place(i, j, size, block):
        if i != j:
            out[at, :, i * size:(i + 1) * size] = block

    return place


Y_BESIDE, Z_BESIDE = ROWS, ROWS + 1


def peer_part(strips):
    return jnp.concatenate([strips[i] for i in range(ROWS)], axis=0)


def own_part(beside, spread):
    size = beside.shape[0]
    return jnp.concatenate(
        [
            jnp.concatenate([spread[:size, :size], beside[:, :size]], axis=1),
            jnp.concatenate([beside[:, size:], spread[size:, size:]], axis=1),
        ],
        axis=0,
    )


def diagonal_kernel(sqrt_iterate, inverse_iterate, diagonal, sems):
    size = sqrt_iterate.shape[1]
    half = size // 2
    copies = []
    for i in range(ROWS):
        for at, source in enumerate((sqrt_iterate, inverse_iterate)):
            block = at * ROWS + i
            for rows in (pl.ds(0, half), pl.ds(half, half)):
                copies.append(
                    pltpu.make_async_copy(
                        source.at[i, rows, pl.ds(0, size)],
                        diagonal.at[block, rows],
                        sems.at[len(copies)],
                    )
                )
                copies[-1].start()
    for copy in copies:
        copy.wait()


def pack_kernel(
    row_devices, col_devices, pattern, keep, order, sqrt_iterate, inverse_iterate, after,
    slots, kept, y_peer, strips, mate, y_side, z_side, to_side,
    pattern_here, keep_here, order_here, sqrt_here, inverse_here, sems,
):
    copies = [
        pltpu.make_async_copy(source, here, sems.at[at])
        for at, (source, here) in enumerate((
            (order, order_here), (pattern, pattern_here), (keep, keep_here),
            (sqrt_iterate, sqrt_here), (inverse_iterate, inverse_here),
        ))
    ]
    for copy in copies:
        copy.start()
    for copy in copies[:3]:
        copy.wait()
    found = look_up(
        row_devices, col_devices, pattern_here, keep_here, order_here, slots, kept
    )

    def slot_of(i, j):
        return found[i][j]

    copies[3].wait()
    places = {
        PEER: (into(y_peer),),
        OWN: (strip_own(strips, Y_BESIDE), into(mate.at[1]), into(to_side.at[0])),
        MATE: (into(mate.at[0]),),
        SIDE: (into(y_side),),
    }
    gather(slot_of, sqrt_here, places)
    copies[4].wait()
    places = {
        PEER: (strip_peer(strips),),
        OWN: (strip_own(strips, Z_BESIDE), into(mate.at[3]), into(to_side.at[1])),
        MATE: (into(mate.at[2]),),
        SIDE: (into(z_side),),
    }
    gather(slot_of, inverse_here, places)


def spread_kernel(diagonal, spread):
    size = diagonal.shape[1]
    for at in range(2):
        for i in range(ROWS):
            for j in range(ROWS):
                rows, cols = quarter(i, j, size)
                block = diagonal[at * ROWS + i]
                spread[at, rows, cols] = block if i == j else jnp.zeros_like(block)


M_OWN, M_Y_OWN, M_Y_MATE, M_Z_OWN, M_Z_MATE = range(5)


def mate_kernel(kept, mate, from_mate, after, mate_terms):
    y_to_mate, y_own, z_to_mate, z_own = (split(mate[at]) for at in range(4))
    mate_y_mate, mate_y_own, mate_z_mate, mate_z_own = (split(from_mate[at]) for at in range(4))
    mate_terms[M_OWN] = products((z_own, y_own), (z_to_mate, mate_y_mate))
    total = products((z_own, y_to_mate), (z_to_mate, mate_y_own))
    f_mate = split(filtered(kept, total, MATE, -0.5))
    total = products((mate_z_own, mate_y_mate), (mate_z_mate, y_own))
    mate_f_mate = split(filtered(kept, total, 0, -0.5, KEPT_MATE_AT, ROWS))
    mate_terms[M_Y_OWN] = products((y_to_mate, mate_f_mate))
    mate_terms[M_Y_MATE] = products((y_own, f_mate))
    mate_terms[M_Z_OWN] = products((f_mate, mate_z_mate))
    mate_terms[M_Z_MATE] = products((f_mate, mate_z_own))


def factor_own_kernel(kept, mate_terms, strips, peer_y, factor_own, *peer_term):
    peer_y_peer = split(peer_y[...])
    total = mate_terms[M_OWN] + products((split(peer_part(strips)), peer_y_peer))
    rows = lax.broadcasted_iota(jnp.int32, total.shape, 0)
    cols = lax.broadcasted_iota(jnp.int32, total.shape, 1)
    factor = jnp.where(rows == cols, 1.5, 0.0) + filtered(kept, total, OWN, -0.5)
    factor_own[...] = factor
    term = products((peer_y_peer, split(factor)))
    term = filtered(kept, term, 0, None, KEPT_PEER_AT, ROWS)
    size = term.shape[0] // ROWS
    for i, place in enumerate(peer_term):
        place[...] = term[i * size:(i + 1) * size]


Y_MATE, Z_MATE, Z_SIDE = range(3)
Y_OWN_PART, Y_SIDE_PART, Z_OWN_PART, Z_PEER_PART, PEER_PART = range(5)
Y_PEER, Y_OWN, Y_SIDE, PEER_Y, Z_PEER = range(5)


def middle_kernel(
    kept, y_peer, strips, mate, y_side, z_side, mate_terms,
    peer_y, from_side, factor_own, mate_factor,
    finished, partial, ready,
):
    def keep(at, parts):
        ready[at, 0], ready[at, 1] = parts

    y_to_mate, y_own, z_to_mate, z_own = (split(mate[at]) for at in range(4))
    y_to_peer, z_to_peer = split(y_peer[...]), split(peer_part(strips))
    y_to_side, z_to_side = split(y_side[...]), split(z_side[...])
    f_own = split(factor_own[...])
    keep(Y_OWN, y_own)
    keep(Y_SIDE, y_to_side)
    keep(Y_PEER, y_to_peer)
    keep(Z_PEER, z_to_peer)
    keep(PEER_Y, split(peer_y[...]))

    total = products((z_own, y_to_side), (z_to_side, split(from_side[0])))
    f_side = split(filtered(kept, total, SIDE, -0.5))
    partial[PEER_PART] = products((z_own, y_to_peer))
    partial[Y_SIDE_PART] = products((y_own, f_side))
    partial[Y_OWN_PART] = mate_terms[M_Y_OWN] + products((y_own, f_own))
    partial[Z_PEER_PART] = products((f_own, z_to_peer))
    partial[Z_OWN_PART] = mate_terms[M_Z_OWN] + products((f_own, z_own))
    value = mate_terms[M_Y_MATE] + products((y_to_mate, split(mate_factor[...])))
    finished[Y_MATE] = filtered(kept, value, MATE)
    value = mate_terms[M_Z_MATE] + products((f_own, z_to_mate))
    finished[Z_MATE] = filtered(kept, value, MATE)
    value = products((f_own, z_to_side), (f_side, split(from_side[1])))
    finished[Z_SIDE] = filtered(kept, value, SIDE)


class Writer:
    def __init__(self, slots, kept, result, sems):
        self.slots, self.kept, self.result, self.sems = slots, kept, result, sems
        self.started = []
        self.held = 0

    def write(self, source, out, region):
        size = out.shape[1]
        for i in range(ROWS):
            for j in range(ROWS):
                rows, cols = quarter(i, j, size)
                slot = self.slots[i * SLOTS + region * ROWS + j, 0]
                copy = pltpu.make_async_copy(
                    source.at[rows, cols],
                    out.at[i, :, pl.ds(pl.multiple_of(slot * size, size), size)],
                    self.sems.at[len(self.started)],
                )
                copy.start()
                self.started.append(copy)

    def finish(self, value, out, region):
        place = self.result.at[self.held]
        self.held += 1
        place[...] = filtered(self.kept, value, region)
        self.write(place, out, region)

    def wait(self):
        for copy in self.started:
            copy.wait()


def peer_kernel(
    slots, kept, finished, partial, ready, from_peer, peer_spread,
    sqrt_next, inverse_next, y_peer_part, result, sems,
):
    def held(at):
        return ready[at, 0], ready[at, 1]

    writer = Writer(slots, kept, result, sems)
    writer.write(finished.at[Y_MATE], sqrt_next, MATE)
    writer.write(finished.at[Z_MATE], inverse_next, MATE)
    writer.write(finished.at[Z_SIDE], inverse_next, SIDE)
    peer_y_own = split(own_part(from_peer[Y_BESIDE], peer_spread[0]))
    peer_z_own = split(own_part(from_peer[Z_BESIDE], peer_spread[1]))
    peer_z_peer = split(peer_part(from_peer))
    total = partial[PEER_PART] + products((held(Z_PEER), peer_y_own))
    f_peer = split(filtered(kept, total, PEER, -0.5))
    total = products((peer_z_own, held(PEER_Y)), (peer_z_peer, held(Y_OWN)))
    peer_f_peer = split(filtered(kept, total, 0, -0.5, KEPT_PEER_AT, ROWS))
    value = partial[Z_PEER_PART] + products((f_peer, peer_z_own))
    writer.finish(value, inverse_next, PEER)
    value = partial[Z_OWN_PART] + products((f_peer, peer_z_peer))
    writer.finish(value, inverse_next, OWN)
    value = partial[Y_OWN_PART] + products((held(Y_PEER), peer_f_peer))
    writer.finish(value, sqrt_next, OWN)
    y_peer_part[...] = filtered(kept, products((held(Y_OWN), f_peer)), PEER)
    writer.wait()


def side_kernel(slots, kept, partial, ready, factor, unfinished, sqrt_next, result, sems):
    left = (ready[Y_SIDE, 0], ready[Y_SIDE, 1])
    value = partial[Y_SIDE_PART] + products((left, split(factor[...])))
    writer = Writer(slots, kept, result, sems)
    writer.finish(value, sqrt_next, SIDE)
    writer.wait()


def last_kernel(i, slots, part, term, unfinished, sqrt_next, result, sems):
    size = sqrt_next.shape[1]
    copies = []
    starts = [slots[i * SLOTS + PEER * ROWS + j, 0] * size for j in range(ROWS)]
    for j in range(ROWS):
        rows, cols = quarter(i, j, size)
        result[j] = part[rows, cols] + term[:, cols]
        out = sqrt_next.at[i, :, pl.ds(pl.multiple_of(starts[j], size), size)]
        copies.append(pltpu.make_async_copy(result.at[j], out, sems.at[j]))
        copies[j].start()
    for copy in copies:
        copy.wait()


def call(
    kernel, outs, operands, micros=0, scratch=(), hbm_in=(), any_in=(), hbm_out=(), in_place=None
):
    def spec(space=pltpu.VMEM):
        return pl.BlockSpec(memory_space=space)

    operands = [
        pltpu.with_memory_space_constraint(array, pltpu.HBM) if at in hbm_in else array
        for at, array in enumerate(operands)
    ]
    return pl.pallas_call(
        kernel,
        out_shape=outs,
        in_specs=[
            spec(pltpu.HBM if at in hbm_in else pl.ANY if at in any_in else pltpu.VMEM)
            for at in range(len(operands))
        ],
        out_specs=tuple(
            spec(pltpu.HBM if at in hbm_out else pltpu.VMEM) for at in range(len(outs))
        ),
        scratch_shapes=scratch,
        input_output_aliases={} if in_place is None else {in_place: 0},
        compiler_params=pltpu.CompilerParams(vmem_limit_bytes=VMEM_LIMIT),
        cost_estimate=pl.CostEstimate(
            flops=int(micros * PEAK), bytes_accessed=0, transcendentals=0
        ),
    )(*operands)


def local(sqrt_iterate, inverse_iterate, pattern, keep_mask, row_order):
    rows_dev, block, width = sqrt_iterate.shape
    row_devices, col_devices = lax.axis_size("row"), lax.axis_size("col")
    assert rows_dev == ROWS and width == SLOTS * block and pattern.shape[1] == SLOTS
    assert row_devices > 3 and row_devices % 2 == 0 and col_devices > 2
    size = ROWS * block

    def to_mate(value):
        return lax.ppermute(value, "row", [(i, i ^ 1) for i in range(row_devices)])

    def to_peer(value):
        route = [(i, (i + (1 if i % 2 else -1)) % row_devices) for i in range(row_devices)]
        return lax.ppermute(value, "row", route)

    def to_side(value):
        route = [((i + 1) % col_devices, i) for i in range(col_devices)]
        return lax.ppermute(value, "col", route)

    def shape(*dims, dtype=jnp.float32):
        return jax.ShapeDtypeStruct(dims, dtype)

    one, pair = shape(size, size), shape(2, size, size)
    (diagonal,) = call(
        diagonal_kernel,
        (shape(2 * ROWS, block, block),),
        (sqrt_iterate, inverse_iterate),
        scratch=[pltpu.SemaphoreType.DMA((4 * ROWS,))],
        hbm_in=range(2),
    )
    peer_diagonal = to_peer(diagonal)
    slots, kept, y_peer, strips, mate, y_side, z_side, own_pair = call(
        functools.partial(pack_kernel, row_devices, col_devices),
        (
            shape(ROWS * SLOTS, block, dtype=jnp.int32), shape(KEPT_LINES, block),
            one, shape(ROWS + 2, block, size), shape(4, size, size), one, one, pair,
        ),
        (pattern.T, keep_mask.T, row_order, sqrt_iterate, inverse_iterate, diagonal),
        scratch=[
            pltpu.SMEM(pattern.T.shape, jnp.int32),
            pltpu.SMEM(keep_mask.T.shape, jnp.int32),
            pltpu.SMEM(row_order.shape, jnp.int32),
            pltpu.VMEM(sqrt_iterate.shape, jnp.float32),
            pltpu.VMEM(inverse_iterate.shape, jnp.float32),
            pltpu.SemaphoreType.DMA((5,)),
        ],
        hbm_in=range(5),
        any_in=(5,),
    )
    peer_y = to_peer(y_peer)
    from_peer = to_peer(strips)
    from_mate = to_mate(mate)
    from_side = to_side(own_pair)
    (peer_spread,) = call(spread_kernel, (pair,), (peer_diagonal,), micros=10)
    (mate_terms,) = call(
        mate_kernel,
        (shape(5, size, size),),
        (kept, mate, from_mate, peer_spread),
        any_in=(3,),
    )
    factor_own, *peer_term = call(
        factor_own_kernel, (one, *[shape(block, size)] * ROWS), (kept, mate_terms, strips, peer_y), micros=5
    )
    mate_factor = to_mate(factor_own)
    term = [to_peer(value) for value in peer_term]
    side_factor = to_side(factor_own)
    finished, partial, ready = call(
        middle_kernel,
        (
            shape(3, size, size), shape(5, size, size),
            shape(5, 2, size, size, dtype=jnp.bfloat16),
        ),
        (
            kept, y_peer, strips, mate, y_side, z_side, mate_terms,
            peer_y, from_side, factor_own, mate_factor,
        ),
    )
    output = shape(rows_dev, block, width)

    def writing(blocks):
        return [
            pltpu.VMEM((blocks, size, size), jnp.float32),
            pltpu.SemaphoreType.DMA((24,)),
        ]

    sqrt_next, inverse_next, y_peer_part = call(
        peer_kernel,
        (output, output, one),
        (slots, kept, finished, partial, ready, from_peer, peer_spread),
        scratch=writing(3),
        hbm_out=(0, 1),
    )
    (sqrt_next,) = call(
        side_kernel,
        (output,),
        (slots, kept, partial, ready, side_factor, sqrt_next),
        scratch=writing(1),
        hbm_in=(5,),
        hbm_out=(0,),
        in_place=5,
    )
    for i in range(ROWS):
        (sqrt_next,) = call(
            functools.partial(last_kernel, i),
            (output,),
            (slots, y_peer_part, term[i], sqrt_next),
            scratch=[
                pltpu.VMEM((ROWS, block, block), jnp.float32),
                pltpu.SemaphoreType.DMA((ROWS,)),
            ],
            hbm_in=(3,),
            hbm_out=(0,),
            in_place=3,
        )
    return sqrt_next, inverse_next


def solution(mesh):
    rows = P(("row", "col"), None, None)
    return jax.shard_map(
        local,
        mesh=mesh,
        in_specs=(rows, rows, P(), P(), P()),
        out_specs=(rows, rows),
        check_vma=False,
    )
```
